32 devices in a mesh: frames: 2 (over x), slabs: 16 (over z, y, core).
Axes of the slice: x: 2, y: 2, z: 4, core: 2. Of those that a mesh axis runs over, the one named last changes fastest.
Arguments:
- movie: bfloat16 [16, 32768], P('frames', 'slabs'), may hold values from -48 to 48
- traces: bfloat16 [16, 256], P('frames', 'slabs'), may hold values from -6 to 6
- voxel_index: int32 [256, 2048], P('slabs'), may hold values from 0 to 4095, as said below
- footprint: float32 [256, 2048], P('slabs'), may hold values from 0 to 1
- block_order: int32 [2], replicated, may hold values from 0 to 1, each once
Outputs:
- updated: float32 [256, 2048], P('slabs')
The draws below stay inside these ranges and needn't reach their ends.
Inputs may be any that keep to these rules, and one draw needn't show every extreme that they name: `voxel_index`: within a row all 2048 positions are distinct and lie in a run of 4096 consecutive positions, whose first and last position are both in the row.
All inputs are finite; a program needn't handle non-finite values.
Results may differ from the reference program's by a relative error of at most 0.0003.
Values may be sent and summed in bfloat16 or wider, within the bound.
A program may use at most 64 MiB of HBM per device.

```python
import jax
import jax.numpy as jnp
from jax import lax

VOXEL_DEV = 2048
SOURCE_DEV = 16
FOOTPRINT = 2048
BLOCK_SIZE = 8
SWEEPS = 2
WINDOW = 4096
MARGIN = 1024
EXTENT = 4096
BLOCKS = 2
FRAMES = 16
VOXELS = 32768
SOURCES = 256
N_SLABS = 16


def draw_voxel_index(key, part):
    keys = jax.random.split(jax.random.fold_in(key, 7), SOURCES)

    def one_row(row_key):
        return jax.random.permutation(row_key, WINDOW - 2)[:FOOTPRINT - 2]
    inner = jax.vmap(one_row)(keys)
    offset = jax.random.randint(jax.random.fold_in(key, 11), (SOURCES,), 0, EXTENT - WINDOW + 1)
    within = jnp.arange(SOURCES) % SOURCE_DEV
    offset = jnp.where(within == 0, 0, jnp.where(within == 1, EXTENT - WINDOW, offset))
    first = offset[:, None]
    last = offset[:, None] + WINDOW - 1
    return jnp.concatenate([first, last, offset[:, None] + 1 + inner], axis=1).astype(jnp.int32)


def shard_levels(rng, dims, shards, least, high):
    def one(position, shards_of):
        steps = jax.random.uniform(jax.random.fold_in(jax.random.fold_in(rng, 6), position), (shards_of,), jnp.float32, least / len(shards), high / len(shards))
        return jnp.repeat(jnp.exp(steps), dims[position] // shards_of).reshape((-1,) + (1,) * (len(dims) - position - 1))

    factor_of = one(*shards[0])
    for cut in shards[1:]:
        factor_of = factor_of * one(*cut)
    return factor_of


def normal_values(rng, extent, spread, most, cuts=(), held_as=jnp.bfloat16):
    gain = shard_levels(rng, extent, cuts, -0.22, 0.18) if cuts else 1.0
    entries = jax.random.normal(rng, extent, jnp.float32) * spread * gain
    return jnp.minimum(jnp.maximum(entries, -most), most).astype(held_as)


def setup_inputs(seed: int = 0) -> dict:
    key_list = jax.random.split(jax.random.key(seed), 6)
    return {
        "movie": normal_values(key_list[0], (FRAMES, VOXELS), 8.0, 48.0, ((0, 2), (1, 16))),
        "traces": normal_values(key_list[1], (FRAMES, SOURCES), 1.0, 6.0, ((0, 2), (1, 16))),
        "voxel_index": draw_voxel_index(jax.random.fold_in(key_list[5], 71), 0),
        "footprint": jnp.clip(1.0 * jax.random.uniform(key_list[3], (SOURCES, FOOTPRINT), jnp.float32) ** shard_levels(key_list[3], (SOURCES, FOOTPRINT), ((0, 16),), -0.2, 0.2), 0.0, 1.0),
        "block_order": jax.random.permutation(key_list[4], BLOCKS).astype(jnp.int32),
    }


def transposed(left, right):
    return lax.dot_general(left, right, (((0,), (0,)), ((), ())), preferred_element_type=jnp.float32)


def sweep_blocks(current, left_rows, right_rows, stat, gram, support, block_order):
    diagonal = jnp.diagonal(gram[:, SOURCE_DEV:2 * SOURCE_DEV]) + 1.0

    def one_block(state, blk):
        start = (blk * BLOCK_SIZE).astype(jnp.int32)
        g_rows = lax.dynamic_slice_in_dim(gram, start, BLOCK_SIZE, 0)
        every = jnp.concatenate([left_rows, state, right_rows], axis=0)
        pulled = jnp.dot(g_rows, every, precision=lax.Precision.HIGHEST, preferred_element_type=jnp.float32)
        old = lax.dynamic_slice_in_dim(state, start, BLOCK_SIZE, 0)
        stat_rows = lax.dynamic_slice_in_dim(stat, start, BLOCK_SIZE, 0)
        mask_rows = lax.dynamic_slice_in_dim(support, start, BLOCK_SIZE, 0)
        scale = lax.dynamic_slice_in_dim(diagonal, start, BLOCK_SIZE, 0)
        fresh = mask_rows * jnp.maximum(old + (stat_rows - pulled) / scale[:, None], 0.0)
        return lax.dynamic_update_slice_in_dim(state, fresh, start, 0), None

    result, unused = lax.scan(one_block, current, block_order)
    return result


def reference(movie, traces, voxel_index, footprint, block_order):
    padded = jnp.pad(movie, ((0, 0), (MARGIN, MARGIN)))
    blank_traces = jnp.zeros((FRAMES, SOURCE_DEV), traces.dtype)
    trace_pad = jnp.concatenate([blank_traces, traces, blank_traces], axis=1)
    slab_ids = jnp.arange(N_SLABS).astype(jnp.int32)
    index_slabs = voxel_index.reshape(N_SLABS, SOURCE_DEV, FOOTPRINT)
    value_slabs = footprint.reshape(N_SLABS, SOURCE_DEV, FOOTPRINT)
    rows = jnp.arange(SOURCE_DEV)[:, None]

    def statistics(slab):
        extended = lax.dynamic_slice_in_dim(padded, (slab * VOXEL_DEV).astype(jnp.int32), EXTENT, 1)
        nearby = lax.dynamic_slice_in_dim(trace_pad, (slab * SOURCE_DEV).astype(jnp.int32), 3 * SOURCE_DEV, 1)
        own = nearby[:, SOURCE_DEV:2 * SOURCE_DEV]
        return transposed(own, extended), transposed(own, nearby)

    stat, gram = lax.map(statistics, slab_ids)

    def build(pair):
        index_rows, value_rows = pair
        dense = jnp.zeros((SOURCE_DEV, EXTENT), jnp.float32).at[rows, index_rows].set(value_rows)
        support = jnp.zeros((SOURCE_DEV, EXTENT), jnp.float32).at[rows, index_rows].set(1.0)
        return dense, support

    dense, support = lax.map(build, (index_slabs, value_slabs))
    blank_half = jnp.zeros((SOURCE_DEV, VOXEL_DEV), jnp.float32)
    for sweep in range(SWEEPS):
        blank_slab = jnp.zeros((1, SOURCE_DEV, EXTENT), jnp.float32)
        widened = jnp.concatenate([blank_slab, dense, blank_slab], axis=0)

        def update(slab):
            before = lax.dynamic_index_in_dim(widened, slab, 0, keepdims=False)
            here = lax.dynamic_index_in_dim(widened, slab + 1, 0, keepdims=False)
            after = lax.dynamic_index_in_dim(widened, slab + 2, 0, keepdims=False)
            left_rows = jnp.concatenate([before[:, VOXEL_DEV:], blank_half], axis=1)
            right_rows = jnp.concatenate([blank_half, after[:, :VOXEL_DEV]], axis=1)
            return sweep_blocks(here, left_rows, right_rows, stat[slab], gram[slab], support[slab], block_order)

        dense = lax.map(update, slab_ids)

    def pick(pair):
        state, index_rows = pair
        return state[rows, index_rows]

    picked = lax.map(pick, (dense, index_slabs))
    return picked.reshape(SOURCES, FOOTPRINT)
```

```python
import functools

import jax
import jax.numpy as jnp
from jax import lax
from jax.experimental import pallas as pl
from jax.experimental.pallas import tpu as pltpu
from jax.sharding import PartitionSpec as P

BLOCK = 8
LANES = 128
MESH = pl.DeviceIdType.MESH
F32 = jnp.float32
BF16 = jnp.bfloat16


def dot_nt(left, right):
    return lax.dot_general(left, right, (((1,), (1,)), ((), ())), preferred_element_type=F32)


def dot_nn(left, right):
    return lax.dot_general(left, right, (((1,), (0,)), ((), ())), preferred_element_type=F32)


def halves(value):
    high = value.astype(BF16)
    low = (value - high.astype(F32)).astype(BF16)
    return high, low


def kernel(
    nf, ns, order_ref, movie_ref, traces_ref, index_ref, foot_ref, out_ref,
    own, left, right, dense, dense_l, dense_r, final, hi_s, lo_s, vh_s, vl_s,
    send_m, recv_m, send_d, recv_d,
):
    f = lax.axis_index("frames")
    s = lax.axis_index("slabs")
    has_l = s > 0
    has_r = s < ns - 1
    frames, voxels = movie_ref.shape
    margin = voxels // 2
    extent = 2 * voxels
    chunks = extent // LANES
    half = chunks // 2
    foot_n = foot_ref.shape[1]

    barrier = pltpu.get_barrier_semaphore()
    for d in range(1, nf):
        pl.semaphore_signal(barrier, inc=1, device_id=(lax.rem(f + d, nf), s), device_id_type=MESH)

    @pl.when(has_l)
    def _():
        for d in range(nf):
            pl.semaphore_signal(
                barrier, inc=1, device_id=(lax.rem(f + d, nf), s - 1), device_id_type=MESH)

    @pl.when(has_r)
    def _():
        for d in range(nf):
            pl.semaphore_signal(
                barrier, inc=1, device_id=(lax.rem(f + d, nf), s + 1), device_id_type=MESH)

    own[f, :, 0:margin] = movie_ref[:, 0:margin].astype(F32)
    own[f, :, margin + LANES:] = movie_ref[:, margin:].astype(F32)
    own[f, :, margin:margin + LANES] = jnp.zeros((frames, LANES), F32)
    own[f, :, margin:margin + 2 * BLOCK] = traces_ref[...].astype(F32)

    @pl.when(jnp.logical_not(has_l))
    def _():
        left[...] = jnp.zeros_like(left)
        dense_l[...] = jnp.full(dense_l.shape, -1.0, F32)

    @pl.when(jnp.logical_not(has_r))
    def _():
        right[...] = jnp.zeros_like(right)
        dense_r[...] = jnp.full(dense_r.shape, -1.0, F32)

    swap = order_ref[0] != 0

    def permuted(ref):
        a = ref[0:BLOCK, :]
        b = ref[BLOCK:2 * BLOCK, :]
        return jnp.concatenate([jnp.where(swap, b, a), jnp.where(swap, a, b)], axis=0)

    index = permuted(index_ref)
    value = permuted(foot_ref)
    hi_s[...] = (index >> 7).astype(F32)
    lo_s[...] = (index & (LANES - 1)).astype(F32)
    v_hi = value.astype(BF16).astype(F32)
    vl_s[...] = value - v_hi
    vh_s[...] = jnp.where(v_hi == 0.0, -1.0, v_hi)

    def peer(d):
        to = lax.rem(f + d, nf)
        return pltpu.make_async_remote_copy(
            src_ref=own.at[f], dst_ref=own.at[f], send_sem=send_m.at[0, to],
            recv_sem=recv_m.at[0, f], device_id=(to, s), device_id_type=MESH)

    def to_right(d):
        to = lax.rem(f + d, nf)
        return pltpu.make_async_remote_copy(
            src_ref=own.at[f, :, pl.ds(margin, margin + LANES)], dst_ref=left.at[f],
            send_sem=send_m.at[1, to], recv_sem=recv_m.at[1, f],
            device_id=(to, s + 1), device_id_type=MESH)

    def to_left(d):
        to = lax.rem(f + d, nf)
        return pltpu.make_async_remote_copy(
            src_ref=own.at[f, :, pl.ds(0, margin + LANES)], dst_ref=right.at[f],
            send_sem=send_m.at[2, to], recv_sem=recv_m.at[2, f],
            device_id=(to, s - 1), device_id_type=MESH)

    count = nf - 1 + nf * has_l.astype(jnp.int32) + nf * has_r.astype(jnp.int32)
    pl.semaphore_wait(barrier, count)

    for d in range(1, nf):
        peer(d).start()

    @pl.when(has_r)
    def _():
        for d in range(nf):
            to_right(d).start()

    @pl.when(has_l)
    def _():
        for d in range(nf):
            to_left(d).start()

    rows16 = 2 * BLOCK
    iota = lax.broadcasted_iota(jnp.int32, (rows16, foot_n), 0).astype(F32)
    span = half * BLOCK

    def dense_right(b):
        return pltpu.make_async_remote_copy(
            src_ref=dense.at[pl.ds((2 * b + 1) * span, span), :],
            dst_ref=dense_l.at[pl.ds(b * span, span), :],
            send_sem=send_d.at[0, b], recv_sem=recv_d.at[0, b],
            device_id=(f, s + 1), device_id_type=MESH)

    def dense_left(b):
        return pltpu.make_async_remote_copy(
            src_ref=dense.at[pl.ds(2 * b * span, span), :],
            dst_ref=dense_r.at[pl.ds(b * span, span), :],
            send_sem=send_d.at[1, b], recv_sem=recv_d.at[1, b],
            device_id=(f, s - 1), device_id_type=MESH)

    for b in range(2):
        def scatter_row(k, carry, b=b):
            row = pl.ds(b * BLOCK + k, 1)

            def spread(ref):
                return jnp.broadcast_to(ref[row, :], (rows16, foot_n)).astype(BF16)

            hi = spread(hi_s)
            lo = spread(lo_s)
            vh = spread(vh_s)
            vl = spread(vl_s)
            zero = jnp.zeros((rows16, foot_n), BF16)
            one = jnp.ones((rows16, foot_n), BF16)
            iota16 = iota.astype(BF16)
            low = [jnp.where(lo == iota16 + BF16(16 * t), one, zero) for t in range(LANES // 16)]
            high = [hi == iota16 + BF16(16 * t) for t in range(chunks // 16)]
            lhs = [jnp.where(m, vh, zero) for m in high] + [jnp.where(m, vl, zero) for m in high]
            got = dot_nt(jnp.concatenate(lhs, axis=0), jnp.concatenate(low, axis=0))
            g_hi = got[:chunks]
            enc = jnp.where(g_hi == 0.0, -1.0, jnp.maximum(g_hi, 0.0) + got[chunks:])
            dense[pl.ds(b * chunks * BLOCK + k, chunks, stride=BLOCK), :] = enc
            return carry

        lax.fori_loop(0, BLOCK, scatter_row, 0)

        @pl.when(has_r)
        def _(b=b):
            dense_right(b).start()

        @pl.when(has_l)
        def _(b=b):
            dense_left(b).start()

    for d in range(1, nf):
        pltpu.make_async_remote_copy(
            src_ref=own.at[f], dst_ref=own.at[lax.rem(f + d, nf)], send_sem=send_m.at[0, 0],
            recv_sem=recv_m.at[0, lax.rem(f + d, nf)], device_id=(f, s),
            device_id_type=MESH).wait_recv()

    @pl.when(has_l)
    def _():
        for d in range(nf):
            pltpu.make_async_remote_copy(
                src_ref=left.at[d], dst_ref=left.at[d], send_sem=send_m.at[1, 0],
                recv_sem=recv_m.at[1, d], device_id=(f, s), device_id_type=MESH).wait_recv()

    @pl.when(has_r)
    def _():
        for d in range(nf):
            pltpu.make_async_remote_copy(
                src_ref=right.at[d], dst_ref=right.at[d], send_sem=send_m.at[2, 0],
                recv_sem=recv_m.at[2, d], device_id=(f, s), device_id_type=MESH).wait_recv()

    def all_frames(pick):
        return jnp.concatenate([pick(g) for g in range(nf)], axis=0)

    movie_l = jnp.concatenate([
        all_frames(lambda g: left[g, :, LANES:]),
        all_frames(lambda g: own[g, :, 0:margin])], axis=1).astype(BF16)
    movie_r = jnp.concatenate([
        all_frames(lambda g: own[g, :, margin + LANES:]),
        all_frames(lambda g: right[g, :, 0:margin])], axis=1).astype(BF16)
    total = nf * frames
    padding = jnp.zeros((LANES - total, LANES), F32)
    eye = (lax.broadcasted_iota(jnp.int32, (rows16, LANES), 0)
           == lax.broadcasted_iota(jnp.int32, (rows16, LANES), 1)).astype(F32).astype(BF16)

    def by_source(pick):
        block = jnp.concatenate([all_frames(pick), padding], axis=0).astype(BF16)
        rows = dot_nt(eye, block)
        return jnp.concatenate([jnp.where(swap, rows[BLOCK:], rows[:BLOCK]),
                                jnp.where(swap, rows[:BLOCK], rows[BLOCK:])], axis=0)

    t_own = by_source(lambda g: own[g, :, margin:margin + LANES])
    t_left = by_source(lambda g: left[g, :, 0:LANES])
    t_right = by_source(lambda g: right[g, :, margin:])

    depth = -(-(total + 3 * 32) // LANES) * LANES
    identity = (lax.broadcasted_iota(jnp.int32, (total, LANES), 0)
                == lax.broadcasted_iota(jnp.int32, (total, LANES), 1)).astype(F32)

    def weights(t_near):
        t32 = jnp.concatenate([t_own, t_near], axis=0)
        stacked = jnp.concatenate(
            [identity, t32, t32, t32,
             jnp.zeros((depth - total - 96, LANES), F32)], axis=0).astype(BF16)
        full = dot_nt(t32.astype(BF16), stacked)
        lane = lax.broadcasted_iota(jnp.int32, full.shape, 1)
        g_hi = full.astype(BF16).astype(F32)
        picked = jnp.where((lane >= total + 32) & (lane < total + 64), full - g_hi, g_hi)
        first = jnp.where(lane < total, full, -picked).astype(BF16)
        t_f = jnp.concatenate([t32[0:8], t32[16:24]], axis=0)
        t_s = jnp.concatenate([t32[8:16], t32[24:32]], axis=0)
        stacked2 = jnp.concatenate(
            [t_f, t_f, t_f, jnp.zeros((LANES - 48, LANES), F32)], axis=0).astype(BF16)
        cross = dot_nt(t_s.astype(BF16), stacked2)
        lane2 = lax.broadcasted_iota(jnp.int32, cross.shape, 1)
        row2 = lax.broadcasted_iota(jnp.int32, cross.shape, 0)
        c_hi = cross.astype(BF16).astype(F32)
        picked2 = jnp.where((lane2 >= 16) & (lane2 < 32), cross - c_hi, c_hi)
        same = (row2 // 8) == ((lane2 // 8) % 2)
        second = jnp.where(same, picked2, 0.0).astype(BF16)
        inverse = 1.0 / (jnp.sum(t32 * t32, axis=1, keepdims=True) + 1.0)
        return first, second, inverse

    w_l, c_l, inv_l = weights(t_left)
    w_r, c_r, inv_r = weights(t_right)

    @pl.when(has_l)
    def _():
        for b in range(2):
            pltpu.make_async_remote_copy(
                src_ref=dense_l.at[pl.ds(b * span, span), :],
                dst_ref=dense_l.at[pl.ds(b * span, span), :],
                send_sem=send_d.at[0, 0], recv_sem=recv_d.at[0, b],
                device_id=(f, s), device_id_type=MESH).wait_recv()

    @pl.when(has_r)
    def _():
        for b in range(2):
            pltpu.make_async_remote_copy(
                src_ref=dense_r.at[pl.ds(b * span, span), :],
                dst_ref=dense_r.at[pl.ds(b * span, span), :],
                send_sem=send_d.at[1, 0], recv_sem=recv_d.at[1, b],
                device_id=(f, s), device_id_type=MESH).wait_recv()

    def wide(ref, start):
        return jnp.concatenate(
            [ref[(start + c) * BLOCK:(start + c + 1) * BLOCK, :] for c in range(half)], axis=1)

    for side, (movie, w, cross, inverse, near) in enumerate(
            ((movie_l, w_l, c_l, inv_l, dense_l), (movie_r, w_r, c_r, inv_r, dense_r))):
        enc = [wide(dense, side * half), wide(dense, chunks + side * half),
               wide(near, 0), wide(near, half)]
        mask = [(e >= 0.0).astype(F32) for e in enc]
        state = [jnp.maximum(e, 0.0) for e in enc]
        pad = jnp.zeros((depth - total - 96, movie.shape[1]), BF16)
        pad2 = jnp.zeros((LANES - 48, movie.shape[1]), BF16)

        def residual(w_rows, state):
            high, low = halves(jnp.concatenate(state, axis=0))
            return dot_nn(w_rows, jnp.concatenate([movie, high, high, low, pad], axis=0))

        def change(c_rows, old, new):
            high, low = halves(jnp.concatenate([n - o for n, o in zip(new, old)], axis=0))
            return dot_nn(c_rows, jnp.concatenate([high, high, low, pad2], axis=0))

        def step(i, rest):
            return mask[i] * jnp.maximum(state[i] + rest * inverse[8 * i:8 * i + 8], 0.0)

        rest = residual(w, state)
        new_f = [step(0, rest[0:8]), step(2, rest[16:24])]
        moved = change(cross, [state[0], state[2]], new_f)
        new_s = [step(1, rest[8:16] - moved[0:8]), step(3, rest[24:32] - moved[8:16])]
        state = [new_f[0], new_s[0], new_f[1], new_s[1]]
        rest = residual(w[0:16], state)
        new_f = step(0, rest[0:8])
        moved = change(cross, [state[0], state[2]], [new_f, state[2]])
        new_s = step(1, rest[8:16] - moved[0:8])
        for c in range(half):
            at = (side * half + c) * BLOCK
            cut = slice(c * LANES, (c + 1) * LANES)
            final[at:at + BLOCK, :] = jnp.where(swap, new_s[:, cut], new_f[:, cut])
            at = at + chunks * BLOCK
            final[at:at + BLOCK, :] = jnp.where(swap, new_f[:, cut], new_s[:, cut])

    for b in range(2):
        place = index_ref[b * BLOCK:(b + 1) * BLOCK, :]
        tiles = foot_n // LANES
        chunk_of = [place[:, j * LANES:(j + 1) * LANES] >> 7 for j in range(tiles)]
        lane_of = [place[:, j * LANES:(j + 1) * LANES] & (LANES - 1) for j in range(tiles)]

        def pick(c, taken, b=b, chunk_of=chunk_of, lane_of=lane_of):
            at = pl.multiple_of((b * chunks + c) * BLOCK, BLOCK)
            tile = final[pl.ds(at, BLOCK), :]
            return tuple(
                jnp.where(chunk_of[j] == c,
                          jnp.take_along_axis(tile, lane_of[j], axis=1, mode="promise_in_bounds"),
                          taken[j])
                for j in range(tiles))

        taken = lax.fori_loop(
            0, chunks, pick, tuple(jnp.zeros((BLOCK, LANES), F32) for _ in range(tiles)))
        for j in range(tiles):
            out_ref[b * BLOCK:(b + 1) * BLOCK, j * LANES:(j + 1) * LANES] = taken[j]

    for d in range(1, nf):
        peer(d).wait_send()

    @pl.when(has_r)
    def _():
        for d in range(nf):
            to_right(d).wait_send()
        for b in range(2):
            dense_right(b).wait_send()

    @pl.when(has_l)
    def _():
        for d in range(nf):
            to_left(d).wait_send()
        for b in range(2):
            dense_left(b).wait_send()


def local(movie, traces, voxel_index, footprint, block_order):
    nf = lax.axis_size("frames")
    ns = lax.axis_size("slabs")
    frames, voxels = movie.shape
    sources, foot_n = footprint.shape
    margin = voxels // 2
    chunks = 2 * voxels // LANES
    vmem = pl.BlockSpec(memory_space=pltpu.VMEM)
    return pl.pallas_call(
        functools.partial(kernel, nf, ns),
        out_shape=jax.ShapeDtypeStruct((sources, foot_n), F32),
        in_specs=[pl.BlockSpec(memory_space=pltpu.SMEM)] + [vmem] * 4,
        out_specs=vmem,
        scratch_shapes=[
            pltpu.VMEM((nf, frames, voxels + LANES), F32),
            pltpu.VMEM((nf, frames, margin + LANES), F32),
            pltpu.VMEM((nf, frames, margin + LANES), F32),
            pltpu.VMEM((sources * chunks, LANES), F32),
            pltpu.VMEM((sources * chunks // 2, LANES), F32),
            pltpu.VMEM((sources * chunks // 2, LANES), F32),
            pltpu.VMEM((sources * chunks, LANES), F32),
            pltpu.VMEM((sources, foot_n), F32),
            pltpu.VMEM((sources, foot_n), F32),
            pltpu.VMEM((sources, foot_n), F32),
            pltpu.VMEM((sources, foot_n), F32),
            pltpu.SemaphoreType.DMA((3, nf)),
            pltpu.SemaphoreType.DMA((3, nf)),
            pltpu.SemaphoreType.DMA((2, 2)),
            pltpu.SemaphoreType.DMA((2, 2)),
        ],
        compiler_params=pltpu.CompilerParams(
            collective_id=0, has_side_effects=True, vmem_limit_bytes=32 * 1024 * 1024),
        cost_estimate=pl.CostEstimate(
            flops=2 * sources * 64 * LANES * foot_n, bytes_accessed=500000, transcendentals=0),
    )(block_order, movie, traces, voxel_index, footprint)


def solution(mesh):
    in_specs = (P("frames", "slabs"), P("frames", "slabs"), P("slabs", None), P("slabs", None), P())
    out_specs = P("slabs", None)
    return jax.shard_map(local, mesh=mesh, in_specs=in_specs, out_specs=out_specs, check_vma=False)
```

```python
import functools

import jax
import jax.numpy as jnp
from jax import lax
from jax.experimental import pallas as pl
from jax.experimental.pallas import tpu as pltpu
from jax.sharding import PartitionSpec as P

BLOCK = 8
LANES = 128
MESH = pl.DeviceIdType.MESH
F32 = jnp.float32
BF16 = jnp.bfloat16


def dot_nt(left, right):
    return lax.dot_general(left, right, (((1,), (1,)), ((), ())), preferred_element_type=F32)


def dot_nn(left, right):
    return lax.dot_general(left, right, (((1,), (0,)), ((), ())), preferred_element_type=F32)


def halves(value):
    high = value.astype(BF16)
    low = (value - high.astype(F32)).astype(BF16)
    return high, low


def kernel(
    nf, ns, order_in, movie_in, traces_in, index_in, foot_in, out_ref,
    order_ref, movie_ref, traces_ref, index_ref, foot_ref, own, left, right, dense, dense_l, dense_r, final, hi_s, lo_s, vh_s, vl_s,
    load_sem, send_m, recv_m, send_d, recv_d,
):
    f = lax.axis_index("frames")
    s = lax.axis_index("slabs")
    has_l = s > 0
    has_r = s < ns - 1
    frames, voxels = movie_ref.shape
    margin = voxels // 2
    extent = 2 * voxels
    chunks = extent // LANES
    half = chunks // 2
    foot_n = foot_ref.shape[1]

    barrier = pltpu.get_barrier_semaphore()
    for d in range(1, nf):
        pl.semaphore_signal(barrier, inc=1, device_id=(lax.rem(f + d, nf), s), device_id_type=MESH)

    @pl.when(has_l)
    def _():
        for d in range(nf):
            pl.semaphore_signal(
                barrier, inc=1, device_id=(lax.rem(f + d, nf), s - 1), device_id_type=MESH)

    @pl.when(has_r)
    def _():
        for d in range(nf):
            pl.semaphore_signal(
                barrier, inc=1, device_id=(lax.rem(f + d, nf), s + 1), device_id_type=MESH)

    pairs = ((index_in, index_ref), (foot_in, foot_ref), (order_in, order_ref),
             (movie_in, movie_ref), (traces_in, traces_ref))
    loads = [pltpu.make_async_copy(a, b, load_sem.at[i]) for i, (a, b) in enumerate(pairs)]
    for load in loads:
        load.start()

    loads[3].wait()
    loads[4].wait()
    own[f, :, 0:margin] = movie_ref[:, 0:margin].astype(F32)
    own[f, :, margin + LANES:] = movie_ref[:, margin:].astype(F32)
    own[f, :, margin:margin + LANES] = jnp.zeros((frames, LANES), F32)
    own[f, :, margin:margin + 2 * BLOCK] = traces_ref[...].astype(F32)

    @pl.when(jnp.logical_not(has_l))
    def _():
        left[...] = jnp.zeros_like(left)
        dense_l[...] = jnp.full(dense_l.shape, -1.0, F32)

    @pl.when(jnp.logical_not(has_r))
    def _():
        right[...] = jnp.zeros_like(right)
        dense_r[...] = jnp.full(dense_r.shape, -1.0, F32)

    for load in loads[:3]:
        load.wait()
    swap = order_ref[0] != 0

    def permuted(ref):
        a = ref[0:BLOCK, :]
        b = ref[BLOCK:2 * BLOCK, :]
        return jnp.concatenate([jnp.where(swap, b, a), jnp.where(swap, a, b)], axis=0)

    index = permuted(index_ref)
    value = permuted(foot_ref)
    hi_s[...] = (index >> 7).astype(F32)
    lo_s[...] = (index & (LANES - 1)).astype(F32)
    v_hi = value.astype(BF16).astype(F32)
    vl_s[...] = value - v_hi
    vh_s[...] = jnp.where(v_hi == 0.0, -1.0, v_hi)

    def peer(d):
        to = lax.rem(f + d, nf)
        return pltpu.make_async_remote_copy(
            src_ref=own.at[f], dst_ref=own.at[f], send_sem=send_m.at[0, to],
            recv_sem=recv_m.at[0, f], device_id=(to, s), device_id_type=MESH)

    def to_right(d):
        to = lax.rem(f + d, nf)
        return pltpu.make_async_remote_copy(
            src_ref=own.at[f, :, pl.ds(margin, margin + LANES)], dst_ref=left.at[f],
            send_sem=send_m.at[1, to], recv_sem=recv_m.at[1, f],
            device_id=(to, s + 1), device_id_type=MESH)

    def to_left(d):
        to = lax.rem(f + d, nf)
        return pltpu.make_async_remote_copy(
            src_ref=own.at[f, :, pl.ds(0, margin + LANES)], dst_ref=right.at[f],
            send_sem=send_m.at[2, to], recv_sem=recv_m.at[2, f],
            device_id=(to, s - 1), device_id_type=MESH)

    count = nf - 1 + nf * has_l.astype(jnp.int32) + nf * has_r.astype(jnp.int32)
    pl.semaphore_wait(barrier, count)

    for d in range(1, nf):
        peer(d).start()

    @pl.when(has_r)
    def _():
        for d in range(nf):
            to_right(d).start()

    @pl.when(has_l)
    def _():
        for d in range(nf):
            to_left(d).start()

    rows16 = 2 * BLOCK
    iota = lax.broadcasted_iota(jnp.int32, (rows16, foot_n), 0).astype(F32)
    span = half * BLOCK

    def dense_right(b):
        return pltpu.make_async_remote_copy(
            src_ref=dense.at[pl.ds((2 * b + 1) * span, span), :],
            dst_ref=dense_l.at[pl.ds(b * span, span), :],
            send_sem=send_d.at[0, b], recv_sem=recv_d.at[0, b],
            device_id=(f, s + 1), device_id_type=MESH)

    def dense_left(b):
        return pltpu.make_async_remote_copy(
            src_ref=dense.at[pl.ds(2 * b * span, span), :],
            dst_ref=dense_r.at[pl.ds(b * span, span), :],
            send_sem=send_d.at[1, b], recv_sem=recv_d.at[1, b],
            device_id=(f, s - 1), device_id_type=MESH)

    for b in range(2):
        def scatter_row(k, b=b):
            row = pl.ds(b * BLOCK + k, 1)

            def spread(ref):
                return jnp.broadcast_to(ref[row, :], (rows16, foot_n)).astype(BF16)

            hi = spread(hi_s)
            lo = spread(lo_s)
            vh = spread(vh_s)
            vl = spread(vl_s)
            zero = jnp.zeros((rows16, foot_n), BF16)
            one = jnp.ones((rows16, foot_n), BF16)
            iota16 = iota.astype(BF16)
            low = [jnp.where(lo == iota16 + BF16(16 * t), one, zero) for t in range(LANES // 16)]
            high = [hi == iota16 + BF16(16 * t) for t in range(chunks // 16)]
            lhs = [jnp.where(m, vh, zero) for m in high] + [jnp.where(m, vl, zero) for m in high]
            got = dot_nt(jnp.concatenate(lhs, axis=0), jnp.concatenate(low, axis=0))
            g_hi = got[:chunks]
            enc = jnp.where(g_hi == 0.0, -1.0, jnp.maximum(g_hi, 0.0) + got[chunks:])
            dense[pl.ds(b * chunks * BLOCK + k, chunks, stride=BLOCK), :] = enc

        for k in range(BLOCK):
            scatter_row(k)

        @pl.when(has_r)
        def _(b=b):
            dense_right(b).start()

        @pl.when(has_l)
        def _(b=b):
            dense_left(b).start()

    for d in range(1, nf):
        pltpu.make_async_remote_copy(
            src_ref=own.at[f], dst_ref=own.at[lax.rem(f + d, nf)], send_sem=send_m.at[0, 0],
            recv_sem=recv_m.at[0, lax.rem(f + d, nf)], device_id=(f, s),
            device_id_type=MESH).wait_recv()

    @pl.when(has_l)
    def _():
        for d in range(nf):
            pltpu.make_async_remote_copy(
                src_ref=left.at[d], dst_ref=left.at[d], send_sem=send_m.at[1, 0],
                recv_sem=recv_m.at[1, d], device_id=(f, s), device_id_type=MESH).wait_recv()

    @pl.when(has_r)
    def _():
        for d in range(nf):
            pltpu.make_async_remote_copy(
                src_ref=right.at[d], dst_ref=right.at[d], send_sem=send_m.at[2, 0],
                recv_sem=recv_m.at[2, d], device_id=(f, s), device_id_type=MESH).wait_recv()

    def all_frames(pick):
        return jnp.concatenate([pick(g) for g in range(nf)], axis=0)

    movie_l = jnp.concatenate([
        all_frames(lambda g: left[g, :, LANES:]),
        all_frames(lambda g: own[g, :, 0:margin])], axis=1).astype(BF16)
    movie_r = jnp.concatenate([
        all_frames(lambda g: own[g, :, margin + LANES:]),
        all_frames(lambda g: right[g, :, 0:margin])], axis=1).astype(BF16)
    total = nf * frames
    padding = jnp.zeros((LANES - total, LANES), F32)
    eye = (lax.broadcasted_iota(jnp.int32, (rows16, LANES), 0)
           == lax.broadcasted_iota(jnp.int32, (rows16, LANES), 1)).astype(F32).astype(BF16)

    def by_source(pick):
        block = jnp.concatenate([all_frames(pick), padding], axis=0).astype(BF16)
        rows = dot_nt(eye, block)
        return jnp.concatenate([jnp.where(swap, rows[BLOCK:], rows[:BLOCK]),
                                jnp.where(swap, rows[:BLOCK], rows[BLOCK:])], axis=0)

    t_own = by_source(lambda g: own[g, :, margin:margin + LANES])
    t_left = by_source(lambda g: left[g, :, 0:LANES])
    t_right = by_source(lambda g: right[g, :, margin:])

    depth = -(-(total + 3 * 32) // LANES) * LANES
    identity = (lax.broadcasted_iota(jnp.int32, (total, LANES), 0)
                == lax.broadcasted_iota(jnp.int32, (total, LANES), 1)).astype(F32)

    def weights(t_near):
        t32 = jnp.concatenate([t_own, t_near], axis=0)
        stacked = jnp.concatenate(
            [identity, t32, t32, t32,
             jnp.zeros((depth - total - 96, LANES), F32)], axis=0).astype(BF16)
        full = dot_nt(t32.astype(BF16), stacked)
        lane = lax.broadcasted_iota(jnp.int32, full.shape, 1)
        g_hi = full.astype(BF16).astype(F32)
        picked = jnp.where((lane >= total + 32) & (lane < total + 64), full - g_hi, g_hi)
        first = jnp.where(lane < total, full, -picked).astype(BF16)
        t_f = jnp.concatenate([t32[0:8], t32[16:24]], axis=0)
        t_s = jnp.concatenate([t32[8:16], t32[24:32]], axis=0)
        stacked2 = jnp.concatenate(
            [t_f, t_f, t_f, jnp.zeros((LANES - 48, LANES), F32)], axis=0).astype(BF16)
        cross = dot_nt(t_s.astype(BF16), stacked2)
        lane2 = lax.broadcasted_iota(jnp.int32, cross.shape, 1)
        row2 = lax.broadcasted_iota(jnp.int32, cross.shape, 0)
        c_hi = cross.astype(BF16).astype(F32)
        picked2 = jnp.where((lane2 >= 16) & (lane2 < 32), cross - c_hi, c_hi)
        same = (row2 // 8) == ((lane2 // 8) % 2)
        second = jnp.where(same, picked2, 0.0).astype(BF16)
        inverse = 1.0 / (jnp.sum(t32 * t32, axis=1, keepdims=True) + 1.0)
        return first, second, inverse

    w_l, c_l, inv_l = weights(t_left)
    w_r, c_r, inv_r = weights(t_right)

    @pl.when(has_l)
    def _():
        for b in range(2):
            pltpu.make_async_remote_copy(
                src_ref=dense_l.at[pl.ds(b * span, span), :],
                dst_ref=dense_l.at[pl.ds(b * span, span), :],
                send_sem=send_d.at[0, 0], recv_sem=recv_d.at[0, b],
                device_id=(f, s), device_id_type=MESH).wait_recv()

    @pl.when(has_r)
    def _():
        for b in range(2):
            pltpu.make_async_remote_copy(
                src_ref=dense_r.at[pl.ds(b * span, span), :],
                dst_ref=dense_r.at[pl.ds(b * span, span), :],
                send_sem=send_d.at[1, 0], recv_sem=recv_d.at[1, b],
                device_id=(f, s), device_id_type=MESH).wait_recv()

    def wide(ref, start):
        return jnp.concatenate(
            [ref[(start + c) * BLOCK:(start + c + 1) * BLOCK, :] for c in range(half)], axis=1)

    for side, (movie, w, cross, inverse, near) in enumerate(
            ((movie_l, w_l, c_l, inv_l, dense_l), (movie_r, w_r, c_r, inv_r, dense_r))):
        enc = [wide(dense, side * half), wide(dense, chunks + side * half),
               wide(near, 0), wide(near, half)]
        mask = [(e >= 0.0).astype(F32) for e in enc]
        state = [jnp.maximum(e, 0.0) for e in enc]
        pad = jnp.zeros((depth - total - 96, movie.shape[1]), BF16)
        pad2 = jnp.zeros((LANES - 48, movie.shape[1]), BF16)

        def residual(w_rows, state):
            high, low = halves(jnp.concatenate(state, axis=0))
            return dot_nn(w_rows, jnp.concatenate([movie, high, high, low, pad], axis=0))

        def change(c_rows, old, new):
            high, low = halves(jnp.concatenate([n - o for n, o in zip(new, old)], axis=0))
            return dot_nn(c_rows, jnp.concatenate([high, high, low, pad2], axis=0))

        def step(i, rest):
            return mask[i] * jnp.maximum(state[i] + rest * inverse[8 * i:8 * i + 8], 0.0)

        rest = residual(w, state)
        new_f = [step(0, rest[0:8]), step(2, rest[16:24])]
        moved = change(cross, [state[0], state[2]], new_f)
        new_s = [step(1, rest[8:16] - moved[0:8]), step(3, rest[24:32] - moved[8:16])]
        state = [new_f[0], new_s[0], new_f[1], new_s[1]]
        rest = residual(w[0:16], state)
        new_f = step(0, rest[0:8])
        moved = change(cross, [state[0], state[2]], [new_f, state[2]])
        new_s = step(1, rest[8:16] - moved[0:8])
        for c in range(half):
            at = (side * half + c) * BLOCK
            cut = slice(c * LANES, (c + 1) * LANES)
            final[at:at + BLOCK, :] = jnp.where(swap, new_s[:, cut], new_f[:, cut])
            at = at + chunks * BLOCK
            final[at:at + BLOCK, :] = jnp.where(swap, new_f[:, cut], new_s[:, cut])

    for b in range(2):
        place = index_ref[b * BLOCK:(b + 1) * BLOCK, :]
        tiles = foot_n // LANES
        chunk_of = [place[:, j * LANES:(j + 1) * LANES] >> 7 for j in range(tiles)]
        lane_of = [place[:, j * LANES:(j + 1) * LANES] & (LANES - 1) for j in range(tiles)]

        taken = [jnp.zeros((BLOCK, LANES), F32) for _ in range(tiles)]
        for c in range(chunks):
            at = (b * chunks + c) * BLOCK
            tile = final[at:at + BLOCK, :]
            for j in range(tiles):
                got = jnp.take_along_axis(tile, lane_of[j], axis=1, mode="promise_in_bounds")
                taken[j] = jnp.where(chunk_of[j] == c, got, taken[j])
        for j in range(tiles):
            out_ref[b * BLOCK:(b + 1) * BLOCK, j * LANES:(j + 1) * LANES] = taken[j]

    for d in range(1, nf):
        peer(d).wait_send()

    @pl.when(has_r)
    def _():
        for d in range(nf):
            to_right(d).wait_send()
        for b in range(2):
            dense_right(b).wait_send()

    @pl.when(has_l)
    def _():
        for d in range(nf):
            to_left(d).wait_send()
        for b in range(2):
            dense_left(b).wait_send()


def local(movie, traces, voxel_index, footprint, block_order):
    nf = lax.axis_size("frames")
    ns = lax.axis_size("slabs")
    frames, voxels = movie.shape
    sources, foot_n = footprint.shape
    margin = voxels // 2
    chunks = 2 * voxels // LANES
    vmem = pl.BlockSpec(memory_space=pltpu.VMEM)
    return pl.pallas_call(
        functools.partial(kernel, nf, ns),
        out_shape=jax.ShapeDtypeStruct((sources, foot_n), F32),
        in_specs=[pl.BlockSpec(memory_space=pltpu.HBM)] * 5,
        out_specs=vmem,
        scratch_shapes=[
            pltpu.SMEM(block_order.shape, block_order.dtype),
            pltpu.VMEM(movie.shape, movie.dtype),
            pltpu.VMEM(traces.shape, traces.dtype),
            pltpu.VMEM(voxel_index.shape, voxel_index.dtype),
            pltpu.VMEM(footprint.shape, footprint.dtype),
            pltpu.VMEM((nf, frames, voxels + LANES), F32),
            pltpu.VMEM((nf, frames, margin + LANES), F32),
            pltpu.VMEM((nf, frames, margin + LANES), F32),
            pltpu.VMEM((sources * chunks, LANES), F32),
            pltpu.VMEM((sources * chunks // 2, LANES), F32),
            pltpu.VMEM((sources * chunks // 2, LANES), F32),
            pltpu.VMEM((sources * chunks, LANES), F32),
            pltpu.VMEM((sources, foot_n), F32),
            pltpu.VMEM((sources, foot_n), F32),
            pltpu.VMEM((sources, foot_n), F32),
            pltpu.VMEM((sources, foot_n), F32),
            pltpu.SemaphoreType.DMA((5,)),
            pltpu.SemaphoreType.DMA((3, nf)),
            pltpu.SemaphoreType.DMA((3, nf)),
            pltpu.SemaphoreType.DMA((2, 2)),
            pltpu.SemaphoreType.DMA((2, 2)),
        ],
        compiler_params=pltpu.CompilerParams(
            collective_id=0, has_side_effects=True, vmem_limit_bytes=60 * 1024 * 1024),
        cost_estimate=pl.CostEstimate(
            flops=2 * sources * 64 * LANES * foot_n, bytes_accessed=500000, transcendentals=0),
    )(block_order, movie, traces, voxel_index, footprint)


def solution(mesh):
    in_specs = (P("frames", "slabs"), P("frames", "slabs"), P("slabs", None), P("slabs", None), P())
    out_specs = P("slabs", None)
    return jax.shard_map(local, mesh=mesh, in_specs=in_specs, out_specs=out_specs, check_vma=False)
```

```python
import functools

import jax
import jax.numpy as jnp
from jax import lax
from jax.experimental import pallas as pl
from jax.experimental.pallas import tpu as pltpu
from jax.sharding import PartitionSpec as P

BLOCK = 8
LANES = 128
MESH = pl.DeviceIdType.MESH
F32 = jnp.float32
BF16 = jnp.bfloat16


def dot_nt(left, right):
    return lax.dot_general(left, right, (((1,), (1,)), ((), ())), preferred_element_type=F32)


def dot_nn(left, right):
    return lax.dot_general(left, right, (((1,), (0,)), ((), ())), preferred_element_type=F32)


def halves(value):
    high = value.astype(BF16)
    low = (value - high.astype(F32)).astype(BF16)
    return high, low


def kernel(
    nf, ns, order_in, movie_in, traces_in, index_in, foot_in, out_ref,
    order_ref, movie_ref, traces_ref, index_ref, foot_ref, own, left, right, dense, dense_l, dense_r, hi_s, lo_s, vh_s, vl_s,
    load_sem, send_m, recv_m, send_d, recv_d,
):
    f = lax.axis_index("frames")
    s = lax.axis_index("slabs")
    has_l = s > 0
    has_r = s < ns - 1
    frames, voxels = movie_ref.shape
    margin = voxels // 2
    extent = 2 * voxels
    chunks = extent // LANES
    half = chunks // 2
    foot_n = foot_ref.shape[1]

    barrier = pltpu.get_barrier_semaphore()
    for d in range(1, nf):
        pl.semaphore_signal(barrier, inc=1, device_id=(lax.rem(f + d, nf), s), device_id_type=MESH)

    @pl.when(has_l)
    def _():
        for d in range(nf):
            pl.semaphore_signal(
                barrier, inc=1, device_id=(lax.rem(f + d, nf), s - 1), device_id_type=MESH)

    @pl.when(has_r)
    def _():
        for d in range(nf):
            pl.semaphore_signal(
                barrier, inc=1, device_id=(lax.rem(f + d, nf), s + 1), device_id_type=MESH)

    pairs = ((index_in, index_ref), (foot_in, foot_ref), (order_in, order_ref),
             (movie_in, movie_ref), (traces_in, traces_ref))
    loads = [pltpu.make_async_copy(a, b, load_sem.at[i]) for i, (a, b) in enumerate(pairs)]
    for load in loads:
        load.start()

    loads[3].wait()
    loads[4].wait()
    quarter = margin // 2
    parts = movie_ref[...].astype(F32)
    for h, at in ((0, 0), (1, quarter + LANES)):
        own[f, :, at:at + quarter] = jnp.concatenate(
            [parts[:, 2 * h * quarter:(2 * h + 1) * quarter],
             parts[:, (2 * h + 1) * quarter:(2 * h + 2) * quarter]], axis=0).astype(BF16)
    lead = jnp.concatenate(
        [traces_ref[...].astype(F32), jnp.zeros((frames, LANES - 2 * BLOCK), F32)], axis=1)
    own[f, :, quarter:quarter + LANES] = jnp.concatenate(
        [lead, jnp.zeros((frames, LANES), F32)], axis=0).astype(BF16)

    @pl.when(jnp.logical_not(has_l))
    def _():
        left[...] = jnp.zeros_like(left)
        dense_l[...] = jnp.full(dense_l.shape, -1.0, F32)

    @pl.when(jnp.logical_not(has_r))
    def _():
        right[...] = jnp.zeros_like(right)
        dense_r[...] = jnp.full(dense_r.shape, -1.0, F32)

    for load in loads[:3]:
        load.wait()
    swap = order_ref[0] != 0

    def permuted(ref):
        a = ref[0:BLOCK, :]
        b = ref[BLOCK:2 * BLOCK, :]
        return jnp.concatenate([jnp.where(swap, b, a), jnp.where(swap, a, b)], axis=0)

    index = permuted(index_ref)
    value = permuted(foot_ref)
    hi_s[...] = (index >> 7).astype(F32)
    lo_s[...] = (index & (LANES - 1)).astype(F32)
    v_hi = value.astype(BF16).astype(F32)
    vl_s[...] = value - v_hi
    vh_s[...] = jnp.where(v_hi == 0.0, -1.0, v_hi)

    def peer(d):
        to = lax.rem(f + d, nf)
        return pltpu.make_async_remote_copy(
            src_ref=own.at[f], dst_ref=own.at[f], send_sem=send_m.at[0, to],
            recv_sem=recv_m.at[0, f], device_id=(to, s), device_id_type=MESH)

    def to_right(d):
        to = lax.rem(f + d, nf)
        return pltpu.make_async_remote_copy(
            src_ref=own.at[f, :, pl.ds(quarter, quarter + LANES)], dst_ref=left.at[f],
            send_sem=send_m.at[1, to], recv_sem=recv_m.at[1, f],
            device_id=(to, s + 1), device_id_type=MESH)

    def to_left(d):
        to = lax.rem(f + d, nf)
        return pltpu.make_async_remote_copy(
            src_ref=own.at[f, :, pl.ds(0, quarter + LANES)], dst_ref=right.at[f],
            send_sem=send_m.at[2, to], recv_sem=recv_m.at[2, f],
            device_id=(to, s - 1), device_id_type=MESH)

    rows16 = 2 * BLOCK
    iota = lax.broadcasted_iota(jnp.int32, (rows16, foot_n), 0).astype(F32)
    span = half * BLOCK

    def dense_right(b):
        return pltpu.make_async_remote_copy(
            src_ref=dense.at[pl.ds((2 * b + 1) * span, span), :],
            dst_ref=dense_l.at[pl.ds(b * span, span), :],
            send_sem=send_d.at[0, b], recv_sem=recv_d.at[0, b],
            device_id=(f, s + 1), device_id_type=MESH)

    def dense_left(b):
        return pltpu.make_async_remote_copy(
            src_ref=dense.at[pl.ds(2 * b * span, span), :],
            dst_ref=dense_r.at[pl.ds(b * span, span), :],
            send_sem=send_d.at[1, b], recv_sem=recv_d.at[1, b],
            device_id=(f, s - 1), device_id_type=MESH)

    for b in range(2):
        def scatter_row(k, b=b):
            row = pl.ds(b * BLOCK + k, 1)

            def spread(ref):
                return jnp.broadcast_to(ref[row, :], (rows16, foot_n)).astype(BF16)

            hi = spread(hi_s)
            lo = spread(lo_s)
            vh = spread(vh_s)
            vl = spread(vl_s)
            zero = jnp.zeros((rows16, foot_n), BF16)
            one = jnp.ones((rows16, foot_n), BF16)
            iota16 = iota.astype(BF16)
            low = [jnp.where(lo == iota16 + BF16(16 * t), one, zero) for t in range(LANES // 16)]
            high = [hi == iota16 + BF16(16 * t) for t in range(chunks // 16)]
            lhs = [jnp.where(m, vh, zero) for m in high] + [jnp.where(m, vl, zero) for m in high]
            got = dot_nt(jnp.concatenate(lhs, axis=0), jnp.concatenate(low, axis=0))
            g_hi = got[:chunks]
            enc = jnp.where(g_hi == 0.0, -1.0, jnp.maximum(g_hi, 0.0) + got[chunks:])
            dense[pl.ds(b * chunks * BLOCK + k, chunks, stride=BLOCK), :] = enc

        for k in range(BLOCK):
            scatter_row(k)

        if b == 0:
            count = nf - 1 + nf * has_l.astype(jnp.int32) + nf * has_r.astype(jnp.int32)
            pl.semaphore_wait(barrier, count)

            for d in range(1, nf):
                peer(d).start()

            @pl.when(has_r)
            def _():
                for d in range(nf):
                    to_right(d).start()

            @pl.when(has_l)
            def _():
                for d in range(nf):
                    to_left(d).start()

        @pl.when(has_r)
        def _(b=b):
            dense_right(b).start()

        @pl.when(has_l)
        def _(b=b):
            dense_left(b).start()

    for d in range(1, nf):
        pltpu.make_async_remote_copy(
            src_ref=own.at[f], dst_ref=own.at[lax.rem(f + d, nf)], send_sem=send_m.at[0, 0],
            recv_sem=recv_m.at[0, lax.rem(f + d, nf)], device_id=(f, s),
            device_id_type=MESH).wait_recv()

    @pl.when(has_l)
    def _():
        for d in range(nf):
            pltpu.make_async_remote_copy(
                src_ref=left.at[d], dst_ref=left.at[d], send_sem=send_m.at[1, 0],
                recv_sem=recv_m.at[1, d], device_id=(f, s), device_id_type=MESH).wait_recv()

    @pl.when(has_r)
    def _():
        for d in range(nf):
            pltpu.make_async_remote_copy(
                src_ref=right.at[d], dst_ref=right.at[d], send_sem=send_m.at[2, 0],
                recv_sem=recv_m.at[2, d], device_id=(f, s), device_id_type=MESH).wait_recv()

    def all_frames(pick):
        return jnp.concatenate([pick(g) for g in range(nf)], axis=0)

    def unpacked(ref, at):
        def one(g):
            both = ref[g, :, at:at + quarter].astype(F32)
            return jnp.concatenate([both[:frames], both[frames:]], axis=1)
        return all_frames(one)

    def trace_rows(ref, at):
        return lambda g: ref[g, :, at:at + LANES].astype(F32)[:frames]

    movie_l = jnp.concatenate([unpacked(left, LANES), unpacked(own, 0)], axis=1).astype(BF16)
    movie_r = jnp.concatenate(
        [unpacked(own, quarter + LANES), unpacked(right, 0)], axis=1).astype(BF16)
    total = nf * frames
    padding = jnp.zeros((LANES - total, LANES), F32)
    eye = (lax.broadcasted_iota(jnp.int32, (rows16, LANES), 0)
           == lax.broadcasted_iota(jnp.int32, (rows16, LANES), 1)).astype(F32).astype(BF16)

    def by_source(pick):
        block = jnp.concatenate([all_frames(pick), padding], axis=0).astype(BF16)
        rows = dot_nt(eye, block)
        return jnp.concatenate([jnp.where(swap, rows[BLOCK:], rows[:BLOCK]),
                                jnp.where(swap, rows[:BLOCK], rows[BLOCK:])], axis=0)

    t_own = by_source(trace_rows(own, quarter))
    t_left = by_source(trace_rows(left, 0))
    t_right = by_source(trace_rows(right, quarter))

    depth = -(-(total + 3 * 32) // LANES) * LANES
    identity = (lax.broadcasted_iota(jnp.int32, (total, LANES), 0)
                == lax.broadcasted_iota(jnp.int32, (total, LANES), 1)).astype(F32)

    def weights(t_near):
        t32 = jnp.concatenate([t_own, t_near], axis=0)
        stacked = jnp.concatenate(
            [identity, t32, t32, t32,
             jnp.zeros((depth - total - 96, LANES), F32)], axis=0).astype(BF16)
        full = dot_nt(t32.astype(BF16), stacked)
        lane = lax.broadcasted_iota(jnp.int32, full.shape, 1)
        g_hi = full.astype(BF16).astype(F32)
        picked = jnp.where((lane >= total + 32) & (lane < total + 64), full - g_hi, g_hi)
        first = jnp.where(lane < total, full, -picked).astype(BF16)
        t_f = jnp.concatenate([t32[0:8], t32[16:24]], axis=0)
        t_s = jnp.concatenate([t32[8:16], t32[24:32]], axis=0)
        stacked2 = jnp.concatenate(
            [t_f, t_f, t_f, jnp.zeros((LANES - 48, LANES), F32)], axis=0).astype(BF16)
        cross = dot_nt(t_s.astype(BF16), stacked2)
        lane2 = lax.broadcasted_iota(jnp.int32, cross.shape, 1)
        row2 = lax.broadcasted_iota(jnp.int32, cross.shape, 0)
        c_hi = cross.astype(BF16).astype(F32)
        picked2 = jnp.where((lane2 >= 16) & (lane2 < 32), cross - c_hi, c_hi)
        same = (row2 // 8) == ((lane2 // 8) % 2)
        second = jnp.where(same, picked2, 0.0).astype(BF16)
        inverse = 1.0 / (jnp.sum(t32 * t32, axis=1, keepdims=True) + 1.0)
        return first[:, :total + 96], second[:, :48], inverse

    w_l, c_l, inv_l = weights(t_left)
    w_r, c_r, inv_r = weights(t_right)

    @pl.when(has_l)
    def _():
        for b in range(2):
            pltpu.make_async_remote_copy(
                src_ref=dense_l.at[pl.ds(b * span, span), :],
                dst_ref=dense_l.at[pl.ds(b * span, span), :],
                send_sem=send_d.at[0, 0], recv_sem=recv_d.at[0, b],
                device_id=(f, s), device_id_type=MESH).wait_recv()

    @pl.when(has_r)
    def _():
        for b in range(2):
            pltpu.make_async_remote_copy(
                src_ref=dense_r.at[pl.ds(b * span, span), :],
                dst_ref=dense_r.at[pl.ds(b * span, span), :],
                send_sem=send_d.at[1, 0], recv_sem=recv_d.at[1, b],
                device_id=(f, s), device_id_type=MESH).wait_recv()

    def wide(ref, start):
        return jnp.concatenate(
            [ref[(start + c) * BLOCK:(start + c + 1) * BLOCK, :] for c in range(half)], axis=1)

    final = ([], [])
    for side, (movie, w, cross, inverse, near) in enumerate(
            ((movie_l, w_l, c_l, inv_l, dense_l), (movie_r, w_r, c_r, inv_r, dense_r))):
        enc = [wide(dense, side * half), wide(dense, chunks + side * half),
               wide(near, 0), wide(near, half)]
        mask = [(e >= 0.0).astype(F32) for e in enc]
        state = [jnp.maximum(e, 0.0) for e in enc]

        def residual(w_rows, state):
            high, low = halves(jnp.concatenate(state, axis=0))
            return dot_nn(w_rows, jnp.concatenate([movie, high, high, low], axis=0))

        def change(c_rows, old, new):
            high, low = halves(jnp.concatenate([n - o for n, o in zip(new, old)], axis=0))
            return dot_nn(c_rows, jnp.concatenate([high, high, low], axis=0))

        def step(i, rest):
            return mask[i] * jnp.maximum(state[i] + rest * inverse[8 * i:8 * i + 8], 0.0)

        rest = residual(w, state)
        new_f = [step(0, rest[0:8]), step(2, rest[16:24])]
        moved = change(cross, [state[0], state[2]], new_f)
        new_s = [step(1, rest[8:16] - moved[0:8]), step(3, rest[24:32] - moved[8:16])]
        state = [new_f[0], new_s[0], new_f[1], new_s[1]]
        rest = residual(w[0:16], state)
        new_f = step(0, rest[0:8])
        moved = change(cross, [state[0], state[2]], [new_f, state[2]])
        new_s = step(1, rest[8:16] - moved[0:8])
        for c in range(half):
            cut = slice(c * LANES, (c + 1) * LANES)
            final[0].append(jnp.where(swap, new_s[:, cut], new_f[:, cut]))
            final[1].append(jnp.where(swap, new_f[:, cut], new_s[:, cut]))

    for b in range(2):
        place = index_ref[b * BLOCK:(b + 1) * BLOCK, :]
        tiles = foot_n // LANES
        chunk_of = [place[:, j * LANES:(j + 1) * LANES] >> 7 for j in range(tiles)]
        lane_of = [place[:, j * LANES:(j + 1) * LANES] & (LANES - 1) for j in range(tiles)]

        taken = [jnp.zeros((BLOCK, LANES), F32) for _ in range(tiles)]
        for c in range(chunks):
            tile = final[b][c]
            for j in range(tiles):
                got = jnp.take_along_axis(tile, lane_of[j], axis=1, mode="promise_in_bounds")
                taken[j] = jnp.where(chunk_of[j] == c, got, taken[j])
        for j in range(tiles):
            out_ref[b * BLOCK:(b + 1) * BLOCK, j * LANES:(j + 1) * LANES] = taken[j]

    for d in range(1, nf):
        peer(d).wait_send()

    @pl.when(has_r)
    def _():
        for d in range(nf):
            to_right(d).wait_send()
        for b in range(2):
            dense_right(b).wait_send()

    @pl.when(has_l)
    def _():
        for d in range(nf):
            to_left(d).wait_send()
        for b in range(2):
            dense_left(b).wait_send()


def local(movie, traces, voxel_index, footprint, block_order):
    nf = lax.axis_size("frames")
    ns = lax.axis_size("slabs")
    frames, voxels = movie.shape
    sources, foot_n = footprint.shape
    margin = voxels // 2
    chunks = 2 * voxels // LANES
    vmem = pl.BlockSpec(memory_space=pltpu.VMEM)
    return pl.pallas_call(
        functools.partial(kernel, nf, ns),
        out_shape=pltpu.VMEM((sources, foot_n), F32),
        in_specs=[pl.BlockSpec(memory_space=pltpu.HBM)] * 5,
        out_specs=vmem,
        scratch_shapes=[
            pltpu.SMEM(block_order.shape, block_order.dtype),
            pltpu.VMEM(movie.shape, movie.dtype),
            pltpu.VMEM(traces.shape, traces.dtype),
            pltpu.VMEM(voxel_index.shape, voxel_index.dtype),
            pltpu.VMEM(footprint.shape, footprint.dtype),
            pltpu.VMEM((nf, 2 * frames, margin + LANES), BF16),
            pltpu.VMEM((nf, 2 * frames, margin // 2 + LANES), BF16),
            pltpu.VMEM((nf, 2 * frames, margin // 2 + LANES), BF16),
            pltpu.VMEM((sources * chunks, LANES), F32),
            pltpu.VMEM((sources * chunks // 2, LANES), F32),
            pltpu.VMEM((sources * chunks // 2, LANES), F32),
            pltpu.VMEM((sources, foot_n), F32),
            pltpu.VMEM((sources, foot_n), F32),
            pltpu.VMEM((sources, foot_n), F32),
            pltpu.VMEM((sources, foot_n), F32),
            pltpu.SemaphoreType.DMA((5,)),
            pltpu.SemaphoreType.DMA((3, nf)),
            pltpu.SemaphoreType.DMA((3, nf)),
            pltpu.SemaphoreType.DMA((2, 2)),
            pltpu.SemaphoreType.DMA((2, 2)),
        ],
        compiler_params=pltpu.CompilerParams(
            collective_id=0, has_side_effects=True, vmem_limit_bytes=32 * 1024 * 1024),
        cost_estimate=pl.CostEstimate(
            flops=2 * sources * 64 * LANES * foot_n, bytes_accessed=500000, transcendentals=0),
    )(*(pltpu.with_memory_space_constraint(x, pltpu.HBM)
        for x in (block_order, movie, traces, voxel_index, footprint)))


def solution(mesh):
    in_specs = (P("frames", "slabs"), P("frames", "slabs"), P("slabs", None), P("slabs", None), P())
    out_specs = P("slabs", None)
    return jax.shard_map(local, mesh=mesh, in_specs=in_specs, out_specs=out_specs, check_vma=False)
```

```python
import functools

import jax
import jax.numpy as jnp
from jax import lax
from jax.experimental import pallas as pl
from jax.experimental.pallas import tpu as pltpu
from jax.sharding import PartitionSpec as P

BLOCK = 8
LANES = 128
MESH = pl.DeviceIdType.MESH
F32 = jnp.float32
BF16 = jnp.bfloat16


def dot_nt(left, right):
    return lax.dot_general(left, right, (((1,), (1,)), ((), ())), preferred_element_type=F32)


def dot_nn(left, right):
    return lax.dot_general(left, right, (((1,), (0,)), ((), ())), preferred_element_type=F32)


def halves(value):
    high = value.astype(BF16)
    low = (value - high.astype(F32)).astype(BF16)
    return high, low


def kernel(
    nf, ns, order_in, movie_in, traces_in, index_in, foot_in, out_ref,
    order_ref, movie_ref, traces_ref, index_ref, foot_ref, own, left, right, dense, near,
    hi_s, lo_s, vh_s, vl_s, movie_s, w_s, c_s, inv_s,
    load_sem, send_m, recv_m, send_d, recv_d,
):
    f = lax.axis_index("frames")
    s = lax.axis_index("slabs")
    has_l = s > 0
    has_r = s < ns - 1
    frames, voxels = movie_ref.shape
    margin = voxels // 2
    extent = 2 * voxels
    chunks = extent // LANES
    half = chunks // 2
    foot_n = foot_ref.shape[1]

    barrier = pltpu.get_barrier_semaphore()
    for d in range(1, nf):
        pl.semaphore_signal(barrier, inc=1, device_id=(lax.rem(f + d, nf), s), device_id_type=MESH)

    @pl.when(has_l)
    def _():
        for d in range(nf):
            pl.semaphore_signal(
                barrier, inc=1, device_id=(lax.rem(f + d, nf), s - 1), device_id_type=MESH)

    @pl.when(has_r)
    def _():
        for d in range(nf):
            pl.semaphore_signal(
                barrier, inc=1, device_id=(lax.rem(f + d, nf), s + 1), device_id_type=MESH)

    pairs = ((index_in, index_ref), (foot_in, foot_ref), (order_in, order_ref),
             (movie_in, movie_ref), (traces_in, traces_ref))
    loads = [pltpu.make_async_copy(a, b, load_sem.at[i]) for i, (a, b) in enumerate(pairs)]
    for load in loads:
        load.start()

    loads[3].wait()
    loads[4].wait()
    quarter = margin // 2
    parts = movie_ref[...].astype(F32)
    for h, at in ((0, 0), (1, quarter + LANES)):
        own[f, :, at:at + quarter] = jnp.concatenate(
            [parts[:, 2 * h * quarter:(2 * h + 1) * quarter],
             parts[:, (2 * h + 1) * quarter:(2 * h + 2) * quarter]], axis=0).astype(BF16)
    lead = jnp.concatenate(
        [traces_ref[...].astype(F32), jnp.zeros((frames, LANES - 2 * BLOCK), F32)], axis=1)
    own[f, :, quarter:quarter + LANES] = jnp.concatenate(
        [lead, jnp.zeros((frames, LANES), F32)], axis=0).astype(BF16)

    @pl.when(jnp.logical_not(has_l))
    def _():
        left[...] = jnp.zeros_like(left)
        near[0] = jnp.full(near.shape[1:], -1.0, F32)

    @pl.when(jnp.logical_not(has_r))
    def _():
        right[...] = jnp.zeros_like(right)
        near[1] = jnp.full(near.shape[1:], -1.0, F32)

    for load in loads[:3]:
        load.wait()
    swap = order_ref[0] != 0

    def permuted(ref):
        a = ref[0:BLOCK, :]
        b = ref[BLOCK:2 * BLOCK, :]
        return jnp.concatenate([jnp.where(swap, b, a), jnp.where(swap, a, b)], axis=0)

    index = permuted(index_ref)
    value = permuted(foot_ref)
    hi_s[...] = (index >> 7).astype(F32)
    lo_s[...] = (index & (LANES - 1)).astype(F32)
    v_hi = value.astype(BF16).astype(F32)
    vl_s[...] = value - v_hi
    vh_s[...] = jnp.where(v_hi == 0.0, -1.0, v_hi)

    def peer(d):
        to = lax.rem(f + d, nf)
        return pltpu.make_async_remote_copy(
            src_ref=own.at[f], dst_ref=own.at[f], send_sem=send_m.at[0, to],
            recv_sem=recv_m.at[0, f], device_id=(to, s), device_id_type=MESH)

    def to_right(d):
        to = lax.rem(f + d, nf)
        return pltpu.make_async_remote_copy(
            src_ref=own.at[f, :, pl.ds(quarter, quarter + LANES)], dst_ref=left.at[f],
            send_sem=send_m.at[1, to], recv_sem=recv_m.at[1, f],
            device_id=(to, s + 1), device_id_type=MESH)

    def to_left(d):
        to = lax.rem(f + d, nf)
        return pltpu.make_async_remote_copy(
            src_ref=own.at[f, :, pl.ds(0, quarter + LANES)], dst_ref=right.at[f],
            send_sem=send_m.at[2, to], recv_sem=recv_m.at[2, f],
            device_id=(to, s - 1), device_id_type=MESH)

    rows16 = 2 * BLOCK
    iota = lax.broadcasted_iota(jnp.int32, (rows16, foot_n), 0).astype(F32)
    span = half * BLOCK

    def dense_right(b):
        return pltpu.make_async_remote_copy(
            src_ref=dense.at[2 * b + 1], dst_ref=near.at[0, pl.ds(b * span, span), :],
            send_sem=send_d.at[0, b], recv_sem=recv_d.at[0, b],
            device_id=(f, s + 1), device_id_type=MESH)

    def dense_left(b):
        return pltpu.make_async_remote_copy(
            src_ref=dense.at[2 * b], dst_ref=near.at[1, pl.ds(b * span, span), :],
            send_sem=send_d.at[1, b], recv_sem=recv_d.at[1, b],
            device_id=(f, s - 1), device_id_type=MESH)

    for b in range(2):
        def scatter_row(k, b=b):
            row = pl.ds(b * BLOCK + k, 1)

            def spread(ref):
                return jnp.broadcast_to(ref[row, :], (rows16, foot_n)).astype(BF16)

            hi = spread(hi_s)
            lo = spread(lo_s)
            vh = spread(vh_s)
            vl = spread(vl_s)
            zero = jnp.zeros((rows16, foot_n), BF16)
            one = jnp.ones((rows16, foot_n), BF16)
            iota16 = iota.astype(BF16)
            low = [jnp.where(lo == iota16 + BF16(16 * t), one, zero) for t in range(LANES // 16)]
            high = [hi == iota16 + BF16(16 * t) for t in range(chunks // 16)]
            lhs = [jnp.where(m, vh, zero) for m in high] + [jnp.where(m, vl, zero) for m in high]
            got = dot_nt(jnp.concatenate(lhs, axis=0), jnp.concatenate(low, axis=0))
            g_hi = got[:chunks]
            enc = jnp.where(g_hi == 0.0, -1.0, jnp.maximum(g_hi, 0.0) + got[chunks:])
            dense[2 * b, pl.ds(k, half, stride=BLOCK), :] = enc[:half]
            dense[2 * b + 1, pl.ds(k, half, stride=BLOCK), :] = enc[half:]

        for k in range(BLOCK):
            scatter_row(k)

            if b == 0 and k == BLOCK // 2 - 1:
                count = nf - 1 + nf * has_l.astype(jnp.int32) + nf * has_r.astype(jnp.int32)
                pl.semaphore_wait(barrier, count)

                for d in range(1, nf):
                    peer(d).start()

                @pl.when(has_r)
                def _():
                    for d in range(nf):
                        to_right(d).start()

                @pl.when(has_l)
                def _():
                    for d in range(nf):
                        to_left(d).start()

        @pl.when(has_r)
        def _(b=b):
            dense_right(b).start()

        @pl.when(has_l)
        def _(b=b):
            dense_left(b).start()

    for d in range(1, nf):
        pltpu.make_async_remote_copy(
            src_ref=own.at[f], dst_ref=own.at[lax.rem(f + d, nf)], send_sem=send_m.at[0, 0],
            recv_sem=recv_m.at[0, lax.rem(f + d, nf)], device_id=(f, s),
            device_id_type=MESH).wait_recv()

    @pl.when(has_l)
    def _():
        for d in range(nf):
            pltpu.make_async_remote_copy(
                src_ref=left.at[d], dst_ref=left.at[d], send_sem=send_m.at[1, 0],
                recv_sem=recv_m.at[1, d], device_id=(f, s), device_id_type=MESH).wait_recv()

    @pl.when(has_r)
    def _():
        for d in range(nf):
            pltpu.make_async_remote_copy(
                src_ref=right.at[d], dst_ref=right.at[d], send_sem=send_m.at[2, 0],
                recv_sem=recv_m.at[2, d], device_id=(f, s), device_id_type=MESH).wait_recv()

    def all_frames(pick):
        return jnp.concatenate([pick(g) for g in range(nf)], axis=0)

    def unpacked(ref, at):
        def one(g):
            both = ref[g, :, at:at + quarter].astype(F32)
            return jnp.concatenate([both[:frames], both[frames:]], axis=1)
        return all_frames(one)

    def trace_rows(ref, at):
        return lambda g: ref[g, :, at:at + LANES].astype(F32)[:frames]

    movie_l = jnp.concatenate([unpacked(left, LANES), unpacked(own, 0)], axis=1).astype(BF16)
    movie_r = jnp.concatenate(
        [unpacked(own, quarter + LANES), unpacked(right, 0)], axis=1).astype(BF16)
    total = nf * frames
    padding = jnp.zeros((LANES - total, LANES), F32)
    eye = (lax.broadcasted_iota(jnp.int32, (rows16, LANES), 0)
           == lax.broadcasted_iota(jnp.int32, (rows16, LANES), 1)).astype(F32).astype(BF16)

    def by_source(pick):
        block = jnp.concatenate([all_frames(pick), padding], axis=0).astype(BF16)
        rows = dot_nt(eye, block)
        return jnp.concatenate([jnp.where(swap, rows[BLOCK:], rows[:BLOCK]),
                                jnp.where(swap, rows[:BLOCK], rows[BLOCK:])], axis=0)

    t_own = by_source(trace_rows(own, quarter))
    t_left = by_source(trace_rows(left, 0))
    t_right = by_source(trace_rows(right, quarter))

    depth = -(-(total + 3 * 32) // LANES) * LANES
    identity = (lax.broadcasted_iota(jnp.int32, (total, LANES), 0)
                == lax.broadcasted_iota(jnp.int32, (total, LANES), 1)).astype(F32)

    def weights(t_near):
        t32 = jnp.concatenate([t_own, t_near], axis=0)
        stacked = jnp.concatenate(
            [identity, t32, t32, t32,
             jnp.zeros((depth - total - 96, LANES), F32)], axis=0).astype(BF16)
        full = dot_nt(t32.astype(BF16), stacked)
        lane = lax.broadcasted_iota(jnp.int32, full.shape, 1)
        g_hi = full.astype(BF16).astype(F32)
        picked = jnp.where((lane >= total + 32) & (lane < total + 64), full - g_hi, g_hi)
        first = jnp.where(lane < total, full, -picked).astype(BF16)
        t_f = jnp.concatenate([t32[0:8], t32[16:24]], axis=0)
        t_s = jnp.concatenate([t32[8:16], t32[24:32]], axis=0)
        stacked2 = jnp.concatenate(
            [t_f, t_f, t_f, jnp.zeros((LANES - 48, LANES), F32)], axis=0).astype(BF16)
        cross = dot_nt(t_s.astype(BF16), stacked2)
        lane2 = lax.broadcasted_iota(jnp.int32, cross.shape, 1)
        row2 = lax.broadcasted_iota(jnp.int32, cross.shape, 0)
        c_hi = cross.astype(BF16).astype(F32)
        picked2 = jnp.where((lane2 >= 16) & (lane2 < 32), cross - c_hi, c_hi)
        same = (row2 // 8) == ((lane2 // 8) % 2)
        second = jnp.where(same, picked2, 0.0).astype(BF16)
        inverse = 1.0 / (jnp.sum(t32 * t32, axis=1, keepdims=True) + 1.0)
        return first, second, inverse

    for side, (movie, t_near) in enumerate(((movie_l, t_left), (movie_r, t_right))):
        w, c, inverse = weights(t_near)
        movie_s[side] = movie
        w_s[side] = w
        c_s[side] = c
        inv_s[side] = jnp.broadcast_to(inverse, (4 * BLOCK, LANES))

    tiles = foot_n // LANES
    places = [[index_ref[b * BLOCK:(b + 1) * BLOCK, j * LANES:(j + 1) * LANES]
               for j in range(tiles)] for b in range(2)]
    taken = [[jnp.zeros((BLOCK, LANES), F32)] * tiles for b in range(2)]

    early = 1 - lax.rem(s, 2)
    for side in (early, 1 - early):
        @pl.when(jnp.where(side == 0, s, ns - 1 - s) > 0)
        def _(side=side):
            for b in range(2):
                pltpu.make_async_remote_copy(
                    src_ref=near.at[side, pl.ds(b * span, span), :],
                    dst_ref=near.at[side, pl.ds(b * span, span), :],
                    send_sem=send_d.at[0, 0], recv_sem=recv_d.at[side, b],
                    device_id=(f, s), device_id_type=MESH).wait_recv()

        def wide(ref, at, start):
            return jnp.concatenate(
                [ref[at, (start + c) * BLOCK:(start + c + 1) * BLOCK, :] for c in range(half)],
                axis=1)

        movie = movie_s[side]
        w = w_s[side][:, :total + 96]
        cross = c_s[side][:, :48]
        inverse = inv_s[side][:, 0:1]
        enc = [wide(dense, side, 0), wide(dense, 2 + side, 0),
               wide(near, side, 0), wide(near, side, half)]
        mask = [(e >= 0.0).astype(F32) for e in enc]
        state = [jnp.maximum(e, 0.0) for e in enc]

        def residual(w_rows, state):
            high, low = halves(jnp.concatenate(state, axis=0))
            return dot_nn(w_rows, jnp.concatenate([movie, high, high, low], axis=0))

        def change(c_rows, old, new):
            high, low = halves(jnp.concatenate([n - o for n, o in zip(new, old)], axis=0))
            return dot_nn(c_rows, jnp.concatenate([high, high, low], axis=0))

        def step(i, rest):
            return mask[i] * jnp.maximum(state[i] + rest * inverse[8 * i:8 * i + 8], 0.0)

        rest = residual(w, state)
        new_f = [step(0, rest[0:8]), step(2, rest[16:24])]
        moved = change(cross, [state[0], state[2]], new_f)
        new_s = [step(1, rest[8:16] - moved[0:8]), step(3, rest[24:32] - moved[8:16])]
        state = [new_f[0], new_s[0], new_f[1], new_s[1]]
        rest = residual(w[0:16], state)
        new_f = step(0, rest[0:8])
        moved = change(cross, [state[0], state[2]], [new_f, state[2]])
        new_s = step(1, rest[8:16] - moved[0:8])
        done = (jnp.where(swap, new_s, new_f), jnp.where(swap, new_f, new_s))
        for b in range(2):
            for j in range(tiles):
                chunk = (places[b][j] >> 7) - half * side
                lane = places[b][j] & (LANES - 1)
                for c in range(half):
                    tile = done[b][:, c * LANES:(c + 1) * LANES]
                    got = jnp.take_along_axis(tile, lane, axis=1, mode="promise_in_bounds")
                    taken[b][j] = jnp.where(chunk == c, got, taken[b][j])

    for b in range(2):
        for j in range(tiles):
            out_ref[b * BLOCK:(b + 1) * BLOCK, j * LANES:(j + 1) * LANES] = taken[b][j]

    for d in range(1, nf):
        peer(d).wait_send()

    @pl.when(has_r)
    def _():
        for d in range(nf):
            to_right(d).wait_send()
        for b in range(2):
            dense_right(b).wait_send()

    @pl.when(has_l)
    def _():
        for d in range(nf):
            to_left(d).wait_send()
        for b in range(2):
            dense_left(b).wait_send()


def local(movie, traces, voxel_index, footprint, block_order):
    nf = lax.axis_size("frames")
    ns = lax.axis_size("slabs")
    frames, voxels = movie.shape
    sources, foot_n = footprint.shape
    margin = voxels // 2
    chunks = 2 * voxels // LANES
    depth = -(-(nf * frames + 3 * 32) // LANES) * LANES
    vmem = pl.BlockSpec(memory_space=pltpu.VMEM)
    return pl.pallas_call(
        functools.partial(kernel, nf, ns),
        out_shape=pltpu.VMEM((sources, foot_n), F32),
        in_specs=[pl.BlockSpec(memory_space=pltpu.HBM)] * 5,
        out_specs=vmem,
        scratch_shapes=[
            pltpu.SMEM(block_order.shape, block_order.dtype),
            pltpu.VMEM(movie.shape, movie.dtype),
            pltpu.VMEM(traces.shape, traces.dtype),
            pltpu.VMEM(voxel_index.shape, voxel_index.dtype),
            pltpu.VMEM(footprint.shape, footprint.dtype),
            pltpu.VMEM((nf, 2 * frames, margin + LANES), BF16),
            pltpu.VMEM((nf, 2 * frames, margin // 2 + LANES), BF16),
            pltpu.VMEM((nf, 2 * frames, margin // 2 + LANES), BF16),
            pltpu.VMEM((4, BLOCK * chunks // 2, LANES), F32),
            pltpu.VMEM((2, BLOCK * chunks, LANES), F32),
            pltpu.VMEM((sources, foot_n), F32),
            pltpu.VMEM((sources, foot_n), F32),
            pltpu.VMEM((sources, foot_n), F32),
            pltpu.VMEM((sources, foot_n), F32),
            pltpu.VMEM((2, nf * frames, voxels), BF16),
            pltpu.VMEM((2, 4 * BLOCK, depth), BF16),
            pltpu.VMEM((2, 2 * BLOCK, LANES), BF16),
            pltpu.VMEM((2, 4 * BLOCK, LANES), F32),
            pltpu.SemaphoreType.DMA((5,)),
            pltpu.SemaphoreType.DMA((3, nf)),
            pltpu.SemaphoreType.DMA((3, nf)),
            pltpu.SemaphoreType.DMA((2, 2)),
            pltpu.SemaphoreType.DMA((2, 2)),
        ],
        compiler_params=pltpu.CompilerParams(
            collective_id=0, has_side_effects=True, vmem_limit_bytes=32 * 1024 * 1024),
        cost_estimate=pl.CostEstimate(
            flops=2 * sources * 64 * LANES * foot_n, bytes_accessed=500000, transcendentals=0),
    )(*(pltpu.with_memory_space_constraint(x, pltpu.HBM)
        for x in (block_order, movie, traces, voxel_index, footprint)))


def solution(mesh):
    in_specs = (P("frames", "slabs"), P("frames", "slabs"), P("slabs", None), P("slabs", None), P())
    out_specs = P("slabs", None)
    return jax.shard_map(local, mesh=mesh, in_specs=in_specs, out_specs=out_specs, check_vma=False)
```

```python
import functools

import jax
import jax.numpy as jnp
from jax import lax
from jax.experimental import pallas as pl
from jax.experimental.pallas import tpu as pltpu
from jax.sharding import PartitionSpec as P

BLOCK = 8
LANES = 128
STEPS = 32767.0
MESH = pl.DeviceIdType.MESH
F32 = jnp.float32
BF16 = jnp.bfloat16


def dot_nt(left, right):
    return lax.dot_general(left, right, (((1,), (1,)), ((), ())), preferred_element_type=F32)


def dot_nn(left, right):
    return lax.dot_general(left, right, (((1,), (0,)), ((), ())), preferred_element_type=F32)


def halves(value):
    high = value.astype(BF16)
    low = (value - high.astype(F32)).astype(BF16)
    return high, low


def kernel(
    nf, ns, order_in, movie_in, traces_in, index_in, foot_in, out_ref,
    order_ref, movie_ref, traces_ref, index_ref, foot_ref, own, left, right, dense, sent, near,
    hi_s, lo_s, vh_s, vl_s, movie_s, w_s, c_s, inv_s, size_s,
    load_sem, send_m, recv_m, send_d, recv_d,
):
    f = lax.axis_index("frames")
    s = lax.axis_index("slabs")
    has_l = s > 0
    has_r = s < ns - 1
    frames, voxels = movie_ref.shape
    margin = voxels // 2
    extent = 2 * voxels
    chunks = extent // LANES
    half = chunks // 2
    foot_n = foot_ref.shape[1]

    barrier = pltpu.get_barrier_semaphore()
    for d in range(1, nf):
        pl.semaphore_signal(barrier, inc=1, device_id=(lax.rem(f + d, nf), s), device_id_type=MESH)

    @pl.when(has_l)
    def _():
        for d in range(nf):
            pl.semaphore_signal(
                barrier, inc=1, device_id=(lax.rem(f + d, nf), s - 1), device_id_type=MESH)

    @pl.when(has_r)
    def _():
        for d in range(nf):
            pl.semaphore_signal(
                barrier, inc=1, device_id=(lax.rem(f + d, nf), s + 1), device_id_type=MESH)

    pairs = ((index_in, index_ref), (foot_in, foot_ref), (order_in, order_ref),
             (movie_in, movie_ref), (traces_in, traces_ref))
    loads = [pltpu.make_async_copy(a, b, load_sem.at[i]) for i, (a, b) in enumerate(pairs)]
    for load in loads:
        load.start()

    loads[3].wait()
    loads[4].wait()
    quarter = margin // 2
    parts = movie_ref[...].astype(F32)
    for h, at in ((0, 0), (1, quarter + LANES)):
        own[f, :, at:at + quarter] = jnp.concatenate(
            [parts[:, 2 * h * quarter:(2 * h + 1) * quarter],
             parts[:, (2 * h + 1) * quarter:(2 * h + 2) * quarter]], axis=0).astype(BF16)

    @pl.when(jnp.logical_not(has_l))
    def _():
        left[...] = jnp.zeros_like(left)
        near[0] = jnp.full(near.shape[1:], -1, jnp.int32).astype(jnp.int16)

    @pl.when(jnp.logical_not(has_r))
    def _():
        right[...] = jnp.zeros_like(right)
        near[1] = jnp.full(near.shape[1:], -1, jnp.int32).astype(jnp.int16)

    for load in loads[:3]:
        load.wait()
    swap = order_ref[0] != 0

    def permuted(ref):
        a = ref[0:BLOCK, :]
        b = ref[BLOCK:2 * BLOCK, :]
        return jnp.concatenate([jnp.where(swap, b, a), jnp.where(swap, a, b)], axis=0)

    index = permuted(index_ref)
    value = permuted(foot_ref)
    hi_s[...] = (index >> 7).astype(F32)
    lo_s[...] = (index & (LANES - 1)).astype(F32)
    v_hi = value.astype(BF16).astype(F32)
    vl_s[...] = value - v_hi
    vh_s[...] = jnp.where(v_hi == 0.0, -1.0, v_hi)

    largest = jnp.max(value, axis=1, keepdims=True) * 1.01 + 1e-30
    largest = jnp.broadcast_to(largest, (2 * BLOCK, LANES)).astype(BF16).astype(F32)
    unit = STEPS / largest
    lane8 = lax.broadcasted_iota(jnp.int32, (BLOCK, LANES), 1)
    lead = jnp.concatenate(
        [traces_ref[...].astype(F32), jnp.zeros((frames, LANES - 2 * BLOCK), F32)], axis=1)
    own[f, :, quarter:quarter + LANES] = jnp.concatenate(
        [lead, jnp.where(lane8 < LANES // 2, largest[:BLOCK], largest[BLOCK:])],
        axis=0).astype(BF16)

    def peer(d):
        to = lax.rem(f + d, nf)
        return pltpu.make_async_remote_copy(
            src_ref=own.at[f], dst_ref=own.at[f], send_sem=send_m.at[0, to],
            recv_sem=recv_m.at[0, f], device_id=(to, s), device_id_type=MESH)

    def to_right(d):
        to = lax.rem(f + d, nf)
        return pltpu.make_async_remote_copy(
            src_ref=own.at[f, :, pl.ds(quarter, quarter + LANES)], dst_ref=left.at[f],
            send_sem=send_m.at[1, to], recv_sem=recv_m.at[1, f],
            device_id=(to, s + 1), device_id_type=MESH)

    def to_left(d):
        to = lax.rem(f + d, nf)
        return pltpu.make_async_remote_copy(
            src_ref=own.at[f, :, pl.ds(0, quarter + LANES)], dst_ref=right.at[f],
            send_sem=send_m.at[2, to], recv_sem=recv_m.at[2, f],
            device_id=(to, s - 1), device_id_type=MESH)

    rows16 = 2 * BLOCK
    iota = lax.broadcasted_iota(jnp.int32, (rows16, foot_n), 0).astype(F32)
    span = half * BLOCK

    def dense_right(b):
        return pltpu.make_async_remote_copy(
            src_ref=sent.at[2 * b + 1], dst_ref=near.at[0, pl.ds(b * span, span), :],
            send_sem=send_d.at[0, b], recv_sem=recv_d.at[0, b],
            device_id=(f, s + 1), device_id_type=MESH)

    def dense_left(b):
        return pltpu.make_async_remote_copy(
            src_ref=sent.at[2 * b], dst_ref=near.at[1, pl.ds(b * span, span), :],
            send_sem=send_d.at[1, b], recv_sem=recv_d.at[1, b],
            device_id=(f, s - 1), device_id_type=MESH)

    for b in range(2):
        def scatter_row(k, b=b):
            row = pl.ds(b * BLOCK + k, 1)

            def spread(ref):
                return jnp.broadcast_to(ref[row, :], (rows16, foot_n)).astype(BF16)

            hi = spread(hi_s)
            lo = spread(lo_s)
            vh = spread(vh_s)
            vl = spread(vl_s)
            zero = jnp.zeros((rows16, foot_n), BF16)
            one = jnp.ones((rows16, foot_n), BF16)
            iota16 = iota.astype(BF16)
            low = [jnp.where(lo == iota16 + BF16(16 * t), one, zero) for t in range(LANES // 16)]
            high = [hi == iota16 + BF16(16 * t) for t in range(chunks // 16)]
            lhs = [jnp.where(m, vh, zero) for m in high] + [jnp.where(m, vl, zero) for m in high]
            got = dot_nt(jnp.concatenate(lhs, axis=0), jnp.concatenate(low, axis=0))
            g_hi = got[:chunks]
            enc = jnp.where(g_hi == 0.0, -1.0, jnp.maximum(g_hi, 0.0) + got[chunks:])
            dense[2 * b, pl.ds(k, half, stride=BLOCK), :] = enc[:half]
            dense[2 * b + 1, pl.ds(k, half, stride=BLOCK), :] = enc[half:]

        for k in range(BLOCK):
            scatter_row(k)

            if b == 0 and k == BLOCK // 2 - 1:
                count = nf - 1 + nf * has_l.astype(jnp.int32) + nf * has_r.astype(jnp.int32)
                pl.semaphore_wait(barrier, count)

                for d in range(1, nf):
                    peer(d).start()

                @pl.when(has_r)
                def _():
                    for d in range(nf):
                        to_right(d).start()

                @pl.when(has_l)
                def _():
                    for d in range(nf):
                        to_left(d).start()

        for side in range(2):
            values = dense[2 * b + side].reshape(half, BLOCK, LANES)
            steps = jnp.where(values < 0.0, -1.0, values * unit[b * BLOCK:(b + 1) * BLOCK] + 0.5)
            sent[2 * b + side] = steps.reshape(span, LANES).astype(jnp.int32).astype(jnp.int16)

        @pl.when(has_r)
        def _(b=b):
            dense_right(b).start()

        @pl.when(has_l)
        def _(b=b):
            dense_left(b).start()

    for d in range(1, nf):
        pltpu.make_async_remote_copy(
            src_ref=own.at[f], dst_ref=own.at[lax.rem(f + d, nf)], send_sem=send_m.at[0, 0],
            recv_sem=recv_m.at[0, lax.rem(f + d, nf)], device_id=(f, s),
            device_id_type=MESH).wait_recv()

    @pl.when(has_l)
    def _():
        for d in range(nf):
            pltpu.make_async_remote_copy(
                src_ref=left.at[d], dst_ref=left.at[d], send_sem=send_m.at[1, 0],
                recv_sem=recv_m.at[1, d], device_id=(f, s), device_id_type=MESH).wait_recv()

    @pl.when(has_r)
    def _():
        for d in range(nf):
            pltpu.make_async_remote_copy(
                src_ref=right.at[d], dst_ref=right.at[d], send_sem=send_m.at[2, 0],
                recv_sem=recv_m.at[2, d], device_id=(f, s), device_id_type=MESH).wait_recv()

    def all_frames(pick):
        return jnp.concatenate([pick(g) for g in range(nf)], axis=0)

    def unpacked(ref, at):
        def one(g):
            both = ref[g, :, at:at + quarter].astype(F32)
            return jnp.concatenate([both[:frames], both[frames:]], axis=1)
        return all_frames(one)

    def trace_rows(ref, at):
        return lambda g: ref[g, :, at:at + LANES].astype(F32)[:frames]

    movie_l = jnp.concatenate([unpacked(left, LANES), unpacked(own, 0)], axis=1).astype(BF16)
    movie_r = jnp.concatenate(
        [unpacked(own, quarter + LANES), unpacked(right, 0)], axis=1).astype(BF16)
    total = nf * frames
    padding = jnp.zeros((LANES - total, LANES), F32)
    eye = (lax.broadcasted_iota(jnp.int32, (rows16, LANES), 0)
           == lax.broadcasted_iota(jnp.int32, (rows16, LANES), 1)).astype(F32).astype(BF16)

    def by_source(pick):
        block = jnp.concatenate([all_frames(pick), padding], axis=0).astype(BF16)
        rows = dot_nt(eye, block)
        return jnp.concatenate([jnp.where(swap, rows[BLOCK:], rows[:BLOCK]),
                                jnp.where(swap, rows[:BLOCK], rows[BLOCK:])], axis=0)

    t_own = by_source(trace_rows(own, quarter))
    t_left = by_source(trace_rows(left, 0))
    t_right = by_source(trace_rows(right, quarter))

    depth = -(-(total + 3 * 32) // LANES) * LANES
    identity = (lax.broadcasted_iota(jnp.int32, (total, LANES), 0)
                == lax.broadcasted_iota(jnp.int32, (total, LANES), 1)).astype(F32)

    def weights(t_near):
        t32 = jnp.concatenate([t_own, t_near], axis=0)
        stacked = jnp.concatenate(
            [identity, t32, t32, t32,
             jnp.zeros((depth - total - 96, LANES), F32)], axis=0).astype(BF16)
        full = dot_nt(t32.astype(BF16), stacked)
        lane = lax.broadcasted_iota(jnp.int32, full.shape, 1)
        g_hi = full.astype(BF16).astype(F32)
        picked = jnp.where((lane >= total + 32) & (lane < total + 64), full - g_hi, g_hi)
        first = jnp.where(lane < total, full, -picked).astype(BF16)
        t_f = jnp.concatenate([t32[0:8], t32[16:24]], axis=0)
        t_s = jnp.concatenate([t32[8:16], t32[24:32]], axis=0)
        stacked2 = jnp.concatenate(
            [t_f, t_f, t_f, jnp.zeros((LANES - 48, LANES), F32)], axis=0).astype(BF16)
        cross = dot_nt(t_s.astype(BF16), stacked2)
        lane2 = lax.broadcasted_iota(jnp.int32, cross.shape, 1)
        row2 = lax.broadcasted_iota(jnp.int32, cross.shape, 0)
        c_hi = cross.astype(BF16).astype(F32)
        picked2 = jnp.where((lane2 >= 16) & (lane2 < 32), cross - c_hi, c_hi)
        same = (row2 // 8) == ((lane2 // 8) % 2)
        second = jnp.where(same, picked2, 0.0).astype(BF16)
        inverse = 1.0 / (jnp.sum(t32 * t32, axis=1, keepdims=True) + 1.0)
        return first, second, inverse

    for side, (movie, t_near) in enumerate(((movie_l, t_left), (movie_r, t_right))):
        w, c, inverse = weights(t_near)
        movie_s[side] = movie
        w_s[side] = w
        c_s[side] = c
        inv_s[side] = jnp.broadcast_to(inverse, (4 * BLOCK, LANES))
        block = ((left, 0), (right, quarter))[side]
        scales = block[0][0, :, block[1]:block[1] + LANES].astype(F32)[frames:] * (1.0 / STEPS)
        size_s[side] = jnp.concatenate(
            [jnp.broadcast_to(scales[:, 0:1], (BLOCK, LANES)),
             jnp.broadcast_to(scales[:, LANES // 2:LANES // 2 + 1], (BLOCK, LANES))], axis=0)

    tiles = foot_n // LANES
    places = [[index_ref[b * BLOCK:(b + 1) * BLOCK, j * LANES:(j + 1) * LANES]
               for j in range(tiles)] for b in range(2)]
    taken = [[jnp.zeros((BLOCK, LANES), F32)] * tiles for b in range(2)]

    early = 1 - lax.rem(s, 2)
    for side in (early, 1 - early):
        @pl.when(jnp.where(side == 0, s, ns - 1 - s) > 0)
        def _(side=side):
            for b in range(2):
                pltpu.make_async_remote_copy(
                    src_ref=near.at[side, pl.ds(b * span, span), :],
                    dst_ref=near.at[side, pl.ds(b * span, span), :],
                    send_sem=send_d.at[0, 0], recv_sem=recv_d.at[side, b],
                    device_id=(f, s), device_id_type=MESH).wait_recv()

        def wide(ref, at, start):
            return jnp.concatenate(
                [ref[at, (start + c) * BLOCK:(start + c + 1) * BLOCK, :] for c in range(half)],
                axis=1)

        movie = movie_s[side]
        w = w_s[side][:, :total + 96]
        cross = c_s[side][:, :48]
        inverse = inv_s[side][:, 0:1]
        steps = near[side].astype(jnp.int32).astype(F32).reshape(2, half, BLOCK, LANES)
        size = size_s[side]
        enc = [wide(dense, side, 0), wide(dense, 2 + side, 0)]
        for b in range(2):
            enc.append(jnp.concatenate(
                [steps[b, c] * size[b * BLOCK:(b + 1) * BLOCK] for c in range(half)], axis=1))
        mask = [(e >= 0.0).astype(F32) for e in enc]
        state = [jnp.maximum(e, 0.0) for e in enc]

        def residual(w_rows, state):
            high, low = halves(jnp.concatenate(state, axis=0))
            return dot_nn(w_rows, jnp.concatenate([movie, high, high, low], axis=0))

        def change(c_rows, old, new):
            high, low = halves(jnp.concatenate([n - o for n, o in zip(new, old)], axis=0))
            return dot_nn(c_rows, jnp.concatenate([high, high, low], axis=0))

        def step(i, rest):
            return mask[i] * jnp.maximum(state[i] + rest * inverse[8 * i:8 * i + 8], 0.0)

        rest = residual(w, state)
        new_f = [step(0, rest[0:8]), step(2, rest[16:24])]
        moved = change(cross, [state[0], state[2]], new_f)
        new_s = [step(1, rest[8:16] - moved[0:8]), step(3, rest[24:32] - moved[8:16])]
        state = [new_f[0], new_s[0], new_f[1], new_s[1]]
        rest = residual(w[0:16], state)
        new_f = step(0, rest[0:8])
        moved = change(cross, [state[0], state[2]], [new_f, state[2]])
        new_s = step(1, rest[8:16] - moved[0:8])
        done = (jnp.where(swap, new_s, new_f), jnp.where(swap, new_f, new_s))
        for b in range(2):
            for j in range(tiles):
                chunk = (places[b][j] >> 7) - half * side
                lane = places[b][j] & (LANES - 1)
                for c in range(half):
                    tile = done[b][:, c * LANES:(c + 1) * LANES]
                    got = jnp.take_along_axis(tile, lane, axis=1, mode="promise_in_bounds")
                    taken[b][j] = jnp.where(chunk == c, got, taken[b][j])

    for b in range(2):
        for j in range(tiles):
            out_ref[b * BLOCK:(b + 1) * BLOCK, j * LANES:(j + 1) * LANES] = taken[b][j]

    for d in range(1, nf):
        peer(d).wait_send()

    @pl.when(has_r)
    def _():
        for d in range(nf):
            to_right(d).wait_send()
        for b in range(2):
            dense_right(b).wait_send()

    @pl.when(has_l)
    def _():
        for d in range(nf):
            to_left(d).wait_send()
        for b in range(2):
            dense_left(b).wait_send()


def local(movie, traces, voxel_index, footprint, block_order):
    nf = lax.axis_size("frames")
    ns = lax.axis_size("slabs")
    frames, voxels = movie.shape
    sources, foot_n = footprint.shape
    margin = voxels // 2
    chunks = 2 * voxels // LANES
    depth = -(-(nf * frames + 3 * 32) // LANES) * LANES
    vmem = pl.BlockSpec(memory_space=pltpu.VMEM)
    return pl.pallas_call(
        functools.partial(kernel, nf, ns),
        out_shape=pltpu.VMEM((sources, foot_n), F32),
        in_specs=[pl.BlockSpec(memory_space=pltpu.HBM)] * 5,
        out_specs=vmem,
        scratch_shapes=[
            pltpu.SMEM(block_order.shape, block_order.dtype),
            pltpu.VMEM(movie.shape, movie.dtype),
            pltpu.VMEM(traces.shape, traces.dtype),
            pltpu.VMEM(voxel_index.shape, voxel_index.dtype),
            pltpu.VMEM(footprint.shape, footprint.dtype),
            pltpu.VMEM((nf, 2 * frames, margin + LANES), BF16),
            pltpu.VMEM((nf, 2 * frames, margin // 2 + LANES), BF16),
            pltpu.VMEM((nf, 2 * frames, margin // 2 + LANES), BF16),
            pltpu.VMEM((4, BLOCK * chunks // 2, LANES), F32),
            pltpu.VMEM((4, BLOCK * chunks // 2, LANES), jnp.int16),
            pltpu.VMEM((2, BLOCK * chunks, LANES), jnp.int16),
            pltpu.VMEM((sources, foot_n), F32),
            pltpu.VMEM((sources, foot_n), F32),
            pltpu.VMEM((sources, foot_n), F32),
            pltpu.VMEM((sources, foot_n), F32),
            pltpu.VMEM((2, nf * frames, voxels), BF16),
            pltpu.VMEM((2, 4 * BLOCK, depth), BF16),
            pltpu.VMEM((2, 2 * BLOCK, LANES), BF16),
            pltpu.VMEM((2, 4 * BLOCK, LANES), F32),
            pltpu.VMEM((2, 2 * BLOCK, LANES), F32),
            pltpu.SemaphoreType.DMA((5,)),
            pltpu.SemaphoreType.DMA((3, nf)),
            pltpu.SemaphoreType.DMA((3, nf)),
            pltpu.SemaphoreType.DMA((2, 2)),
            pltpu.SemaphoreType.DMA((2, 2)),
        ],
        compiler_params=pltpu.CompilerParams(
            collective_id=0, has_side_effects=True, vmem_limit_bytes=32 * 1024 * 1024),
        cost_estimate=pl.CostEstimate(
            flops=2 * sources * 64 * LANES * foot_n, bytes_accessed=500000, transcendentals=0),
    )(*(pltpu.with_memory_space_constraint(x, pltpu.HBM)
        for x in (block_order, movie, traces, voxel_index, footprint)))


def solution(mesh):
    in_specs = (P("frames", "slabs"), P("frames", "slabs"), P("slabs", None), P("slabs", None), P())
    out_specs = P("slabs", None)
    return jax.shard_map(local, mesh=mesh, in_specs=in_specs, out_specs=out_specs, check_vma=False)
```

```python
import functools

import jax
import jax.numpy as jnp
from jax import lax
from jax.experimental import pallas as pl
from jax.experimental.pallas import tpu as pltpu
from jax.sharding import PartitionSpec as P

BLOCK = 8
LANES = 128
STEPS = 32767.0
MESH = pl.DeviceIdType.MESH
F32 = jnp.float32
BF16 = jnp.bfloat16


def dot_nt(left, right):
    return lax.dot_general(left, right, (((1,), (1,)), ((), ())), preferred_element_type=F32)


def dot_nn(left, right):
    return lax.dot_general(left, right, (((1,), (0,)), ((), ())), preferred_element_type=F32)


def halves(value):
    high = value.astype(BF16)
    low = (value - high.astype(F32)).astype(BF16)
    return high, low


def kernel(
    nf, ns, order_in, movie_in, traces_in, index_in, foot_in, out_ref,
    order_ref, movie_ref, traces_ref, index_ref, foot_ref, own, left, right, dense, sent, near,
    hi_s, lo_s, vh_s, vl_s, movie_s, w_s, c_s, inv_s, size_s, unit_s,
    load_sem, send_m, recv_m, send_d, recv_d,
):
    f = lax.axis_index("frames")
    s = lax.axis_index("slabs")
    has_l = s > 0
    has_r = s < ns - 1
    frames, voxels = movie_ref.shape
    margin = voxels // 2
    extent = 2 * voxels
    chunks = extent // LANES
    half = chunks // 2
    foot_n = foot_ref.shape[1]

    barrier = pltpu.get_barrier_semaphore()
    for d in range(1, nf):
        pl.semaphore_signal(barrier, inc=1, device_id=(lax.rem(f + d, nf), s), device_id_type=MESH)

    @pl.when(has_l)
    def _():
        for d in range(nf):
            pl.semaphore_signal(
                barrier, inc=1, device_id=(lax.rem(f + d, nf), s - 1), device_id_type=MESH)

    @pl.when(has_r)
    def _():
        for d in range(nf):
            pl.semaphore_signal(
                barrier, inc=1, device_id=(lax.rem(f + d, nf), s + 1), device_id_type=MESH)

    pairs = ((index_in, index_ref), (foot_in, foot_ref), (order_in, order_ref),
             (movie_in, movie_ref), (traces_in, traces_ref))
    loads = [pltpu.make_async_copy(a, b, load_sem.at[i]) for i, (a, b) in enumerate(pairs)]
    for load in loads:
        load.start()

    loads[3].wait()
    loads[4].wait()
    quarter = margin // 2
    parts = movie_ref[...].astype(F32)
    for h, at in ((0, 0), (1, quarter + LANES)):
        own[f, :, at:at + quarter] = jnp.concatenate(
            [parts[:, 2 * h * quarter:(2 * h + 1) * quarter],
             parts[:, (2 * h + 1) * quarter:(2 * h + 2) * quarter]], axis=0).astype(BF16)

    @pl.when(jnp.logical_not(has_l))
    def _():
        left[...] = jnp.zeros_like(left)
        near[0] = jnp.full(near.shape[1:], -1, jnp.int32).astype(jnp.int16)

    @pl.when(jnp.logical_not(has_r))
    def _():
        right[...] = jnp.zeros_like(right)
        near[1] = jnp.full(near.shape[1:], -1, jnp.int32).astype(jnp.int16)

    for load in loads[:3]:
        load.wait()
    swap = order_ref[0] != 0

    def permuted(ref):
        a = ref[0:BLOCK, :]
        b = ref[BLOCK:2 * BLOCK, :]
        return jnp.concatenate([jnp.where(swap, b, a), jnp.where(swap, a, b)], axis=0)

    index = permuted(index_ref)
    value = permuted(foot_ref)
    v_hi = value.astype(BF16).astype(F32)
    for ref, rows in ((hi_s, (index >> 7).astype(F32)),
                      (lo_s, (index & (LANES - 1)).astype(F32)),
                      (vl_s, value - v_hi),
                      (vh_s, jnp.where(v_hi == 0.0, -1.0, v_hi))):
        ref[0] = rows[:BLOCK]
        ref[1] = rows[BLOCK:]

    largest = jnp.max(value, axis=1, keepdims=True) * 1.01 + 1e-30
    largest = jnp.broadcast_to(largest, (2 * BLOCK, LANES)).astype(BF16).astype(F32)
    unit_s[0] = STEPS / largest[:BLOCK]
    unit_s[1] = STEPS / largest[BLOCK:]
    lane8 = lax.broadcasted_iota(jnp.int32, (BLOCK, LANES), 1)
    lead = jnp.concatenate(
        [traces_ref[...].astype(F32), jnp.zeros((frames, LANES - 2 * BLOCK), F32)], axis=1)
    own[f, :, quarter:quarter + LANES] = jnp.concatenate(
        [lead, jnp.where(lane8 < LANES // 2, largest[:BLOCK], largest[BLOCK:])],
        axis=0).astype(BF16)

    def peer(d):
        to = lax.rem(f + d, nf)
        return pltpu.make_async_remote_copy(
            src_ref=own.at[f], dst_ref=own.at[f], send_sem=send_m.at[0, to],
            recv_sem=recv_m.at[0, f], device_id=(to, s), device_id_type=MESH)

    def to_right(d):
        to = lax.rem(f + d, nf)
        return pltpu.make_async_remote_copy(
            src_ref=own.at[f, :, pl.ds(quarter, quarter + LANES)], dst_ref=left.at[f],
            send_sem=send_m.at[1, to], recv_sem=recv_m.at[1, f],
            device_id=(to, s + 1), device_id_type=MESH)

    def to_left(d):
        to = lax.rem(f + d, nf)
        return pltpu.make_async_remote_copy(
            src_ref=own.at[f, :, pl.ds(0, quarter + LANES)], dst_ref=right.at[f],
            send_sem=send_m.at[2, to], recv_sem=recv_m.at[2, f],
            device_id=(to, s - 1), device_id_type=MESH)

    rows16 = 2 * BLOCK
    iota = lax.broadcasted_iota(jnp.int32, (rows16, foot_n), 0).astype(F32)
    span = half * BLOCK

    def dense_right(b):
        return pltpu.make_async_remote_copy(
            src_ref=sent.at[2 * b + 1], dst_ref=near.at[0, pl.ds(b * span, span), :],
            send_sem=send_d.at[0, b], recv_sem=recv_d.at[0, b],
            device_id=(f, s + 1), device_id_type=MESH)

    def dense_left(b):
        return pltpu.make_async_remote_copy(
            src_ref=sent.at[2 * b], dst_ref=near.at[1, pl.ds(b * span, span), :],
            send_sem=send_d.at[1, b], recv_sem=recv_d.at[1, b],
            device_id=(f, s - 1), device_id_type=MESH)

    def scatter_block(b, carry):
        def scatter_row(k):

            def spread(ref):
                return jnp.broadcast_to(ref[b, k:k + 1, :], (rows16, foot_n)).astype(BF16)

            hi = spread(hi_s)
            lo = spread(lo_s)
            vh = spread(vh_s)
            vl = spread(vl_s)
            zero = jnp.zeros((rows16, foot_n), BF16)
            one = jnp.ones((rows16, foot_n), BF16)
            iota16 = iota.astype(BF16)
            low = [jnp.where(lo == iota16 + BF16(16 * t), one, zero) for t in range(LANES // 16)]
            high = [hi == iota16 + BF16(16 * t) for t in range(chunks // 16)]
            lhs = [jnp.where(m, vh, zero) for m in high] + [jnp.where(m, vl, zero) for m in high]
            got = dot_nt(jnp.concatenate(lhs, axis=0), jnp.concatenate(low, axis=0))
            g_hi = got[:chunks]
            enc = jnp.where(g_hi == 0.0, -1.0, jnp.maximum(g_hi, 0.0) + got[chunks:])
            dense[2 * b, pl.ds(k, half, stride=BLOCK), :] = enc[:half]
            dense[2 * b + 1, pl.ds(k, half, stride=BLOCK), :] = enc[half:]

        for k in range(BLOCK):
            scatter_row(k)

            if k == BLOCK // 2 - 1:
                @pl.when(b == 0)
                def _():
                    count = nf - 1 + nf * has_l.astype(jnp.int32) + nf * has_r.astype(jnp.int32)
                    pl.semaphore_wait(barrier, count)

                    for d in range(1, nf):
                        peer(d).start()

                    @pl.when(has_r)
                    def _():
                        for d in range(nf):
                            to_right(d).start()

                    @pl.when(has_l)
                    def _():
                        for d in range(nf):
                            to_left(d).start()

        for side in range(2):
            values = dense[2 * b + side].reshape(half, BLOCK, LANES)
            steps = jnp.where(values < 0.0, -1.0, values * unit_s[b] + 0.5)
            sent[2 * b + side] = steps.reshape(span, LANES).astype(jnp.int32).astype(jnp.int16)

        @pl.when(has_r)
        def _():
            dense_right(b).start()

        @pl.when(has_l)
        def _():
            dense_left(b).start()

        return carry

    lax.fori_loop(0, 2, scatter_block, 0)

    for d in range(1, nf):
        pltpu.make_async_remote_copy(
            src_ref=own.at[f], dst_ref=own.at[lax.rem(f + d, nf)], send_sem=send_m.at[0, 0],
            recv_sem=recv_m.at[0, lax.rem(f + d, nf)], device_id=(f, s),
            device_id_type=MESH).wait_recv()

    @pl.when(has_l)
    def _():
        for d in range(nf):
            pltpu.make_async_remote_copy(
                src_ref=left.at[d], dst_ref=left.at[d], send_sem=send_m.at[1, 0],
                recv_sem=recv_m.at[1, d], device_id=(f, s), device_id_type=MESH).wait_recv()

    @pl.when(has_r)
    def _():
        for d in range(nf):
            pltpu.make_async_remote_copy(
                src_ref=right.at[d], dst_ref=right.at[d], send_sem=send_m.at[2, 0],
                recv_sem=recv_m.at[2, d], device_id=(f, s), device_id_type=MESH).wait_recv()

    def all_frames(pick):
        return jnp.concatenate([pick(g) for g in range(nf)], axis=0)

    def unpacked(ref, at):
        def one(g):
            both = ref[g, :, at:at + quarter].astype(F32)
            return jnp.concatenate([both[:frames], both[frames:]], axis=1)
        return all_frames(one)

    def trace_rows(ref, at):
        return lambda g: ref[g, :, at:at + LANES].astype(F32)[:frames]

    movie_l = jnp.concatenate([unpacked(left, LANES), unpacked(own, 0)], axis=1).astype(BF16)
    movie_r = jnp.concatenate(
        [unpacked(own, quarter + LANES), unpacked(right, 0)], axis=1).astype(BF16)
    total = nf * frames
    padding = jnp.zeros((LANES - total, LANES), F32)
    eye = (lax.broadcasted_iota(jnp.int32, (rows16, LANES), 0)
           == lax.broadcasted_iota(jnp.int32, (rows16, LANES), 1)).astype(F32).astype(BF16)

    def by_source(pick):
        block = jnp.concatenate([all_frames(pick), padding], axis=0).astype(BF16)
        rows = dot_nt(eye, block)
        return jnp.concatenate([jnp.where(swap, rows[BLOCK:], rows[:BLOCK]),
                                jnp.where(swap, rows[:BLOCK], rows[BLOCK:])], axis=0)

    t_own = by_source(trace_rows(own, quarter))
    t_left = by_source(trace_rows(left, 0))
    t_right = by_source(trace_rows(right, quarter))

    depth = -(-(total + 3 * 32) // LANES) * LANES
    identity = (lax.broadcasted_iota(jnp.int32, (total, LANES), 0)
                == lax.broadcasted_iota(jnp.int32, (total, LANES), 1)).astype(F32)

    def weights(t_near):
        t32 = jnp.concatenate([t_own, t_near], axis=0)
        stacked = jnp.concatenate(
            [identity, t32, t32, t32,
             jnp.zeros((depth - total - 96, LANES), F32)], axis=0).astype(BF16)
        full = dot_nt(t32.astype(BF16), stacked)
        lane = lax.broadcasted_iota(jnp.int32, full.shape, 1)
        g_hi = full.astype(BF16).astype(F32)
        picked = jnp.where((lane >= total + 32) & (lane < total + 64), full - g_hi, g_hi)
        first = jnp.where(lane < total, full, -picked).astype(BF16)
        t_f = jnp.concatenate([t32[0:8], t32[16:24]], axis=0)
        t_s = jnp.concatenate([t32[8:16], t32[24:32]], axis=0)
        stacked2 = jnp.concatenate(
            [t_f, t_f, t_f, jnp.zeros((LANES - 48, LANES), F32)], axis=0).astype(BF16)
        cross = dot_nt(t_s.astype(BF16), stacked2)
        lane2 = lax.broadcasted_iota(jnp.int32, cross.shape, 1)
        row2 = lax.broadcasted_iota(jnp.int32, cross.shape, 0)
        c_hi = cross.astype(BF16).astype(F32)
        picked2 = jnp.where((lane2 >= 16) & (lane2 < 32), cross - c_hi, c_hi)
        same = (row2 // 8) == ((lane2 // 8) % 2)
        second = jnp.where(same, picked2, 0.0).astype(BF16)
        inverse = 1.0 / (jnp.sum(t32 * t32, axis=1, keepdims=True) + 1.0)
        return first, second, inverse

    for side, (movie, t_near) in enumerate(((movie_l, t_left), (movie_r, t_right))):
        w, c, inverse = weights(t_near)
        movie_s[side] = movie
        w_s[side] = w
        c_s[side] = c
        inv_s[side] = jnp.broadcast_to(inverse, (4 * BLOCK, LANES))
        block = ((left, 0), (right, quarter))[side]
        scales = block[0][0, :, block[1]:block[1] + LANES].astype(F32)[frames:] * (1.0 / STEPS)
        size_s[side] = jnp.concatenate(
            [jnp.broadcast_to(scales[:, 0:1], (BLOCK, LANES)),
             jnp.broadcast_to(scales[:, LANES // 2:LANES // 2 + 1], (BLOCK, LANES))], axis=0)

    tiles = foot_n // LANES
    out_ref[...] = jnp.zeros_like(out_ref)

    early = 1 - lax.rem(s, 2)

    def one_side(i, carry):
        side = jnp.where(i == 0, early, 1 - early)

        @pl.when(jnp.where(side == 0, s, ns - 1 - s) > 0)
        def _():
            for b in range(2):
                pltpu.make_async_remote_copy(
                    src_ref=near.at[side, pl.ds(b * span, span), :],
                    dst_ref=near.at[side, pl.ds(b * span, span), :],
                    send_sem=send_d.at[0, 0], recv_sem=recv_d.at[side, b],
                    device_id=(f, s), device_id_type=MESH).wait_recv()

        def wide(ref, at, start):
            return jnp.concatenate(
                [ref[at, (start + c) * BLOCK:(start + c + 1) * BLOCK, :] for c in range(half)],
                axis=1)

        movie = movie_s[side]
        w = w_s[side][:, :total + 96]
        cross = c_s[side][:, :48]
        inverse = inv_s[side][:, 0:1]
        steps = near[side].astype(jnp.int32).astype(F32).reshape(2, half, BLOCK, LANES)
        size = size_s[side]
        enc = [wide(dense, side, 0), wide(dense, 2 + side, 0)]
        for b in range(2):
            enc.append(jnp.concatenate(
                [steps[b, c] * size[b * BLOCK:(b + 1) * BLOCK] for c in range(half)], axis=1))
        mask = [(e >= 0.0).astype(F32) for e in enc]
        state = [jnp.maximum(e, 0.0) for e in enc]

        def residual(w_rows, state):
            high, low = halves(jnp.concatenate(state, axis=0))
            return dot_nn(w_rows, jnp.concatenate([movie, high, high, low], axis=0))

        def change(c_rows, old, new):
            high, low = halves(jnp.concatenate([n - o for n, o in zip(new, old)], axis=0))
            return dot_nn(c_rows, jnp.concatenate([high, high, low], axis=0))

        def step(i, rest):
            return mask[i] * jnp.maximum(state[i] + rest * inverse[8 * i:8 * i + 8], 0.0)

        rest = residual(w, state)
        new_f = [step(0, rest[0:8]), step(2, rest[16:24])]
        moved = change(cross, [state[0], state[2]], new_f)
        new_s = [step(1, rest[8:16] - moved[0:8]), step(3, rest[24:32] - moved[8:16])]
        state = [new_f[0], new_s[0], new_f[1], new_s[1]]
        rest = residual(w[0:16], state)
        new_f = step(0, rest[0:8])
        moved = change(cross, [state[0], state[2]], [new_f, state[2]])
        new_s = step(1, rest[8:16] - moved[0:8])
        done = (jnp.where(swap, new_s, new_f), jnp.where(swap, new_f, new_s))
        for b in range(2):
            for j in range(tiles):
                at = (slice(b * BLOCK, (b + 1) * BLOCK), slice(j * LANES, (j + 1) * LANES))
                place = index_ref[at]
                chunk = (place >> 7) - half * side
                lane = place & (LANES - 1)
                taken = out_ref[at]
                for c in range(half):
                    tile = done[b][:, c * LANES:(c + 1) * LANES]
                    got = jnp.take_along_axis(tile, lane, axis=1, mode="promise_in_bounds")
                    taken = jnp.where(chunk == c, got, taken)
                out_ref[at] = taken
        return carry

    lax.fori_loop(0, 2, one_side, 0)

    for d in range(1, nf):
        peer(d).wait_send()

    @pl.when(has_r)
    def _():
        for d in range(nf):
            to_right(d).wait_send()
        for b in range(2):
            dense_right(b).wait_send()

    @pl.when(has_l)
    def _():
        for d in range(nf):
            to_left(d).wait_send()
        for b in range(2):
            dense_left(b).wait_send()


def local(movie, traces, voxel_index, footprint, block_order):
    nf = lax.axis_size("frames")
    ns = lax.axis_size("slabs")
    frames, voxels = movie.shape
    sources, foot_n = footprint.shape
    margin = voxels // 2
    chunks = 2 * voxels // LANES
    depth = -(-(nf * frames + 3 * 32) // LANES) * LANES
    vmem = pl.BlockSpec(memory_space=pltpu.VMEM)
    return pl.pallas_call(
        functools.partial(kernel, nf, ns),
        out_shape=pltpu.VMEM((sources, foot_n), F32),
        in_specs=[pl.BlockSpec(memory_space=pltpu.HBM)] * 5,
        out_specs=vmem,
        scratch_shapes=[
            pltpu.SMEM(block_order.shape, block_order.dtype),
            pltpu.VMEM(movie.shape, movie.dtype),
            pltpu.VMEM(traces.shape, traces.dtype),
            pltpu.VMEM(voxel_index.shape, voxel_index.dtype),
            pltpu.VMEM(footprint.shape, footprint.dtype),
            pltpu.VMEM((nf, 2 * frames, margin + LANES), BF16),
            pltpu.VMEM((nf, 2 * frames, margin // 2 + LANES), BF16),
            pltpu.VMEM((nf, 2 * frames, margin // 2 + LANES), BF16),
            pltpu.VMEM((4, BLOCK * chunks // 2, LANES), F32),
            pltpu.VMEM((4, BLOCK * chunks // 2, LANES), jnp.int16),
            pltpu.VMEM((2, BLOCK * chunks, LANES), jnp.int16),
            pltpu.VMEM((2, BLOCK, foot_n), F32),
            pltpu.VMEM((2, BLOCK, foot_n), F32),
            pltpu.VMEM((2, BLOCK, foot_n), F32),
            pltpu.VMEM((2, BLOCK, foot_n), F32),
            pltpu.VMEM((2, nf * frames, voxels), BF16),
            pltpu.VMEM((2, 4 * BLOCK, depth), BF16),
            pltpu.VMEM((2, 2 * BLOCK, LANES), BF16),
            pltpu.VMEM((2, 4 * BLOCK, LANES), F32),
            pltpu.VMEM((2, 2 * BLOCK, LANES), F32),
            pltpu.VMEM((2, BLOCK, LANES), F32),
            pltpu.SemaphoreType.DMA((5,)),
            pltpu.SemaphoreType.DMA((3, nf)),
            pltpu.SemaphoreType.DMA((3, nf)),
            pltpu.SemaphoreType.DMA((2, 2)),
            pltpu.SemaphoreType.DMA((2, 2)),
        ],
        compiler_params=pltpu.CompilerParams(
            collective_id=0, has_side_effects=True, vmem_limit_bytes=32 * 1024 * 1024),
        cost_estimate=pl.CostEstimate(
            flops=2 * sources * 64 * LANES * foot_n, bytes_accessed=500000, transcendentals=0),
    )(*(pltpu.with_memory_space_constraint(x, pltpu.HBM)
        for x in (block_order, movie, traces, voxel_index, footprint)))


def solution(mesh):
    in_specs = (P("frames", "slabs"), P("frames", "slabs"), P("slabs", None), P("slabs", None), P())
    out_specs = P("slabs", None)
    return jax.shard_map(local, mesh=mesh, in_specs=in_specs, out_specs=out_specs, check_vma=False)
```

```python
import functools

import jax
import jax.numpy as jnp
from jax import lax
from jax.experimental import pallas as pl
from jax.experimental.pallas import tpu as pltpu
from jax.sharding import PartitionSpec as P

BLOCK = 8
LANES = 128
STEPS = 32767.0
MESH = pl.DeviceIdType.MESH
F32 = jnp.float32
BF16 = jnp.bfloat16


def dot_nt(left, right):
    return lax.dot_general(left, right, (((1,), (1,)), ((), ())), preferred_element_type=F32)


def dot_nn(left, right):
    return lax.dot_general(left, right, (((1,), (0,)), ((), ())), preferred_element_type=F32)


def halves(value):
    high = value.astype(BF16)
    low = (value - high.astype(F32)).astype(BF16)
    return high, low


def kernel(
    nf, ns, order_in, movie_in, traces_in, index_in, foot_in, out_ref,
    order_ref, movie_ref, traces_ref, index_ref, foot_ref, own, left, right, dense, sent, near,
    hi_s, lo_s, vh_s, vl_s, movie_s, w_s, c_s, inv_s, size_s, unit_s,
    load_sem, send_m, recv_m, send_d, recv_d,
):
    f = lax.axis_index("frames")
    s = lax.axis_index("slabs")
    has_l = s > 0
    has_r = s < ns - 1
    frames, voxels = movie_ref.shape
    margin = voxels // 2
    extent = 2 * voxels
    chunks = extent // LANES
    half = chunks // 2
    foot_n = foot_ref.shape[1]

    barrier = pltpu.get_barrier_semaphore()
    for d in range(1, nf):
        pl.semaphore_signal(barrier, inc=1, device_id=(lax.rem(f + d, nf), s), device_id_type=MESH)

    @pl.when(has_l)
    def _():
        for d in range(nf):
            pl.semaphore_signal(
                barrier, inc=1, device_id=(lax.rem(f + d, nf), s - 1), device_id_type=MESH)

    @pl.when(has_r)
    def _():
        for d in range(nf):
            pl.semaphore_signal(
                barrier, inc=1, device_id=(lax.rem(f + d, nf), s + 1), device_id_type=MESH)

    pairs = ((index_in, index_ref), (foot_in, foot_ref), (order_in, order_ref),
             (movie_in, movie_ref), (traces_in, traces_ref))
    loads = [pltpu.make_async_copy(a, b, load_sem.at[i]) for i, (a, b) in enumerate(pairs)]
    for i in (3, 4, 1, 0, 2):
        loads[i].start()

    loads[3].wait()
    loads[4].wait()
    quarter = margin // 2
    parts = movie_ref[...].astype(F32)
    for h, at in ((0, 0), (1, quarter + LANES)):
        own[f, :, at:at + quarter] = jnp.concatenate(
            [parts[:, 2 * h * quarter:(2 * h + 1) * quarter],
             parts[:, (2 * h + 1) * quarter:(2 * h + 2) * quarter]], axis=0).astype(BF16)

    @pl.when(jnp.logical_not(has_l))
    def _():
        left[...] = jnp.zeros_like(left)
        near[0] = jnp.full(near.shape[1:], -1, jnp.int32).astype(jnp.int16)

    @pl.when(jnp.logical_not(has_r))
    def _():
        right[...] = jnp.zeros_like(right)
        near[1] = jnp.full(near.shape[1:], -1, jnp.int32).astype(jnp.int16)

    for load in loads[:3]:
        load.wait()
    swap = order_ref[0] != 0

    def permuted(ref):
        a = ref[0:BLOCK, :]
        b = ref[BLOCK:2 * BLOCK, :]
        return jnp.concatenate([jnp.where(swap, b, a), jnp.where(swap, a, b)], axis=0)

    index = permuted(index_ref)
    value = permuted(foot_ref)
    v_hi = value.astype(BF16).astype(F32)
    for ref, rows in ((hi_s, (index >> 7).astype(F32)),
                      (lo_s, (index & (LANES - 1)).astype(F32)),
                      (vl_s, value - v_hi),
                      (vh_s, jnp.where(v_hi == 0.0, -1.0, v_hi))):
        ref[0] = rows[:BLOCK]
        ref[1] = rows[BLOCK:]

    largest = jnp.max(value, axis=1, keepdims=True) * 1.01 + 1e-30
    largest = jnp.broadcast_to(largest, (2 * BLOCK, LANES)).astype(BF16).astype(F32)
    unit_s[0] = STEPS / largest[:BLOCK]
    unit_s[1] = STEPS / largest[BLOCK:]
    lane8 = lax.broadcasted_iota(jnp.int32, (BLOCK, LANES), 1)
    lead = jnp.concatenate(
        [traces_ref[...].astype(F32), jnp.zeros((frames, LANES - 2 * BLOCK), F32)], axis=1)
    own[f, :, quarter:quarter + LANES] = jnp.concatenate(
        [lead, jnp.where(lane8 < LANES // 2, largest[:BLOCK], largest[BLOCK:])],
        axis=0).astype(BF16)

    def peer(d):
        to = lax.rem(f + d, nf)
        return pltpu.make_async_remote_copy(
            src_ref=own.at[f], dst_ref=own.at[f], send_sem=send_m.at[0, to],
            recv_sem=recv_m.at[0, f], device_id=(to, s), device_id_type=MESH)

    def to_right(d):
        to = lax.rem(f + d, nf)
        return pltpu.make_async_remote_copy(
            src_ref=own.at[f, :, pl.ds(quarter, quarter + LANES)], dst_ref=left.at[f],
            send_sem=send_m.at[1, to], recv_sem=recv_m.at[1, f],
            device_id=(to, s + 1), device_id_type=MESH)

    def to_left(d):
        to = lax.rem(f + d, nf)
        return pltpu.make_async_remote_copy(
            src_ref=own.at[f, :, pl.ds(0, quarter + LANES)], dst_ref=right.at[f],
            send_sem=send_m.at[2, to], recv_sem=recv_m.at[2, f],
            device_id=(to, s - 1), device_id_type=MESH)

    rows16 = 2 * BLOCK
    iota = lax.broadcasted_iota(jnp.int32, (rows16, foot_n), 0).astype(F32)
    span = half * BLOCK

    def dense_right(b):
        return pltpu.make_async_remote_copy(
            src_ref=sent.at[2 * b + 1], dst_ref=near.at[0, pl.ds(b * span, span), :],
            send_sem=send_d.at[0, b], recv_sem=recv_d.at[0, b],
            device_id=(f, s + 1), device_id_type=MESH)

    def dense_left(b):
        return pltpu.make_async_remote_copy(
            src_ref=sent.at[2 * b], dst_ref=near.at[1, pl.ds(b * span, span), :],
            send_sem=send_d.at[1, b], recv_sem=recv_d.at[1, b],
            device_id=(f, s - 1), device_id_type=MESH)

    def scatter_block(b, carry):
        def scatter_row(k):

            def spread(ref):
                return jnp.broadcast_to(ref[b, k:k + 1, :], (rows16, foot_n)).astype(BF16)

            hi = spread(hi_s)
            lo = spread(lo_s)
            vh = spread(vh_s)
            vl = spread(vl_s)
            zero = jnp.zeros((rows16, foot_n), BF16)
            one = jnp.ones((rows16, foot_n), BF16)
            iota16 = iota.astype(BF16)
            low = [jnp.where(lo == iota16 + BF16(16 * t), one, zero) for t in range(LANES // 16)]
            high = [hi == iota16 + BF16(16 * t) for t in range(chunks // 16)]
            lhs = [jnp.where(m, vh, zero) for m in high] + [jnp.where(m, vl, zero) for m in high]
            got = dot_nt(jnp.concatenate(lhs, axis=0), jnp.concatenate(low, axis=0))
            g_hi = got[:chunks]
            enc = jnp.where(g_hi == 0.0, -1.0, jnp.maximum(g_hi, 0.0) + got[chunks:])
            dense[2 * b, pl.ds(k, half, stride=BLOCK), :] = enc[:half]
            dense[2 * b + 1, pl.ds(k, half, stride=BLOCK), :] = enc[half:]

        for k in range(BLOCK):
            scatter_row(k)

            if k == 0:
                @pl.when(b == 0)
                def _():
                    count = nf - 1 + nf * has_l.astype(jnp.int32) + nf * has_r.astype(jnp.int32)
                    pl.semaphore_wait(barrier, count)

                    for d in range(1, nf):
                        peer(d).start()

                    @pl.when(has_r)
                    def _():
                        for d in range(nf):
                            to_right(d).start()

                    @pl.when(has_l)
                    def _():
                        for d in range(nf):
                            to_left(d).start()

        for side in range(2):
            values = dense[2 * b + side].reshape(half, BLOCK, LANES)
            steps = jnp.where(values < 0.0, -1.0, values * unit_s[b] + 0.5)
            sent[2 * b + side] = steps.reshape(span, LANES).astype(jnp.int32).astype(jnp.int16)

        @pl.when(has_r)
        def _():
            dense_right(b).start()

        @pl.when(has_l)
        def _():
            dense_left(b).start()

        return carry

    lax.fori_loop(0, 2, scatter_block, 0)

    for d in range(1, nf):
        pltpu.make_async_remote_copy(
            src_ref=own.at[f], dst_ref=own.at[lax.rem(f + d, nf)], send_sem=send_m.at[0, 0],
            recv_sem=recv_m.at[0, lax.rem(f + d, nf)], device_id=(f, s),
            device_id_type=MESH).wait_recv()

    @pl.when(has_l)
    def _():
        for d in range(nf):
            pltpu.make_async_remote_copy(
                src_ref=left.at[d], dst_ref=left.at[d], send_sem=send_m.at[1, 0],
                recv_sem=recv_m.at[1, d], device_id=(f, s), device_id_type=MESH).wait_recv()

    @pl.when(has_r)
    def _():
        for d in range(nf):
            pltpu.make_async_remote_copy(
                src_ref=right.at[d], dst_ref=right.at[d], send_sem=send_m.at[2, 0],
                recv_sem=recv_m.at[2, d], device_id=(f, s), device_id_type=MESH).wait_recv()

    def all_frames(pick):
        return jnp.concatenate([pick(g) for g in range(nf)], axis=0)

    def unpacked(ref, at):
        def one(g):
            both = ref[g, :, at:at + quarter].astype(F32)
            return jnp.concatenate([both[:frames], both[frames:]], axis=1)
        return all_frames(one)

    def trace_rows(ref, at):
        return lambda g: ref[g, :, at:at + LANES].astype(F32)[:frames]

    movie_l = jnp.concatenate([unpacked(left, LANES), unpacked(own, 0)], axis=1).astype(BF16)
    movie_r = jnp.concatenate(
        [unpacked(own, quarter + LANES), unpacked(right, 0)], axis=1).astype(BF16)
    total = nf * frames
    padding = jnp.zeros((LANES - total, LANES), F32)
    eye = (lax.broadcasted_iota(jnp.int32, (rows16, LANES), 0)
           == lax.broadcasted_iota(jnp.int32, (rows16, LANES), 1)).astype(F32).astype(BF16)

    def by_source(pick):
        block = jnp.concatenate([all_frames(pick), padding], axis=0).astype(BF16)
        rows = dot_nt(eye, block)
        return jnp.concatenate([jnp.where(swap, rows[BLOCK:], rows[:BLOCK]),
                                jnp.where(swap, rows[:BLOCK], rows[BLOCK:])], axis=0)

    t_own = by_source(trace_rows(own, quarter))
    t_left = by_source(trace_rows(left, 0))
    t_right = by_source(trace_rows(right, quarter))

    depth = -(-(total + 3 * 32) // LANES) * LANES
    identity = (lax.broadcasted_iota(jnp.int32, (total, LANES), 0)
                == lax.broadcasted_iota(jnp.int32, (total, LANES), 1)).astype(F32)

    def weights(t_near):
        t32 = jnp.concatenate([t_own, t_near], axis=0)
        stacked = jnp.concatenate(
            [identity, t32, t32, t32,
             jnp.zeros((depth - total - 96, LANES), F32)], axis=0).astype(BF16)
        full = dot_nt(t32.astype(BF16), stacked)
        lane = lax.broadcasted_iota(jnp.int32, full.shape, 1)
        g_hi = full.astype(BF16).astype(F32)
        picked = jnp.where((lane >= total + 32) & (lane < total + 64), full - g_hi, g_hi)
        first = jnp.where(lane < total, full, -picked).astype(BF16)
        t_f = jnp.concatenate([t32[0:8], t32[16:24]], axis=0)
        t_s = jnp.concatenate([t32[8:16], t32[24:32]], axis=0)
        stacked2 = jnp.concatenate(
            [t_f, t_f, t_f, jnp.zeros((LANES - 48, LANES), F32)], axis=0).astype(BF16)
        cross = dot_nt(t_s.astype(BF16), stacked2)
        lane2 = lax.broadcasted_iota(jnp.int32, cross.shape, 1)
        row2 = lax.broadcasted_iota(jnp.int32, cross.shape, 0)
        c_hi = cross.astype(BF16).astype(F32)
        picked2 = jnp.where((lane2 >= 16) & (lane2 < 32), cross - c_hi, c_hi)
        same = (row2 // 8) == ((lane2 // 8) % 2)
        second = jnp.where(same, picked2, 0.0).astype(BF16)
        inverse = 1.0 / (jnp.sum(t32 * t32, axis=1, keepdims=True) + 1.0)
        return first, second, inverse

    for side, (movie, t_near) in enumerate(((movie_l, t_left), (movie_r, t_right))):
        w, c, inverse = weights(t_near)
        movie_s[side] = movie
        w_s[side] = w
        c_s[side] = c
        inv_s[side] = jnp.broadcast_to(inverse, (4 * BLOCK, LANES))
        block = ((left, 0), (right, quarter))[side]
        scales = block[0][0, :, block[1]:block[1] + LANES].astype(F32)[frames:] * (1.0 / STEPS)
        size_s[side] = jnp.concatenate(
            [jnp.broadcast_to(scales[:, 0:1], (BLOCK, LANES)),
             jnp.broadcast_to(scales[:, LANES // 2:LANES // 2 + 1], (BLOCK, LANES))], axis=0)

    tiles = foot_n // LANES
    out_ref[...] = jnp.zeros_like(out_ref)

    early = 1 - lax.rem(s, 2)

    def one_side(i, carry):
        side = jnp.where(i == 0, early, 1 - early)

        @pl.when(jnp.where(side == 0, s, ns - 1 - s) > 0)
        def _():
            for b in range(2):
                pltpu.make_async_remote_copy(
                    src_ref=near.at[side, pl.ds(b * span, span), :],
                    dst_ref=near.at[side, pl.ds(b * span, span), :],
                    send_sem=send_d.at[0, 0], recv_sem=recv_d.at[side, b],
                    device_id=(f, s), device_id_type=MESH).wait_recv()

        def wide(ref, at, start):
            return jnp.concatenate(
                [ref[at, (start + c) * BLOCK:(start + c + 1) * BLOCK, :] for c in range(half)],
                axis=1)

        movie = movie_s[side]
        w = w_s[side][:, :total + 96]
        cross = c_s[side][:, :48]
        inverse = inv_s[side][:, 0:1]
        steps = near[side].astype(jnp.int32).astype(F32).reshape(2, half, BLOCK, LANES)
        size = size_s[side]
        enc = [wide(dense, side, 0), wide(dense, 2 + side, 0)]
        for b in range(2):
            enc.append(jnp.concatenate(
                [steps[b, c] * size[b * BLOCK:(b + 1) * BLOCK] for c in range(half)], axis=1))
        mask = [(e >= 0.0).astype(F32) for e in enc]
        state = [jnp.maximum(e, 0.0) for e in enc]

        def residual(w_rows, state):
            high, low = halves(jnp.concatenate(state, axis=0))
            return dot_nn(w_rows, jnp.concatenate([movie, high, high, low], axis=0))

        def change(c_rows, old, new):
            high, low = halves(jnp.concatenate([n - o for n, o in zip(new, old)], axis=0))
            return dot_nn(c_rows, jnp.concatenate([high, high, low], axis=0))

        def step(i, rest):
            return mask[i] * jnp.maximum(state[i] + rest * inverse[8 * i:8 * i + 8], 0.0)

        rest = residual(w, state)
        new_f = [step(0, rest[0:8]), step(2, rest[16:24])]
        moved = change(cross, [state[0], state[2]], new_f)
        new_s = [step(1, rest[8:16] - moved[0:8]), step(3, rest[24:32] - moved[8:16])]
        state = [new_f[0], new_s[0], new_f[1], new_s[1]]
        rest = residual(w[0:16], state)
        new_f = step(0, rest[0:8])
        moved = change(cross, [state[0], state[2]], [new_f, state[2]])
        new_s = step(1, rest[8:16] - moved[0:8])
        done = (jnp.where(swap, new_s, new_f), jnp.where(swap, new_f, new_s))
        for b in range(2):
            for j in range(tiles):
                at = (slice(b * BLOCK, (b + 1) * BLOCK), slice(j * LANES, (j + 1) * LANES))
                place = index_ref[at]
                chunk = (place >> 7) - half * side
                lane = place & (LANES - 1)
                taken = out_ref[at]
                for c in range(half):
                    tile = done[b][:, c * LANES:(c + 1) * LANES]
                    got = jnp.take_along_axis(tile, lane, axis=1, mode="promise_in_bounds")
                    taken = jnp.where(chunk == c, got, taken)
                out_ref[at] = taken
        return carry

    lax.fori_loop(0, 2, one_side, 0)

    for d in range(1, nf):
        peer(d).wait_send()

    @pl.when(has_r)
    def _():
        for d in range(nf):
            to_right(d).wait_send()
        for b in range(2):
            dense_right(b).wait_send()

    @pl.when(has_l)
    def _():
        for d in range(nf):
            to_left(d).wait_send()
        for b in range(2):
            dense_left(b).wait_send()


def local(movie, traces, voxel_index, footprint, block_order):
    nf = lax.axis_size("frames")
    ns = lax.axis_size("slabs")
    frames, voxels = movie.shape
    sources, foot_n = footprint.shape
    margin = voxels // 2
    chunks = 2 * voxels // LANES
    depth = -(-(nf * frames + 3 * 32) // LANES) * LANES
    vmem = pl.BlockSpec(memory_space=pltpu.VMEM)
    return pl.pallas_call(
        functools.partial(kernel, nf, ns),
        out_shape=pltpu.VMEM((sources, foot_n), F32),
        in_specs=[pl.BlockSpec(memory_space=pltpu.HBM)] * 5,
        out_specs=vmem,
        scratch_shapes=[
            pltpu.SMEM(block_order.shape, block_order.dtype),
            pltpu.VMEM(movie.shape, movie.dtype),
            pltpu.VMEM(traces.shape, traces.dtype),
            pltpu.VMEM(voxel_index.shape, voxel_index.dtype),
            pltpu.VMEM(footprint.shape, footprint.dtype),
            pltpu.VMEM((nf, 2 * frames, margin + LANES), BF16),
            pltpu.VMEM((nf, 2 * frames, margin // 2 + LANES), BF16),
            pltpu.VMEM((nf, 2 * frames, margin // 2 + LANES), BF16),
            pltpu.VMEM((4, BLOCK * chunks // 2, LANES), F32),
            pltpu.VMEM((4, BLOCK * chunks // 2, LANES), jnp.int16),
            pltpu.VMEM((2, BLOCK * chunks, LANES), jnp.int16),
            pltpu.VMEM((2, BLOCK, foot_n), F32),
            pltpu.VMEM((2, BLOCK, foot_n), F32),
            pltpu.VMEM((2, BLOCK, foot_n), F32),
            pltpu.VMEM((2, BLOCK, foot_n), F32),
            pltpu.VMEM((2, nf * frames, voxels), BF16),
            pltpu.VMEM((2, 4 * BLOCK, depth), BF16),
            pltpu.VMEM((2, 2 * BLOCK, LANES), BF16),
            pltpu.VMEM((2, 4 * BLOCK, LANES), F32),
            pltpu.VMEM((2, 2 * BLOCK, LANES), F32),
            pltpu.VMEM((2, BLOCK, LANES), F32),
            pltpu.SemaphoreType.DMA((5,)),
            pltpu.SemaphoreType.DMA((3, nf)),
            pltpu.SemaphoreType.DMA((3, nf)),
            pltpu.SemaphoreType.DMA((2, 2)),
            pltpu.SemaphoreType.DMA((2, 2)),
        ],
        compiler_params=pltpu.CompilerParams(
            collective_id=0, has_side_effects=True, vmem_limit_bytes=32 * 1024 * 1024),
        cost_estimate=pl.CostEstimate(
            flops=2 * sources * 64 * LANES * foot_n, bytes_accessed=500000, transcendentals=0),
    )(*(pltpu.with_memory_space_constraint(x, pltpu.HBM)
        for x in (block_order, movie, traces, voxel_index, footprint)))


def solution(mesh):
    in_specs = (P("frames", "slabs"), P("frames", "slabs"), P("slabs", None), P("slabs", None), P())
    out_specs = P("slabs", None)
    return jax.shard_map(local, mesh=mesh, in_specs=in_specs, out_specs=out_specs, check_vma=False)
```

```python
import functools

import jax
import jax.numpy as jnp
from jax import lax
from jax.experimental import pallas as pl
from jax.experimental.pallas import tpu as pltpu
from jax.sharding import PartitionSpec as P

BLOCK = 8
LANES = 128
STEPS = 32767.0
MESH = pl.DeviceIdType.MESH
F32 = jnp.float32
BF16 = jnp.bfloat16


def dot_nt(left, right):
    return lax.dot_general(left, right, (((1,), (1,)), ((), ())), preferred_element_type=F32)


def dot_nn(left, right):
    return lax.dot_general(left, right, (((1,), (0,)), ((), ())), preferred_element_type=F32)


def halves(value):
    high = value.astype(BF16)
    low = (value - high.astype(F32)).astype(BF16)
    return high, low


def kernel(
    nf, ns, order_in, movie_in, traces_in, index_in, foot_in, out_ref,
    order_ref, movie_ref, traces_ref, index_ref, foot_ref, own, left, right, dense, sent, near,
    hi_s, lo_s, vh_s, vl_s, movie_s, w_s, c_s, inv_s, size_s, unit_s,
    load_sem, send_m, recv_m, send_d, recv_d,
):
    f = lax.axis_index("frames")
    s = lax.axis_index("slabs")
    has_l = s > 0
    has_r = s < ns - 1
    frames, voxels = movie_ref.shape
    margin = voxels // 2
    extent = 2 * voxels
    chunks = extent // LANES
    half = chunks // 2
    foot_n = foot_ref.shape[1]

    barrier = pltpu.get_barrier_semaphore()
    for d in range(1, nf):
        pl.semaphore_signal(barrier, inc=1, device_id=(lax.rem(f + d, nf), s), device_id_type=MESH)

    @pl.when(has_l)
    def _():
        for d in range(nf):
            pl.semaphore_signal(
                barrier, inc=1, device_id=(lax.rem(f + d, nf), s - 1), device_id_type=MESH)

    @pl.when(has_r)
    def _():
        for d in range(nf):
            pl.semaphore_signal(
                barrier, inc=1, device_id=(lax.rem(f + d, nf), s + 1), device_id_type=MESH)

    pairs = ((index_in, index_ref), (foot_in, foot_ref), (order_in, order_ref),
             (movie_in, movie_ref), (traces_in, traces_ref))
    loads = [pltpu.make_async_copy(a, b, load_sem.at[i]) for i, (a, b) in enumerate(pairs)]
    for load in loads:
        load.start()

    loads[3].wait()
    loads[4].wait()
    quarter = margin // 2
    parts = movie_ref[...].astype(F32)
    for h, at in ((0, 0), (1, quarter + LANES)):
        own[f, :, at:at + quarter] = jnp.concatenate(
            [parts[:, 2 * h * quarter:(2 * h + 1) * quarter],
             parts[:, (2 * h + 1) * quarter:(2 * h + 2) * quarter]], axis=0).astype(BF16)

    @pl.when(jnp.logical_not(has_l))
    def _():
        left[...] = jnp.zeros_like(left)
        near[0] = jnp.full(near.shape[1:], -1, jnp.int32).astype(jnp.int16)

    @pl.when(jnp.logical_not(has_r))
    def _():
        right[...] = jnp.zeros_like(right)
        near[1] = jnp.full(near.shape[1:], -1, jnp.int32).astype(jnp.int16)

    for load in loads[:3]:
        load.wait()
    swap = order_ref[0] != 0

    def permuted(ref):
        a = ref[0:BLOCK, :]
        b = ref[BLOCK:2 * BLOCK, :]
        return jnp.concatenate([jnp.where(swap, b, a), jnp.where(swap, a, b)], axis=0)

    index = permuted(index_ref)
    value = permuted(foot_ref)
    v_hi = value.astype(BF16).astype(F32)
    for ref, rows in ((hi_s, (index >> 7).astype(F32)),
                      (lo_s, (index & (LANES - 1)).astype(F32)),
                      (vl_s, value - v_hi),
                      (vh_s, jnp.where(v_hi == 0.0, -1.0, v_hi))):
        ref[0] = rows[:BLOCK]
        ref[1] = rows[BLOCK:]

    largest = jnp.max(value, axis=1, keepdims=True) * 1.01 + 1e-30
    largest = jnp.broadcast_to(largest, (2 * BLOCK, LANES)).astype(BF16).astype(F32)
    unit_s[0] = STEPS / largest[:BLOCK]
    unit_s[1] = STEPS / largest[BLOCK:]
    lane8 = lax.broadcasted_iota(jnp.int32, (BLOCK, LANES), 1)
    lead = jnp.concatenate(
        [traces_ref[...].astype(F32), jnp.zeros((frames, LANES - 2 * BLOCK), F32)], axis=1)
    own[f, :, quarter:quarter + LANES] = jnp.concatenate(
        [lead, jnp.where(lane8 < LANES // 2, largest[:BLOCK], largest[BLOCK:])],
        axis=0).astype(BF16)

    def peer(d):
        to = lax.rem(f + d, nf)
        return pltpu.make_async_remote_copy(
            src_ref=own.at[f], dst_ref=own.at[f], send_sem=send_m.at[0, to],
            recv_sem=recv_m.at[0, f], device_id=(to, s), device_id_type=MESH)

    def to_right(d):
        to = lax.rem(f + d, nf)
        return pltpu.make_async_remote_copy(
            src_ref=own.at[f, :, pl.ds(quarter, quarter + LANES)], dst_ref=left.at[f],
            send_sem=send_m.at[1, to], recv_sem=recv_m.at[1, f],
            device_id=(to, s + 1), device_id_type=MESH)

    def to_left(d):
        to = lax.rem(f + d, nf)
        return pltpu.make_async_remote_copy(
            src_ref=own.at[f, :, pl.ds(0, quarter + LANES)], dst_ref=right.at[f],
            send_sem=send_m.at[2, to], recv_sem=recv_m.at[2, f],
            device_id=(to, s - 1), device_id_type=MESH)

    rows16 = 2 * BLOCK
    iota = lax.broadcasted_iota(jnp.int32, (rows16, foot_n), 0).astype(F32)
    span = half * BLOCK

    def dense_right(b):
        return pltpu.make_async_remote_copy(
            src_ref=sent.at[2 * b + 1], dst_ref=near.at[0, pl.ds(b * span, span), :],
            send_sem=send_d.at[0, b], recv_sem=recv_d.at[0, b],
            device_id=(f, s + 1), device_id_type=MESH)

    def dense_left(b):
        return pltpu.make_async_remote_copy(
            src_ref=sent.at[2 * b], dst_ref=near.at[1, pl.ds(b * span, span), :],
            send_sem=send_d.at[1, b], recv_sem=recv_d.at[1, b],
            device_id=(f, s - 1), device_id_type=MESH)

    def scatter_block(b, carry):
        def scatter_row(k):

            def spread(ref):
                return jnp.broadcast_to(ref[b, k:k + 1, :], (rows16, foot_n)).astype(BF16)

            hi = spread(hi_s)
            lo = spread(lo_s)
            vh = spread(vh_s)
            vl = spread(vl_s)
            zero = jnp.zeros((rows16, foot_n), BF16)
            one = jnp.ones((rows16, foot_n), BF16)
            iota16 = iota.astype(BF16)
            low = [jnp.where(lo == iota16 + BF16(16 * t), one, zero) for t in range(LANES // 16)]
            high = [hi == iota16 + BF16(16 * t) for t in range(chunks // 16)]
            lhs = [jnp.where(m, vh, zero) for m in high] + [jnp.where(m, vl, zero) for m in high]
            got = dot_nt(jnp.concatenate(lhs, axis=0), jnp.concatenate(low, axis=0))
            g_hi = got[:chunks]
            enc = jnp.where(g_hi == 0.0, -1.0, jnp.maximum(g_hi, 0.0) + got[chunks:])
            dense[2 * b, pl.ds(k, half, stride=BLOCK), :] = enc[:half]
            dense[2 * b + 1, pl.ds(k, half, stride=BLOCK), :] = enc[half:]

        for k in range(BLOCK):
            scatter_row(k)

            if k == BLOCK - 1:
                @pl.when(b == 0)
                def _():
                    count = nf - 1 + nf * has_l.astype(jnp.int32) + nf * has_r.astype(jnp.int32)
                    pl.semaphore_wait(barrier, count)

                    for d in range(1, nf):
                        peer(d).start()

                    @pl.when(has_r)
                    def _():
                        for d in range(nf):
                            to_right(d).start()

                    @pl.when(has_l)
                    def _():
                        for d in range(nf):
                            to_left(d).start()

        for side in range(2):
            values = dense[2 * b + side].reshape(half, BLOCK, LANES)
            steps = jnp.where(values < 0.0, -1.0, values * unit_s[b] + 0.5)
            sent[2 * b + side] = steps.reshape(span, LANES).astype(jnp.int32).astype(jnp.int16)

        @pl.when(has_r)
        def _():
            dense_right(b).start()

        @pl.when(has_l)
        def _():
            dense_left(b).start()

        return carry

    lax.fori_loop(0, 2, scatter_block, 0)

    for d in range(1, nf):
        pltpu.make_async_remote_copy(
            src_ref=own.at[f], dst_ref=own.at[lax.rem(f + d, nf)], send_sem=send_m.at[0, 0],
            recv_sem=recv_m.at[0, lax.rem(f + d, nf)], device_id=(f, s),
            device_id_type=MESH).wait_recv()

    @pl.when(has_l)
    def _():
        for d in range(nf):
            pltpu.make_async_remote_copy(
                src_ref=left.at[d], dst_ref=left.at[d], send_sem=send_m.at[1, 0],
                recv_sem=recv_m.at[1, d], device_id=(f, s), device_id_type=MESH).wait_recv()

    @pl.when(has_r)
    def _():
        for d in range(nf):
            pltpu.make_async_remote_copy(
                src_ref=right.at[d], dst_ref=right.at[d], send_sem=send_m.at[2, 0],
                recv_sem=recv_m.at[2, d], device_id=(f, s), device_id_type=MESH).wait_recv()

    def all_frames(pick):
        return jnp.concatenate([pick(g) for g in range(nf)], axis=0)

    def unpacked(ref, at):
        def one(g):
            both = ref[g, :, at:at + quarter].astype(F32)
            return jnp.concatenate([both[:frames], both[frames:]], axis=1)
        return all_frames(one)

    def trace_rows(ref, at):
        return lambda g: ref[g, :, at:at + LANES].astype(F32)[:frames]

    movie_l = jnp.concatenate([unpacked(left, LANES), unpacked(own, 0)], axis=1).astype(BF16)
    movie_r = jnp.concatenate(
        [unpacked(own, quarter + LANES), unpacked(right, 0)], axis=1).astype(BF16)
    total = nf * frames
    padding = jnp.zeros((LANES - total, LANES), F32)
    eye = (lax.broadcasted_iota(jnp.int32, (rows16, LANES), 0)
           == lax.broadcasted_iota(jnp.int32, (rows16, LANES), 1)).astype(F32).astype(BF16)

    def by_source(pick):
        block = jnp.concatenate([all_frames(pick), padding], axis=0).astype(BF16)
        rows = dot_nt(eye, block)
        return jnp.concatenate([jnp.where(swap, rows[BLOCK:], rows[:BLOCK]),
                                jnp.where(swap, rows[:BLOCK], rows[BLOCK:])], axis=0)

    t_own = by_source(trace_rows(own, quarter))
    t_left = by_source(trace_rows(left, 0))
    t_right = by_source(trace_rows(right, quarter))

    depth = -(-(total + 3 * 32) // LANES) * LANES
    identity = (lax.broadcasted_iota(jnp.int32, (total, LANES), 0)
                == lax.broadcasted_iota(jnp.int32, (total, LANES), 1)).astype(F32)

    def weights(t_near):
        t32 = jnp.concatenate([t_own, t_near], axis=0)
        stacked = jnp.concatenate(
            [identity, t32, t32, t32,
             jnp.zeros((depth - total - 96, LANES), F32)], axis=0).astype(BF16)
        full = dot_nt(t32.astype(BF16), stacked)
        lane = lax.broadcasted_iota(jnp.int32, full.shape, 1)
        g_hi = full.astype(BF16).astype(F32)
        picked = jnp.where((lane >= total + 32) & (lane < total + 64), full - g_hi, g_hi)
        first = jnp.where(lane < total, full, -picked).astype(BF16)
        t_f = jnp.concatenate([t32[0:8], t32[16:24]], axis=0)
        t_s = jnp.concatenate([t32[8:16], t32[24:32]], axis=0)
        stacked2 = jnp.concatenate(
            [t_f, t_f, t_f, jnp.zeros((LANES - 48, LANES), F32)], axis=0).astype(BF16)
        cross = dot_nt(t_s.astype(BF16), stacked2)
        lane2 = lax.broadcasted_iota(jnp.int32, cross.shape, 1)
        row2 = lax.broadcasted_iota(jnp.int32, cross.shape, 0)
        c_hi = cross.astype(BF16).astype(F32)
        picked2 = jnp.where((lane2 >= 16) & (lane2 < 32), cross - c_hi, c_hi)
        same = (row2 // 8) == ((lane2 // 8) % 2)
        second = jnp.where(same, picked2, 0.0).astype(BF16)
        inverse = 1.0 / (jnp.sum(t32 * t32, axis=1, keepdims=True) + 1.0)
        return first, second, inverse

    for side, (movie, t_near) in enumerate(((movie_l, t_left), (movie_r, t_right))):
        w, c, inverse = weights(t_near)
        movie_s[side] = movie
        w_s[side] = w
        c_s[side] = c
        inv_s[side] = jnp.broadcast_to(inverse, (4 * BLOCK, LANES))
        block = ((left, 0), (right, quarter))[side]
        scales = block[0][0, :, block[1]:block[1] + LANES].astype(F32)[frames:] * (1.0 / STEPS)
        size_s[side] = jnp.concatenate(
            [jnp.broadcast_to(scales[:, 0:1], (BLOCK, LANES)),
             jnp.broadcast_to(scales[:, LANES // 2:LANES // 2 + 1], (BLOCK, LANES))], axis=0)

    tiles = foot_n // LANES
    out_ref[...] = jnp.zeros_like(out_ref)

    early = 1 - lax.rem(s, 2)

    def update_side(side):
        @pl.when(jnp.where(side == 0, s, ns - 1 - s) > 0)
        def _():
            for b in range(2):
                pltpu.make_async_remote_copy(
                    src_ref=near.at[side, pl.ds(b * span, span), :],
                    dst_ref=near.at[side, pl.ds(b * span, span), :],
                    send_sem=send_d.at[0, 0], recv_sem=recv_d.at[side, b],
                    device_id=(f, s), device_id_type=MESH).wait_recv()

        def wide(ref, at, start):
            return jnp.concatenate(
                [ref[at, (start + c) * BLOCK:(start + c + 1) * BLOCK, :] for c in range(half)],
                axis=1)

        movie = movie_s[side]
        w = w_s[side][:, :total + 96]
        cross = c_s[side][:, :48]
        inverse = inv_s[side][:, 0:1]
        steps = near[side].astype(jnp.int32).astype(F32).reshape(2, half, BLOCK, LANES)
        size = size_s[side]
        enc = [wide(dense, side, 0), wide(dense, 2 + side, 0)]
        for b in range(2):
            enc.append(jnp.concatenate(
                [steps[b, c] * size[b * BLOCK:(b + 1) * BLOCK] for c in range(half)], axis=1))
        mask = [(e >= 0.0).astype(F32) for e in enc]
        state = [jnp.maximum(e, 0.0) for e in enc]

        def residual(w_rows, state):
            high, low = halves(jnp.concatenate(state, axis=0))
            return dot_nn(w_rows, jnp.concatenate([movie, high, high, low], axis=0))

        def change(c_rows, old, new):
            high, low = halves(jnp.concatenate([n - o for n, o in zip(new, old)], axis=0))
            return dot_nn(c_rows, jnp.concatenate([high, high, low], axis=0))

        def step(i, rest):
            return mask[i] * jnp.maximum(state[i] + rest * inverse[8 * i:8 * i + 8], 0.0)

        rest = residual(w, state)
        new_f = [step(0, rest[0:8]), step(2, rest[16:24])]
        moved = change(cross, [state[0], state[2]], new_f)
        new_s = [step(1, rest[8:16] - moved[0:8]), step(3, rest[24:32] - moved[8:16])]
        state = [new_f[0], new_s[0], new_f[1], new_s[1]]
        rest = residual(w[0:16], state)
        new_f = step(0, rest[0:8])
        moved = change(cross, [state[0], state[2]], [new_f, state[2]])
        new_s = step(1, rest[8:16] - moved[0:8])
        done = (jnp.where(swap, new_s, new_f), jnp.where(swap, new_f, new_s))
        return done

    done_early = update_side(early)
    done_late = update_side(1 - early)
    for side, done in ((early, done_early), (1 - early, done_late)):
        for b in range(2):
            for j in range(tiles):
                at = (slice(b * BLOCK, (b + 1) * BLOCK), slice(j * LANES, (j + 1) * LANES))
                place = index_ref[at]
                chunk = (place >> 7) - half * side
                lane = place & (LANES - 1)
                taken = out_ref[at]
                for c in range(half):
                    tile = done[b][:, c * LANES:(c + 1) * LANES]
                    got = jnp.take_along_axis(tile, lane, axis=1, mode="promise_in_bounds")
                    taken = jnp.where(chunk == c, got, taken)
                out_ref[at] = taken

    for d in range(1, nf):
        peer(d).wait_send()

    @pl.when(has_r)
    def _():
        for d in range(nf):
            to_right(d).wait_send()
        for b in range(2):
            dense_right(b).wait_send()

    @pl.when(has_l)
    def _():
        for d in range(nf):
            to_left(d).wait_send()
        for b in range(2):
            dense_left(b).wait_send()


def local(movie, traces, voxel_index, footprint, block_order):
    nf = lax.axis_size("frames")
    ns = lax.axis_size("slabs")
    frames, voxels = movie.shape
    sources, foot_n = footprint.shape
    margin = voxels // 2
    chunks = 2 * voxels // LANES
    depth = -(-(nf * frames + 3 * 32) // LANES) * LANES
    vmem = pl.BlockSpec(memory_space=pltpu.VMEM)
    return pl.pallas_call(
        functools.partial(kernel, nf, ns),
        out_shape=pltpu.VMEM((sources, foot_n), F32),
        in_specs=[pl.BlockSpec(memory_space=pltpu.HBM)] * 5,
        out_specs=vmem,
        scratch_shapes=[
            pltpu.SMEM(block_order.shape, block_order.dtype),
            pltpu.VMEM(movie.shape, movie.dtype),
            pltpu.VMEM(traces.shape, traces.dtype),
            pltpu.VMEM(voxel_index.shape, voxel_index.dtype),
            pltpu.VMEM(footprint.shape, footprint.dtype),
            pltpu.VMEM((nf, 2 * frames, margin + LANES), BF16),
            pltpu.VMEM((nf, 2 * frames, margin // 2 + LANES), BF16),
            pltpu.VMEM((nf, 2 * frames, margin // 2 + LANES), BF16),
            pltpu.VMEM((4, BLOCK * chunks // 2, LANES), F32),
            pltpu.VMEM((4, BLOCK * chunks // 2, LANES), jnp.int16),
            pltpu.VMEM((2, BLOCK * chunks, LANES), jnp.int16),
            pltpu.VMEM((2, BLOCK, foot_n), F32),
            pltpu.VMEM((2, BLOCK, foot_n), F32),
            pltpu.VMEM((2, BLOCK, foot_n), F32),
            pltpu.VMEM((2, BLOCK, foot_n), F32),
            pltpu.VMEM((2, nf * frames, voxels), BF16),
            pltpu.VMEM((2, 4 * BLOCK, depth), BF16),
            pltpu.VMEM((2, 2 * BLOCK, LANES), BF16),
            pltpu.VMEM((2, 4 * BLOCK, LANES), F32),
            pltpu.VMEM((2, 2 * BLOCK, LANES), F32),
            pltpu.VMEM((2, BLOCK, LANES), F32),
            pltpu.SemaphoreType.DMA((5,)),
            pltpu.SemaphoreType.DMA((3, nf)),
            pltpu.SemaphoreType.DMA((3, nf)),
            pltpu.SemaphoreType.DMA((2, 2)),
            pltpu.SemaphoreType.DMA((2, 2)),
        ],
        compiler_params=pltpu.CompilerParams(
            collective_id=0, has_side_effects=True, vmem_limit_bytes=32 * 1024 * 1024),
        cost_estimate=pl.CostEstimate(
            flops=2 * sources * 64 * LANES * foot_n, bytes_accessed=500000, transcendentals=0),
    )(*(pltpu.with_memory_space_constraint(x, pltpu.HBM)
        for x in (block_order, movie, traces, voxel_index, footprint)))


def solution(mesh):
    in_specs = (P("frames", "slabs"), P("frames", "slabs"), P("slabs", None), P("slabs", None), P())
    out_specs = P("slabs", None)
    return jax.shard_map(local, mesh=mesh, in_specs=in_specs, out_specs=out_specs, check_vma=False)
```

```python
import functools

import jax
import jax.numpy as jnp
from jax import lax
from jax.experimental import pallas as pl
from jax.experimental.pallas import tpu as pltpu
from jax.sharding import PartitionSpec as P

BLOCK = 8
LANES = 128
STEPS = 32767.0
MESH = pl.DeviceIdType.MESH
F32 = jnp.float32
BF16 = jnp.bfloat16


def dot_nt(left, right):
    return lax.dot_general(left, right, (((1,), (1,)), ((), ())), preferred_element_type=F32)


def dot_nn(left, right):
    return lax.dot_general(left, right, (((1,), (0,)), ((), ())), preferred_element_type=F32)


def halves(value):
    high = value.astype(BF16)
    low = (value - high.astype(F32)).astype(BF16)
    return high, low


def kernel(
    nf, ns, order_in, movie_in, traces_in, index_in, foot_in, out_ref,
    order_ref, movie_ref, traces_ref, index_ref, foot_ref, own, margins, dense, sent, near,
    hi_s, lo_s, vh_s, vl_s, unit_s,
    load_sem, send_m, recv_m, send_d, recv_d,
):
    f = lax.axis_index("frames")
    s = lax.axis_index("slabs")
    has_l = s > 0
    has_r = s < ns - 1
    frames, voxels = movie_ref.shape
    margin = voxels // 2
    extent = 2 * voxels
    chunks = extent // LANES
    half = chunks // 2
    foot_n = foot_ref.shape[1]

    barrier = pltpu.get_barrier_semaphore()
    for d in range(1, nf):
        pl.semaphore_signal(barrier, inc=1, device_id=(lax.rem(f + d, nf), s), device_id_type=MESH)

    @pl.when(has_l)
    def _():
        for d in range(nf):
            pl.semaphore_signal(
                barrier, inc=1, device_id=(lax.rem(f + d, nf), s - 1), device_id_type=MESH)

    @pl.when(has_r)
    def _():
        for d in range(nf):
            pl.semaphore_signal(
                barrier, inc=1, device_id=(lax.rem(f + d, nf), s + 1), device_id_type=MESH)

    pairs = ((index_in, index_ref), (foot_in, foot_ref), (order_in, order_ref),
             (movie_in, movie_ref), (traces_in, traces_ref))
    loads = [pltpu.make_async_copy(a, b, load_sem.at[i]) for i, (a, b) in enumerate(pairs)]
    for load in loads:
        load.start()

    loads[3].wait()
    loads[4].wait()
    quarter = margin // 2
    parts = movie_ref[...].astype(F32)
    for h, at in ((0, 0), (1, quarter + LANES)):
        own[f, :, at:at + quarter] = jnp.concatenate(
            [parts[:, 2 * h * quarter:(2 * h + 1) * quarter],
             parts[:, (2 * h + 1) * quarter:(2 * h + 2) * quarter]], axis=0).astype(BF16)

    @pl.when(jnp.logical_not(has_l))
    def _():
        margins[0] = jnp.zeros(margins.shape[1:], BF16)
        near[0] = jnp.full(near.shape[1:], -1, jnp.int32).astype(jnp.int16)

    @pl.when(jnp.logical_not(has_r))
    def _():
        margins[1] = jnp.zeros(margins.shape[1:], BF16)
        near[1] = jnp.full(near.shape[1:], -1, jnp.int32).astype(jnp.int16)

    for load in loads[:3]:
        load.wait()
    swap = order_ref[0] != 0

    def permuted(ref):
        a = ref[0:BLOCK, :]
        b = ref[BLOCK:2 * BLOCK, :]
        return jnp.concatenate([jnp.where(swap, b, a), jnp.where(swap, a, b)], axis=0)

    index = permuted(index_ref)
    value = permuted(foot_ref)
    v_hi = value.astype(BF16).astype(F32)
    for ref, rows in ((hi_s, (index >> 7).astype(F32)),
                      (lo_s, (index & (LANES - 1)).astype(F32)),
                      (vl_s, value - v_hi),
                      (vh_s, jnp.where(v_hi == 0.0, -1.0, v_hi))):
        ref[0] = rows[:BLOCK]
        ref[1] = rows[BLOCK:]

    largest = jnp.max(value, axis=1, keepdims=True) * 1.01 + 1e-30
    largest = jnp.broadcast_to(largest, (2 * BLOCK, LANES)).astype(BF16).astype(F32)
    unit_s[0] = STEPS / largest[:BLOCK]
    unit_s[1] = STEPS / largest[BLOCK:]
    lane8 = lax.broadcasted_iota(jnp.int32, (BLOCK, LANES), 1)
    lead = jnp.concatenate(
        [traces_ref[...].astype(F32), jnp.zeros((frames, LANES - 2 * BLOCK), F32)], axis=1)
    own[f, :, quarter:quarter + LANES] = jnp.concatenate(
        [lead, jnp.where(lane8 < LANES // 2, largest[:BLOCK], largest[BLOCK:])],
        axis=0).astype(BF16)

    def peer(d):
        to = lax.rem(f + d, nf)
        return pltpu.make_async_remote_copy(
            src_ref=own.at[f], dst_ref=own.at[f], send_sem=send_m.at[0, to],
            recv_sem=recv_m.at[0, f], device_id=(to, s), device_id_type=MESH)

    def to_right(d):
        to = lax.rem(f + d, nf)
        return pltpu.make_async_remote_copy(
            src_ref=own.at[f, :, pl.ds(quarter, quarter + LANES)], dst_ref=margins.at[0, f],
            send_sem=send_m.at[1, to], recv_sem=recv_m.at[1, f],
            device_id=(to, s + 1), device_id_type=MESH)

    def to_left(d):
        to = lax.rem(f + d, nf)
        return pltpu.make_async_remote_copy(
            src_ref=own.at[f, :, pl.ds(0, quarter + LANES)], dst_ref=margins.at[1, f],
            send_sem=send_m.at[2, to], recv_sem=recv_m.at[2, f],
            device_id=(to, s - 1), device_id_type=MESH)

    rows16 = 2 * BLOCK
    iota = lax.broadcasted_iota(jnp.int32, (rows16, foot_n), 0).astype(F32)
    span = half * BLOCK

    def dense_right(b):
        return pltpu.make_async_remote_copy(
            src_ref=sent.at[2 * b + 1], dst_ref=near.at[0, pl.ds(b * span, span), :],
            send_sem=send_d.at[0, b], recv_sem=recv_d.at[0, b],
            device_id=(f, s + 1), device_id_type=MESH)

    def dense_left(b):
        return pltpu.make_async_remote_copy(
            src_ref=sent.at[2 * b], dst_ref=near.at[1, pl.ds(b * span, span), :],
            send_sem=send_d.at[1, b], recv_sem=recv_d.at[1, b],
            device_id=(f, s - 1), device_id_type=MESH)

    def scatter_block(b, carry):
        def scatter_row(k):

            def spread(ref):
                return jnp.broadcast_to(ref[b, k:k + 1, :], (rows16, foot_n)).astype(BF16)

            hi = spread(hi_s)
            lo = spread(lo_s)
            vh = spread(vh_s)
            vl = spread(vl_s)
            zero = jnp.zeros((rows16, foot_n), BF16)
            one = jnp.ones((rows16, foot_n), BF16)
            iota16 = iota.astype(BF16)
            low = [jnp.where(lo == iota16 + BF16(16 * t), one, zero) for t in range(LANES // 16)]
            high = [hi == iota16 + BF16(16 * t) for t in range(chunks // 16)]
            lhs = [jnp.where(m, vh, zero) for m in high] + [jnp.where(m, vl, zero) for m in high]
            got = dot_nt(jnp.concatenate(lhs, axis=0), jnp.concatenate(low, axis=0))
            g_hi = got[:chunks]
            enc = jnp.where(g_hi == 0.0, -1.0, jnp.maximum(g_hi, 0.0) + got[chunks:])
            dense[2 * b, pl.ds(k, half, stride=BLOCK), :] = enc[:half]
            dense[2 * b + 1, pl.ds(k, half, stride=BLOCK), :] = enc[half:]

        for k in range(BLOCK):
            scatter_row(k)

            if k == BLOCK - 1:
                @pl.when(b == 0)
                def _():
                    count = nf - 1 + nf * has_l.astype(jnp.int32) + nf * has_r.astype(jnp.int32)
                    pl.semaphore_wait(barrier, count)

                    for d in range(1, nf):
                        peer(d).start()

                    @pl.when(has_r)
                    def _():
                        for d in range(nf):
                            to_right(d).start()

                    @pl.when(has_l)
                    def _():
                        for d in range(nf):
                            to_left(d).start()

        for side in range(2):
            values = dense[2 * b + side].reshape(half, BLOCK, LANES)
            steps = jnp.where(values < 0.0, -1.0, values * unit_s[b] + 0.5)
            sent[2 * b + side] = steps.reshape(span, LANES).astype(jnp.int32).astype(jnp.int16)

        @pl.when(has_r)
        def _():
            dense_right(b).start()

        @pl.when(has_l)
        def _():
            dense_left(b).start()

        return carry

    lax.fori_loop(0, 2, scatter_block, 0)

    for d in range(1, nf):
        pltpu.make_async_remote_copy(
            src_ref=own.at[f], dst_ref=own.at[lax.rem(f + d, nf)], send_sem=send_m.at[0, 0],
            recv_sem=recv_m.at[0, lax.rem(f + d, nf)], device_id=(f, s),
            device_id_type=MESH).wait_recv()

    def all_frames(pick):
        return jnp.concatenate([pick(g) for g in range(nf)], axis=0)

    def unpacked(load):
        def one(g):
            both = load(g).astype(F32)
            return jnp.concatenate([both[:frames], both[frames:]], axis=1)
        return all_frames(one)

    own_l = unpacked(lambda g: own[g, :, 0:quarter])
    own_r = unpacked(lambda g: own[g, :, quarter + LANES:])
    total = nf * frames
    padding = jnp.zeros((LANES - total, LANES), F32)
    eye = (lax.broadcasted_iota(jnp.int32, (rows16, LANES), 0)
           == lax.broadcasted_iota(jnp.int32, (rows16, LANES), 1)).astype(F32).astype(BF16)

    def by_source(pick):
        block = jnp.concatenate([all_frames(pick), padding], axis=0).astype(BF16)
        rows = dot_nt(eye, block)
        return jnp.concatenate([jnp.where(swap, rows[BLOCK:], rows[:BLOCK]),
                                jnp.where(swap, rows[:BLOCK], rows[BLOCK:])], axis=0)

    t_own = by_source(lambda g: own[g, :, quarter:quarter + LANES].astype(F32)[:frames])

    depth = -(-(total + 3 * 32) // LANES) * LANES
    identity = (lax.broadcasted_iota(jnp.int32, (total, LANES), 0)
                == lax.broadcasted_iota(jnp.int32, (total, LANES), 1)).astype(F32)

    def weights(t_near):
        t32 = jnp.concatenate([t_own, t_near], axis=0)
        stacked = jnp.concatenate(
            [identity, t32, t32, t32,
             jnp.zeros((depth - total - 96, LANES), F32)], axis=0).astype(BF16)
        full = dot_nt(t32.astype(BF16), stacked)
        lane = lax.broadcasted_iota(jnp.int32, full.shape, 1)
        g_hi = full.astype(BF16).astype(F32)
        picked = jnp.where((lane >= total + 32) & (lane < total + 64), full - g_hi, g_hi)
        first = jnp.where(lane < total, full, -picked).astype(BF16)
        t_f = jnp.concatenate([t32[0:8], t32[16:24]], axis=0)
        t_s = jnp.concatenate([t32[8:16], t32[24:32]], axis=0)
        stacked2 = jnp.concatenate(
            [t_f, t_f, t_f, jnp.zeros((LANES - 48, LANES), F32)], axis=0).astype(BF16)
        cross = dot_nt(t_s.astype(BF16), stacked2)
        lane2 = lax.broadcasted_iota(jnp.int32, cross.shape, 1)
        row2 = lax.broadcasted_iota(jnp.int32, cross.shape, 0)
        c_hi = cross.astype(BF16).astype(F32)
        picked2 = jnp.where((lane2 >= 16) & (lane2 < 32), cross - c_hi, c_hi)
        same = (row2 // 8) == ((lane2 // 8) % 2)
        second = jnp.where(same, picked2, 0.0).astype(BF16)
        inverse = 1.0 / (jnp.sum(t32 * t32, axis=1, keepdims=True) + 1.0)
        return first, second, inverse

    tiles = foot_n // LANES
    out_ref[...] = jnp.zeros_like(out_ref)

    early = 1 - lax.rem(s, 2)

    def update_side(side):
        present = jnp.where(side == 0, s, ns - 1 - s) > 0

        @pl.when(present)
        def _():
            for d in range(nf):
                pltpu.make_async_remote_copy(
                    src_ref=margins.at[side, d], dst_ref=margins.at[side, d],
                    send_sem=send_m.at[0, 0], recv_sem=recv_m.at[1 + side, d],
                    device_id=(f, s), device_id_type=MESH).wait_recv()

        def wide(ref, at, start):
            return jnp.concatenate(
                [ref[at, (start + c) * BLOCK:(start + c + 1) * BLOCK, :] for c in range(half)],
                axis=1)

        def margin_part(g, first, last, width):
            return jnp.where(side == 0, margins[side, g, :, first:first + width].astype(F32),
                             margins[side, g, :, last:last + width].astype(F32))

        outer = unpacked(lambda g: margin_part(g, LANES, 0, quarter))
        movie = jnp.where(side == 0, jnp.concatenate([outer, own_l], axis=1),
                          jnp.concatenate([own_r, outer], axis=1)).astype(BF16)
        w, cross, inverse = weights(
            by_source(lambda g: margin_part(g, 0, quarter, LANES)[:frames]))
        w = w[:, :total + 96]
        cross = cross[:, :48]
        scales = margin_part(0, 0, quarter, LANES)[frames:] * (1.0 / STEPS)
        size = jnp.concatenate(
            [jnp.broadcast_to(scales[:, 0:1], (BLOCK, LANES)),
             jnp.broadcast_to(scales[:, LANES // 2:LANES // 2 + 1], (BLOCK, LANES))], axis=0)
        @pl.when(present)
        def _():
            for b in range(2):
                pltpu.make_async_remote_copy(
                    src_ref=near.at[side, pl.ds(b * span, span), :],
                    dst_ref=near.at[side, pl.ds(b * span, span), :],
                    send_sem=send_d.at[0, 0], recv_sem=recv_d.at[side, b],
                    device_id=(f, s), device_id_type=MESH).wait_recv()

        steps = near[side].astype(jnp.int32).astype(F32).reshape(2, half, BLOCK, LANES)
        enc = [wide(dense, side, 0), wide(dense, 2 + side, 0)]
        for b in range(2):
            enc.append(jnp.concatenate(
                [steps[b, c] * size[b * BLOCK:(b + 1) * BLOCK] for c in range(half)], axis=1))
        mask = [(e >= 0.0).astype(F32) for e in enc]
        state = [jnp.maximum(e, 0.0) for e in enc]

        def residual(w_rows, state):
            high, low = halves(jnp.concatenate(state, axis=0))
            return dot_nn(w_rows, jnp.concatenate([movie, high, high, low], axis=0))

        def change(c_rows, old, new):
            high, low = halves(jnp.concatenate([n - o for n, o in zip(new, old)], axis=0))
            return dot_nn(c_rows, jnp.concatenate([high, high, low], axis=0))

        def step(i, rest):
            return mask[i] * jnp.maximum(state[i] + rest * inverse[8 * i:8 * i + 8], 0.0)

        rest = residual(w, state)
        new_f = [step(0, rest[0:8]), step(2, rest[16:24])]
        moved = change(cross, [state[0], state[2]], new_f)
        new_s = [step(1, rest[8:16] - moved[0:8]), step(3, rest[24:32] - moved[8:16])]
        state = [new_f[0], new_s[0], new_f[1], new_s[1]]
        rest = residual(w[0:16], state)
        new_f = step(0, rest[0:8])
        moved = change(cross, [state[0], state[2]], [new_f, state[2]])
        new_s = step(1, rest[8:16] - moved[0:8])
        done = (jnp.where(swap, new_s, new_f), jnp.where(swap, new_f, new_s))
        return done

    done_early = update_side(early)
    done_late = update_side(1 - early)
    for side, done in ((early, done_early), (1 - early, done_late)):
        for b in range(2):
            for j in range(tiles):
                at = (slice(b * BLOCK, (b + 1) * BLOCK), slice(j * LANES, (j + 1) * LANES))
                place = index_ref[at]
                chunk = (place >> 7) - half * side
                lane = place & (LANES - 1)
                taken = out_ref[at]
                for c in range(half):
                    tile = done[b][:, c * LANES:(c + 1) * LANES]
                    got = jnp.take_along_axis(tile, lane, axis=1, mode="promise_in_bounds")
                    taken = jnp.where(chunk == c, got, taken)
                out_ref[at] = taken

    for d in range(1, nf):
        peer(d).wait_send()

    @pl.when(has_r)
    def _():
        for d in range(nf):
            to_right(d).wait_send()
        for b in range(2):
            dense_right(b).wait_send()

    @pl.when(has_l)
    def _():
        for d in range(nf):
            to_left(d).wait_send()
        for b in range(2):
            dense_left(b).wait_send()


def local(movie, traces, voxel_index, footprint, block_order):
    nf = lax.axis_size("frames")
    ns = lax.axis_size("slabs")
    frames, voxels = movie.shape
    sources, foot_n = footprint.shape
    margin = voxels // 2
    chunks = 2 * voxels // LANES
    vmem = pl.BlockSpec(memory_space=pltpu.VMEM)
    return pl.pallas_call(
        functools.partial(kernel, nf, ns),
        out_shape=pltpu.VMEM((sources, foot_n), F32),
        in_specs=[pl.BlockSpec(memory_space=pltpu.HBM)] * 5,
        out_specs=vmem,
        scratch_shapes=[
            pltpu.SMEM(block_order.shape, block_order.dtype),
            pltpu.VMEM(movie.shape, movie.dtype),
            pltpu.VMEM(traces.shape, traces.dtype),
            pltpu.VMEM(voxel_index.shape, voxel_index.dtype),
            pltpu.VMEM(footprint.shape, footprint.dtype),
            pltpu.VMEM((nf, 2 * frames, margin + LANES), BF16),
            pltpu.VMEM((2, nf, 2 * frames, margin // 2 + LANES), BF16),
            pltpu.VMEM((4, BLOCK * chunks // 2, LANES), F32),
            pltpu.VMEM((4, BLOCK * chunks // 2, LANES), jnp.int16),
            pltpu.VMEM((2, BLOCK * chunks, LANES), jnp.int16),
            pltpu.VMEM((2, BLOCK, foot_n), F32),
            pltpu.VMEM((2, BLOCK, foot_n), F32),
            pltpu.VMEM((2, BLOCK, foot_n), F32),
            pltpu.VMEM((2, BLOCK, foot_n), F32),
            pltpu.VMEM((2, BLOCK, LANES), F32),
            pltpu.SemaphoreType.DMA((5,)),
            pltpu.SemaphoreType.DMA((3, nf)),
            pltpu.SemaphoreType.DMA((3, nf)),
            pltpu.SemaphoreType.DMA((2, 2)),
            pltpu.SemaphoreType.DMA((2, 2)),
        ],
        compiler_params=pltpu.CompilerParams(
            collective_id=0, has_side_effects=True, vmem_limit_bytes=32 * 1024 * 1024),
        cost_estimate=pl.CostEstimate(
            flops=2 * sources * 64 * LANES * foot_n, bytes_accessed=500000, transcendentals=0),
    )(*(pltpu.with_memory_space_constraint(x, pltpu.HBM)
        for x in (block_order, movie, traces, voxel_index, footprint)))


def solution(mesh):
    in_specs = (P("frames", "slabs"), P("frames", "slabs"), P("slabs", None), P("slabs", None), P())
    out_specs = P("slabs", None)
    return jax.shard_map(local, mesh=mesh, in_specs=in_specs, out_specs=out_specs, check_vma=False)
```

```python
import functools

import jax
import jax.numpy as jnp
from jax import lax
from jax.experimental import pallas as pl
from jax.experimental.pallas import tpu as pltpu
from jax.sharding import PartitionSpec as P

BLOCK = 8
LANES = 128
STEPS = 32767.0
MESH = pl.DeviceIdType.MESH
F32 = jnp.float32
BF16 = jnp.bfloat16


def dot_nt(left, right):
    return lax.dot_general(left, right, (((1,), (1,)), ((), ())), preferred_element_type=F32)


def dot_nn(left, right):
    return lax.dot_general(left, right, (((1,), (0,)), ((), ())), preferred_element_type=F32)


def halves(value):
    high = value.astype(BF16)
    low = (value - high.astype(F32)).astype(BF16)
    return high, low


def kernel(
    nf, ns, order_in, movie_in, traces_in, index_in, foot_in, out_ref,
    order_ref, movie_ref, traces_ref, index_ref, foot_ref, own, margins, dense, sent, near,
    hi_s, lo_s, vh_s, vl_s, unit_s,
    load_sem, send_m, recv_m, send_d, recv_d,
):
    f = lax.axis_index("frames")
    s = lax.axis_index("slabs")
    has_l = s > 0
    has_r = s < ns - 1
    frames, voxels = movie_ref.shape
    margin = voxels // 2
    extent = 2 * voxels
    chunks = extent // LANES
    half = chunks // 2
    foot_n = foot_ref.shape[1]

    barrier = pltpu.get_barrier_semaphore()
    for d in range(1, nf):
        pl.semaphore_signal(barrier, inc=1, device_id=(lax.rem(f + d, nf), s), device_id_type=MESH)

    @pl.when(has_l)
    def _():
        for d in range(nf):
            pl.semaphore_signal(
                barrier, inc=1, device_id=(lax.rem(f + d, nf), s - 1), device_id_type=MESH)

    @pl.when(has_r)
    def _():
        for d in range(nf):
            pl.semaphore_signal(
                barrier, inc=1, device_id=(lax.rem(f + d, nf), s + 1), device_id_type=MESH)

    pairs = ((index_in, index_ref), (foot_in, foot_ref), (order_in, order_ref),
             (movie_in, movie_ref), (traces_in, traces_ref))
    loads = [pltpu.make_async_copy(a, b, load_sem.at[i]) for i, (a, b) in enumerate(pairs)]
    for load in loads:
        load.start()

    loads[3].wait()
    loads[4].wait()
    quarter = margin // 2
    parts = movie_ref[...].astype(F32)
    for h, at in ((0, 0), (1, quarter + LANES)):
        own[f, :, at:at + quarter] = jnp.concatenate(
            [parts[:, 2 * h * quarter:(2 * h + 1) * quarter],
             parts[:, (2 * h + 1) * quarter:(2 * h + 2) * quarter]], axis=0).astype(BF16)

    @pl.when(jnp.logical_not(has_l))
    def _():
        margins[0] = jnp.zeros(margins.shape[1:], BF16)
        near[0] = jnp.full(near.shape[1:], -1, jnp.int32).astype(jnp.int16)

    @pl.when(jnp.logical_not(has_r))
    def _():
        margins[1] = jnp.zeros(margins.shape[1:], BF16)
        near[1] = jnp.full(near.shape[1:], -1, jnp.int32).astype(jnp.int16)

    for load in loads[:3]:
        load.wait()
    swap = order_ref[0] != 0

    def permuted(ref):
        a = ref[0:BLOCK, :]
        b = ref[BLOCK:2 * BLOCK, :]
        return jnp.concatenate([jnp.where(swap, b, a), jnp.where(swap, a, b)], axis=0)

    index = permuted(index_ref)
    value = permuted(foot_ref)
    v_hi = value.astype(BF16).astype(F32)
    for ref, rows in ((hi_s, (index >> 7).astype(F32)),
                      (lo_s, (index & (LANES - 1)).astype(F32)),
                      (vl_s, value - v_hi),
                      (vh_s, jnp.where(v_hi == 0.0, -1.0, v_hi))):
        ref[0] = rows[:BLOCK]
        ref[1] = rows[BLOCK:]

    largest = jnp.max(value, axis=1, keepdims=True) * 1.01 + 1e-30
    largest = jnp.broadcast_to(largest, (2 * BLOCK, LANES)).astype(BF16).astype(F32)
    unit_s[0] = STEPS / largest[:BLOCK]
    unit_s[1] = STEPS / largest[BLOCK:]
    lane8 = lax.broadcasted_iota(jnp.int32, (BLOCK, LANES), 1)
    lead = jnp.concatenate(
        [traces_ref[...].astype(F32), jnp.zeros((frames, LANES - 2 * BLOCK), F32)], axis=1)
    own[f, :, quarter:quarter + LANES] = jnp.concatenate(
        [lead, jnp.where(lane8 < LANES // 2, largest[:BLOCK], largest[BLOCK:])],
        axis=0).astype(BF16)

    def peer(d):
        to = lax.rem(f + d, nf)
        return pltpu.make_async_remote_copy(
            src_ref=own.at[f], dst_ref=own.at[f], send_sem=send_m.at[0, to],
            recv_sem=recv_m.at[0, f], device_id=(to, s), device_id_type=MESH)

    def to_right(d):
        to = lax.rem(f + d, nf)
        return pltpu.make_async_remote_copy(
            src_ref=own.at[f, :, pl.ds(quarter, quarter + LANES)], dst_ref=margins.at[0, f],
            send_sem=send_m.at[1, to], recv_sem=recv_m.at[1, f],
            device_id=(to, s + 1), device_id_type=MESH)

    def to_left(d):
        to = lax.rem(f + d, nf)
        return pltpu.make_async_remote_copy(
            src_ref=own.at[f, :, pl.ds(0, quarter + LANES)], dst_ref=margins.at[1, f],
            send_sem=send_m.at[2, to], recv_sem=recv_m.at[2, f],
            device_id=(to, s - 1), device_id_type=MESH)

    rows16 = 2 * BLOCK
    iota = lax.broadcasted_iota(jnp.int32, (rows16, foot_n), 0).astype(F32)
    span = half * BLOCK

    def dense_right(b):
        return pltpu.make_async_remote_copy(
            src_ref=sent.at[2 * b + 1], dst_ref=near.at[0, pl.ds(b * span, span), :],
            send_sem=send_d.at[0, b], recv_sem=recv_d.at[0, b],
            device_id=(f, s + 1), device_id_type=MESH)

    def dense_left(b):
        return pltpu.make_async_remote_copy(
            src_ref=sent.at[2 * b], dst_ref=near.at[1, pl.ds(b * span, span), :],
            send_sem=send_d.at[1, b], recv_sem=recv_d.at[1, b],
            device_id=(f, s - 1), device_id_type=MESH)

    def scatter_block(b, carry):
        def scatter_row(k):

            def spread(ref):
                return jnp.broadcast_to(ref[b, k:k + 1, :], (rows16, foot_n)).astype(BF16)

            hi = spread(hi_s)
            lo = spread(lo_s)
            vh = spread(vh_s)
            vl = spread(vl_s)
            zero = jnp.zeros((rows16, foot_n), BF16)
            one = jnp.ones((rows16, foot_n), BF16)
            iota16 = iota.astype(BF16)
            low = [jnp.where(lo == iota16 + BF16(16 * t), one, zero) for t in range(LANES // 16)]
            high = [hi == iota16 + BF16(16 * t) for t in range(chunks // 16)]
            lhs = [jnp.where(m, vh, zero) for m in high] + [jnp.where(m, vl, zero) for m in high]
            got = dot_nt(jnp.concatenate(lhs, axis=0), jnp.concatenate(low, axis=0))
            g_hi = got[:chunks]
            enc = jnp.where(g_hi == 0.0, -1.0, jnp.maximum(g_hi, 0.0) + got[chunks:])
            dense[2 * b, pl.ds(k, half, stride=BLOCK), :] = enc[:half]
            dense[2 * b + 1, pl.ds(k, half, stride=BLOCK), :] = enc[half:]

        for k in range(BLOCK):
            scatter_row(k)

            if k == BLOCK - 3:
                @pl.when(b == 0)
                def _():
                    count = nf - 1 + nf * has_l.astype(jnp.int32) + nf * has_r.astype(jnp.int32)
                    pl.semaphore_wait(barrier, count)

                    for d in range(1, nf):
                        peer(d).start()

                    @pl.when(has_r)
                    def _():
                        for d in range(nf):
                            to_right(d).start()

                    @pl.when(has_l)
                    def _():
                        for d in range(nf):
                            to_left(d).start()

        for side in range(2):
            values = dense[2 * b + side].reshape(half, BLOCK, LANES)
            steps = jnp.where(values < 0.0, -1.0, values * unit_s[b] + 0.5)
            sent[2 * b + side] = steps.reshape(span, LANES).astype(jnp.int32).astype(jnp.int16)

        @pl.when(has_r)
        def _():
            dense_right(b).start()

        @pl.when(has_l)
        def _():
            dense_left(b).start()

        return carry

    lax.fori_loop(0, 2, scatter_block, 0)

    for d in range(1, nf):
        pltpu.make_async_remote_copy(
            src_ref=own.at[f], dst_ref=own.at[lax.rem(f + d, nf)], send_sem=send_m.at[0, 0],
            recv_sem=recv_m.at[0, lax.rem(f + d, nf)], device_id=(f, s),
            device_id_type=MESH).wait_recv()

    def all_frames(pick):
        return jnp.concatenate([pick(g) for g in range(nf)], axis=0)

    def unpacked(load):
        def one(g):
            both = load(g).astype(F32)
            return jnp.concatenate([both[:frames], both[frames:]], axis=1)
        return all_frames(one)

    own_l = unpacked(lambda g: own[g, :, 0:quarter])
    own_r = unpacked(lambda g: own[g, :, quarter + LANES:])
    total = nf * frames
    padding = jnp.zeros((LANES - total, LANES), F32)
    eye = (lax.broadcasted_iota(jnp.int32, (rows16, LANES), 0)
           == lax.broadcasted_iota(jnp.int32, (rows16, LANES), 1)).astype(F32).astype(BF16)

    def by_source(pick):
        block = jnp.concatenate([all_frames(pick), padding], axis=0).astype(BF16)
        rows = dot_nt(eye, block)
        return jnp.concatenate([jnp.where(swap, rows[BLOCK:], rows[:BLOCK]),
                                jnp.where(swap, rows[:BLOCK], rows[BLOCK:])], axis=0)

    t_own = by_source(lambda g: own[g, :, quarter:quarter + LANES].astype(F32)[:frames])

    depth = -(-(total + 3 * 32) // LANES) * LANES
    identity = (lax.broadcasted_iota(jnp.int32, (total, LANES), 0)
                == lax.broadcasted_iota(jnp.int32, (total, LANES), 1)).astype(F32)

    def weights(t_near):
        t32 = jnp.concatenate([t_own, t_near], axis=0)
        stacked = jnp.concatenate(
            [identity, t32, t32, t32,
             jnp.zeros((depth - total - 96, LANES), F32)], axis=0).astype(BF16)
        full = dot_nt(t32.astype(BF16), stacked)
        lane = lax.broadcasted_iota(jnp.int32, full.shape, 1)
        g_hi = full.astype(BF16).astype(F32)
        picked = jnp.where((lane >= total + 32) & (lane < total + 64), full - g_hi, g_hi)
        first = jnp.where(lane < total, full, -picked).astype(BF16)
        t_f = jnp.concatenate([t32[0:8], t32[16:24]], axis=0)
        t_s = jnp.concatenate([t32[8:16], t32[24:32]], axis=0)
        stacked2 = jnp.concatenate(
            [t_f, t_f, t_f, jnp.zeros((LANES - 48, LANES), F32)], axis=0).astype(BF16)
        cross = dot_nt(t_s.astype(BF16), stacked2)
        lane2 = lax.broadcasted_iota(jnp.int32, cross.shape, 1)
        row2 = lax.broadcasted_iota(jnp.int32, cross.shape, 0)
        c_hi = cross.astype(BF16).astype(F32)
        picked2 = jnp.where((lane2 >= 16) & (lane2 < 32), cross - c_hi, c_hi)
        same = (row2 // 8) == ((lane2 // 8) % 2)
        second = jnp.where(same, picked2, 0.0).astype(BF16)
        inverse = 1.0 / (jnp.sum(t32 * t32, axis=1, keepdims=True) + 1.0)
        return first, second, inverse

    tiles = foot_n // LANES
    out_ref[...] = jnp.zeros_like(out_ref)

    early = 1 - lax.rem(s, 2)

    def update_side(side):
        present = jnp.where(side == 0, s, ns - 1 - s) > 0

        @pl.when(present)
        def _():
            for d in range(nf):
                pltpu.make_async_remote_copy(
                    src_ref=margins.at[side, d], dst_ref=margins.at[side, d],
                    send_sem=send_m.at[0, 0], recv_sem=recv_m.at[1 + side, d],
                    device_id=(f, s), device_id_type=MESH).wait_recv()

        def wide(ref, at, start):
            return jnp.concatenate(
                [ref[at, (start + c) * BLOCK:(start + c + 1) * BLOCK, :] for c in range(half)],
                axis=1)

        def margin_part(g, first, last, width):
            return jnp.where(side == 0, margins[side, g, :, first:first + width].astype(F32),
                             margins[side, g, :, last:last + width].astype(F32))

        outer = unpacked(lambda g: margin_part(g, LANES, 0, quarter))
        movie = jnp.where(side == 0, jnp.concatenate([outer, own_l], axis=1),
                          jnp.concatenate([own_r, outer], axis=1)).astype(BF16)
        w, cross, inverse = weights(
            by_source(lambda g: margin_part(g, 0, quarter, LANES)[:frames]))
        w = w[:, :total + 96]
        cross = cross[:, :48]
        scales = margin_part(0, 0, quarter, LANES)[frames:] * (1.0 / STEPS)
        size = jnp.concatenate(
            [jnp.broadcast_to(scales[:, 0:1], (BLOCK, LANES)),
             jnp.broadcast_to(scales[:, LANES // 2:LANES // 2 + 1], (BLOCK, LANES))], axis=0)
        @pl.when(present)
        def _():
            for b in range(2):
                pltpu.make_async_remote_copy(
                    src_ref=near.at[side, pl.ds(b * span, span), :],
                    dst_ref=near.at[side, pl.ds(b * span, span), :],
                    send_sem=send_d.at[0, 0], recv_sem=recv_d.at[side, b],
                    device_id=(f, s), device_id_type=MESH).wait_recv()

        steps = near[side].astype(jnp.int32).astype(F32).reshape(2, half, BLOCK, LANES)
        enc = [wide(dense, side, 0), wide(dense, 2 + side, 0)]
        for b in range(2):
            enc.append(jnp.concatenate(
                [steps[b, c] * size[b * BLOCK:(b + 1) * BLOCK] for c in range(half)], axis=1))
        mask = [(e >= 0.0).astype(F32) for e in enc]
        state = [jnp.maximum(e, 0.0) for e in enc]

        def residual(w_rows, state):
            high, low = halves(jnp.concatenate(state, axis=0))
            return dot_nn(w_rows, jnp.concatenate([movie, high, high, low], axis=0))

        def change(c_rows, old, new):
            high, low = halves(jnp.concatenate([n - o for n, o in zip(new, old)], axis=0))
            return dot_nn(c_rows, jnp.concatenate([high, high, low], axis=0))

        def step(i, rest):
            return mask[i] * jnp.maximum(state[i] + rest * inverse[8 * i:8 * i + 8], 0.0)

        rest = residual(w, state)
        new_f = [step(0, rest[0:8]), step(2, rest[16:24])]
        moved = change(cross, [state[0], state[2]], new_f)
        new_s = [step(1, rest[8:16] - moved[0:8]), step(3, rest[24:32] - moved[8:16])]
        state = [new_f[0], new_s[0], new_f[1], new_s[1]]
        rest = residual(w[0:16], state)
        new_f = step(0, rest[0:8])
        moved = change(cross, [state[0], state[2]], [new_f, state[2]])
        new_s = step(1, rest[8:16] - moved[0:8])
        done = (jnp.where(swap, new_s, new_f), jnp.where(swap, new_f, new_s))
        return done

    done_early = update_side(early)
    done_late = update_side(1 - early)
    for side, done in ((early, done_early), (1 - early, done_late)):
        for b in range(2):
            for j in range(tiles):
                at = (slice(b * BLOCK, (b + 1) * BLOCK), slice(j * LANES, (j + 1) * LANES))
                place = index_ref[at]
                chunk = (place >> 7) - half * side
                lane = place & (LANES - 1)
                taken = out_ref[at]
                for c in range(half):
                    tile = done[b][:, c * LANES:(c + 1) * LANES]
                    got = jnp.take_along_axis(tile, lane, axis=1, mode="promise_in_bounds")
                    taken = jnp.where(chunk == c, got, taken)
                out_ref[at] = taken

    for d in range(1, nf):
        peer(d).wait_send()

    @pl.when(has_r)
    def _():
        for d in range(nf):
            to_right(d).wait_send()
        for b in range(2):
            dense_right(b).wait_send()

    @pl.when(has_l)
    def _():
        for d in range(nf):
            to_left(d).wait_send()
        for b in range(2):
            dense_left(b).wait_send()


def local(movie, traces, voxel_index, footprint, block_order):
    nf = lax.axis_size("frames")
    ns = lax.axis_size("slabs")
    frames, voxels = movie.shape
    sources, foot_n = footprint.shape
    margin = voxels // 2
    chunks = 2 * voxels // LANES
    vmem = pl.BlockSpec(memory_space=pltpu.VMEM)
    return pl.pallas_call(
        functools.partial(kernel, nf, ns),
        out_shape=pltpu.VMEM((sources, foot_n), F32),
        in_specs=[pl.BlockSpec(memory_space=pltpu.HBM)] * 5,
        out_specs=vmem,
        scratch_shapes=[
            pltpu.SMEM(block_order.shape, block_order.dtype),
            pltpu.VMEM(movie.shape, movie.dtype),
            pltpu.VMEM(traces.shape, traces.dtype),
            pltpu.VMEM(voxel_index.shape, voxel_index.dtype),
            pltpu.VMEM(footprint.shape, footprint.dtype),
            pltpu.VMEM((nf, 2 * frames, margin + LANES), BF16),
            pltpu.VMEM((2, nf, 2 * frames, margin // 2 + LANES), BF16),
            pltpu.VMEM((4, BLOCK * chunks // 2, LANES), F32),
            pltpu.VMEM((4, BLOCK * chunks // 2, LANES), jnp.int16),
            pltpu.VMEM((2, BLOCK * chunks, LANES), jnp.int16),
            pltpu.VMEM((2, BLOCK, foot_n), F32),
            pltpu.VMEM((2, BLOCK, foot_n), F32),
            pltpu.VMEM((2, BLOCK, foot_n), F32),
            pltpu.VMEM((2, BLOCK, foot_n), F32),
            pltpu.VMEM((2, BLOCK, LANES), F32),
            pltpu.SemaphoreType.DMA((5,)),
            pltpu.SemaphoreType.DMA((3, nf)),
            pltpu.SemaphoreType.DMA((3, nf)),
            pltpu.SemaphoreType.DMA((2, 2)),
            pltpu.SemaphoreType.DMA((2, 2)),
        ],
        compiler_params=pltpu.CompilerParams(
            collective_id=0, has_side_effects=True, vmem_limit_bytes=32 * 1024 * 1024),
        cost_estimate=pl.CostEstimate(
            flops=2 * sources * 64 * LANES * foot_n, bytes_accessed=500000, transcendentals=0),
    )(*(pltpu.with_memory_space_constraint(x, pltpu.HBM)
        for x in (block_order, movie, traces, voxel_index, footprint)))


def solution(mesh):
    in_specs = (P("frames", "slabs"), P("frames", "slabs"), P("slabs", None), P("slabs", None), P())
    out_specs = P("slabs", None)
    return jax.shard_map(local, mesh=mesh, in_specs=in_specs, out_specs=out_specs, check_vma=False)
```
